32 devices in a mesh: dp: 8 (over y, x, core), blk: 4 (over z).
Axes of the slice: x: 2, y: 2, z: 4, core: 2. Of those that a mesh axis runs over, the one named last changes fastest.
Arguments:
- tokens: bfloat16 [16, 1024, 768], P('dp', 'blk'), may hold values from -6 to 6
- language: int32 [16], P('dp'), may hold values from 0 to 7
- lengths: int32 [16], P('dp'), may hold values from 1 to 1024, as said below
- rel_bucket: int32 [2047], replicated, may hold values from 0 to 31, as said below
- lang_table: bfloat16 [8, 768], replicated, may hold values from -3 to 3
- gain_first: float32 [768], replicated, may hold values from 0.5 to 1.5
- w_query: bfloat16 [768, 768], replicated, may hold values from -0.109375 to 0.109375
- w_key: bfloat16 [768, 768], replicated, may hold values from -0.109375 to 0.109375
- w_value: bfloat16 [768, 768], replicated, may hold values from -0.21875 to 0.21875
- w_output: bfloat16 [768, 768], replicated, may hold values from -0.4375 to 0.4375
- bias_table: float32 [32, 12], replicated, may hold values from -4 to 4
- gain_second: float32 [768], replicated, may hold values from 0.5 to 1.5
- w_in: bfloat16 [768, 3072], replicated, may hold values from -0.21875 to 0.21875
- w_out: bfloat16 [3072, 768], replicated, may hold values from -0.15625 to 0.15625
- cotangent: bfloat16 [16, 1024, 768], P('dp', 'blk'), may hold values from -6 to 6
Outputs:
- output: bfloat16 [16, 1024, 768], P('dp', 'blk')
- grad_tokens: bfloat16 [16, 1024, 768], P('dp', 'blk')
- grad_lang_table: float32 [8, 768], P(None, ('dp', 'blk'))
- grad_gain_first: float32 [768], P(('dp', 'blk'))
- grad_w_query: float32 [768, 768], P(('dp', 'blk'))
- grad_w_key: float32 [768, 768], P(('dp', 'blk'))
- grad_w_value: float32 [768, 768], P(('dp', 'blk'))
- grad_w_output: float32 [768, 768], P(('dp', 'blk'))
- grad_bias_table: float32 [32, 12], replicated
- grad_gain_second: float32 [768], P(('dp', 'blk'))
- grad_w_in: float32 [768, 3072], P(('dp', 'blk'))
- grad_w_out: float32 [3072, 768], P(('dp', 'blk'))
The draws below stay inside these ranges and needn't reach their ends.
Inputs may be any that keep to these rules, and one draw needn't show every extreme that they name: `lengths`: in each group of 2 consecutive sequences one, drawn from the seed, has the full length 1024. `rel_bucket`: the bucket is 0 at relative position 0, never falls as the distance grows on either side, is below 16 for keys at or before the query and at least 16 for keys after it.
All inputs are finite; a program needn't handle non-finite values.
Results may differ from the reference program's by a relative error of at most 0.015.
Values may be sent and summed in bfloat16 or wider, within the bound.
A program may use at most 320 MiB of HBM per device.

```python
import math
import jax
import jax.numpy as jnp
import numpy as np
from jax import lax

D = 768
HEADS = 12
HEAD_DIM = 64
FF = 3072
BUCKETS = 32
LANGS = 8
LENGTH = 1024
SEQS_DEV = 2
SEQS = 16


def draw_lengths(key, part):
    key = jax.random.fold_in(key, 7)
    pick_key, length_key = jax.random.split(key)
    groups = SEQS // SEQS_DEV
    sampled = jax.random.randint(length_key, (groups, SEQS_DEV), 1, LENGTH + 1)
    chosen = jax.random.randint(pick_key, (groups, 1), 0, SEQS_DEV)
    full_slot = jnp.arange(SEQS_DEV)[None, :] == chosen
    return jnp.where(full_slot, LENGTH, sampled).reshape(SEQS).astype(jnp.int32)


def side_bounds(key):
    boundary_count = BUCKETS // 2 - 1
    spacing = max(1, 2 * LENGTH // (boundary_count * (boundary_count + 1)))
    ceilings = 1 + spacing * (jnp.arange(boundary_count) + 1)
    intervals = jax.random.randint(key, (boundary_count,), 1, ceilings)
    return jnp.cumsum(intervals)


def draw_rel_bucket(key, part):
    key = jax.random.fold_in(key, 13)
    lower_key, upper_key = jax.random.split(key)
    distance = jnp.arange(2 * LENGTH - 1) - (LENGTH - 1)
    magnitude = jnp.abs(distance)
    lower_side = jnp.sum((side_bounds(lower_key)[None, :] <= magnitude[:, None]).astype(jnp.int32), axis=1)
    upper_side = jnp.sum((side_bounds(upper_key)[None, :] <= magnitude[:, None]).astype(jnp.int32), axis=1)
    return jnp.where(distance > 0, BUCKETS // 2 + upper_side, lower_side).astype(jnp.int32)


def touch_ends(drawn, rng, low, largest):
    spot = [jax.random.randint(jax.random.fold_in(rng, axis), (), 0, length) for axis, length in enumerate(drawn.shape)]
    main_axis = drawn.shape.index(max(drawn.shape))
    next_to = spot[:main_axis] + [(spot[main_axis] + 1) % drawn.shape[main_axis]] + spot[main_axis + 1:]
    return drawn.at[tuple(spot)].set(low).at[tuple(next_to)].set(largest)


def block_levels(own_key, extent, pieces, low, top_value):
    level = 1.0
    for dim, parts in pieces:
        draws = jax.random.uniform(jax.random.fold_in(jax.random.fold_in(own_key, 6), dim), (parts,), jnp.float32, low / len(pieces), top_value / len(pieces))
        level = level * jnp.repeat(jnp.exp(draws), extent[dim] // parts).reshape((-1,) + (1,) * (len(extent) - 1 - dim))
    return level


def cumulative_ranks(count, skew):
    loads = [(1 << 20) // math.isqrt(rank ** skew) + 1 for rank in range(1, count + 1)]
    deviation = 1 + sum(loads) // (1 << 30)
    return np.cumsum(np.array([max(1, weight // deviation) for weight in loads]))


def skewed_ids(key, dims, amount, lean):
    grid = cumulative_ranks(amount, lean)
    ticket = jax.random.randint(jax.random.fold_in(key, 1), dims, 0, int(grid[amount - 1]))
    standing = jnp.searchsorted(jnp.asarray(grid, jnp.int32), ticket, side="right")
    return jax.random.permutation(jax.random.fold_in(key, 2), amount)[standing].astype(jnp.int32)


def scatter_about(own_key, dims, spread, reach, cuts=(), kind=jnp.bfloat16):
    gain = block_levels(own_key, dims, cuts, -0.22, 0.18) if cuts else 1.0
    values = jax.random.normal(own_key, dims, jnp.float32) * spread * gain
    return jnp.minimum(jnp.maximum(values, -reach), reach).astype(kind)


def setup_inputs(seed: int = 0) -> dict:
    arg_keys = jax.random.split(jax.random.key(seed), 16)
    return {
        "tokens": scatter_about(arg_keys[0], (SEQS, LENGTH, D), 1.0, 6.0, ((0, 8), (1, 4))),
        "language": touch_ends(skewed_ids(arg_keys[1], (SEQS,), LANGS, 2), jax.random.fold_in(arg_keys[1], 3), 0, LANGS - 1).astype(jnp.int32),
        "lengths": draw_lengths(jax.random.fold_in(arg_keys[15], 71), 0),
        "rel_bucket": draw_rel_bucket(jax.random.fold_in(arg_keys[15], 71), 0),
        "lang_table": scatter_about(arg_keys[4], (LANGS, D), 0.5, 3.0),
        "gain_first": jnp.clip(1.0 + 0.1 * jax.random.normal(arg_keys[5], (D,), jnp.float32), 0.5, 1.5),
        "w_query": scatter_about(arg_keys[6], (D, D), (4 * D) ** -0.5, 0.109375),
        "w_key": scatter_about(arg_keys[7], (D, D), (4 * D) ** -0.5, 0.109375),
        "w_value": scatter_about(arg_keys[8], (D, D), D ** -0.5, 0.21875),
        "w_output": scatter_about(arg_keys[9], (D, D), (D // 4) ** -0.5, 0.4375),
        "bias_table": scatter_about(arg_keys[10], (BUCKETS, HEADS), 1.0, 4.0, (), jnp.float32),
        "gain_second": jnp.clip(1.0 + 0.1 * jax.random.normal(arg_keys[11], (D,), jnp.float32), 0.5, 1.5),
        "w_in": scatter_about(arg_keys[12], (D, FF), D ** -0.5, 0.21875),
        "w_out": scatter_about(arg_keys[13], (FF, D), (FF // 2) ** -0.5, 0.15625),
        "cotangent": scatter_about(arg_keys[14], (SEQS, LENGTH, D), 1.0, 6.0, ((0, 8), (1, 4))),
    }


@jax.custom_vjp
def low(v):
    return lax.optimization_barrier(v.astype(jnp.bfloat16)).astype(jnp.float32)

@jax.custom_vjp
def low_back(v):
    return v

def low_keep(v):
    return (low(v), None)

def low_pass(kept, grad):
    return (grad,)

def back_keep(v):
    return (v, None)

def back_low(kept, grad):
    return (low(grad),)
low.defvjp(low_keep, low_pass)
low_back.defvjp(back_keep, back_low)
highest = lax.Precision.HIGHEST
eps_norm = 1e-06
masked_score = -1e+30

def rms_norm(values, scaling):
    return values * lax.rsqrt(lax.optimization_barrier(jnp.mean(values * values, axis=-1, keepdims=True)) + eps_norm) * scaling

def block_forward(language, lengths, rel_bucket, tokens, lang_table, gain_first, w_query, w_key, w_value, w_output, bias_table, gain_second, w_in, w_out):
    seq_count, seq_len, model_width = tokens.shape
    lang_hot = (language[:, None] == jnp.arange(LANGS)[None, :]).astype(jnp.float32)
    with_lang = tokens + jnp.dot(lang_hot, lang_table, precision=highest)[:, None, :]
    normed = low(rms_norm(with_lang, gain_first)).reshape(-1, model_width)

    def project(weight):
        return low(low_back(jnp.dot(normed, weight, precision=highest))).reshape(seq_count, seq_len, HEADS, HEAD_DIM)
    query_all = project(w_query)
    key_all = project(w_key)
    value_all = project(w_value)
    bucket_hot = (rel_bucket[:, None] == jnp.arange(BUCKETS)[None, :]).astype(jnp.float32)
    bias_rel = jnp.dot(bucket_hot, bias_table, precision=highest)
    offset = (jnp.arange(seq_len)[None, :] - jnp.arange(seq_len)[:, None] + seq_len - 1).astype(jnp.int32)
    bias_full = jnp.transpose(bias_rel[offset], (2, 0, 1))

    def attend(sequence_item):
        query_seq, key_seq, value_seq, seq_length = sequence_item
        scores = low_back(jnp.einsum('rhe,khe->hrk', query_seq, key_seq, precision=highest) + bias_full)
        valid = jnp.arange(seq_len)[None, None, :] < seq_length
        scores = jnp.where(valid, scores, masked_score)
        shifted = scores - lax.optimization_barrier(jnp.max(scores, axis=-1, keepdims=True))
        weights = jnp.exp(shifted)
        weights = weights / lax.optimization_barrier(jnp.sum(weights, axis=-1, keepdims=True))
        mixture = jnp.einsum('hrk,khe->rhe', weights, value_seq, precision=highest)
        return low(low_back(mixture)).reshape(seq_len, model_width)
    mixture = lax.map(jax.checkpoint(attend), (query_all, key_all, value_all, lengths))
    attended = low_back(jnp.dot(mixture.reshape(-1, model_width), w_output, precision=highest))
    middle = with_lang + attended.reshape(seq_count, seq_len, model_width)
    normed_second = low(rms_norm(middle, gain_second)).reshape(-1, model_width)
    hidden = low_back(jnp.dot(normed_second, w_in, precision=highest))
    active = low(jax.nn.gelu(hidden, approximate=True))
    return middle + jnp.dot(active, w_out, precision=highest).reshape(seq_count, seq_len, model_width)

def reference(tokens, language, lengths, rel_bucket, lang_table, gain_first, w_query, w_key, w_value, w_output, bias_table, gain_second, w_in, w_out, cotangent):

    def primal(tok, lang_w, gain_one, query_w, key_w, value_w, output_w, bias_w, gain_two, in_w, out_w):
        return block_forward(language, lengths, rel_bucket, tok, lang_w, gain_one, query_w, key_w, value_w, output_w, bias_w, gain_two, in_w, out_w)
    result, pullback = jax.vjp(primal, tokens.astype(jnp.float32), lang_table.astype(jnp.float32), gain_first.astype(jnp.float32), w_query.astype(jnp.float32), w_key.astype(jnp.float32), w_value.astype(jnp.float32), w_output.astype(jnp.float32), bias_table.astype(jnp.float32), gain_second.astype(jnp.float32), w_in.astype(jnp.float32), w_out.astype(jnp.float32))
    gradients = pullback(cotangent.astype(jnp.float32))
    return (result.astype(jnp.bfloat16), gradients[0].astype(jnp.bfloat16), gradients[1], gradients[2], gradients[3], gradients[4], gradients[5], gradients[6], gradients[7], gradients[8], gradients[9], gradients[10])
```

```python
import functools

import jax
import jax.numpy as jnp
from jax import lax
from jax.experimental import pallas as pl
from jax.experimental.pallas import tpu as pltpu
from jax.sharding import PartitionSpec as P

MESH = pl.DeviceIdType.MESH
bf16 = jnp.bfloat16
f32 = jnp.float32
eps_norm = 1e-06
masked_score = -1e30
highest = lax.Precision.HIGHEST
LANE = 128
VMEM_BYTES = 60 * 2**20


def dot(left, right, left_dim, right_dim):
    return lax.dot_general(
        left, right, (((left_dim,), (right_dim,)), ((), ())), preferred_element_type=f32
    )


def move_pairs(dp_size, blk_size, same):
    half = blk_size // 2
    pairs = []
    for d in range(dp_size):
        for z in range(blk_size):
            low = z % 2 if same else 1 - z % 2
            target = (2 * (d // 2) + z // half, 2 * (d % 2) + low)
            pairs.append((d * blk_size + z, target[0] * blk_size + target[1]))
    return pairs


def swap_core(value):
    size = lax.axis_size("dp")
    return lax.ppermute(value, "dp", [(d, d ^ 1) for d in range(size)])


def to_rows(value, odd):
    dp_size, blk_size = lax.axis_size("dp"), lax.axis_size("blk")
    first = jnp.where(odd, value[1], value[0])
    second = jnp.where(odd, value[0], value[1])
    first = lax.ppermute(first, ("dp", "blk"), move_pairs(dp_size, blk_size, True))
    second = lax.ppermute(second, ("dp", "blk"), move_pairs(dp_size, blk_size, False))
    return jnp.where(odd, jnp.concatenate([second, first]), jnp.concatenate([first, second]))


def from_rows(value, odd):
    dp_size, blk_size = lax.axis_size("dp"), lax.axis_size("blk")
    low, high = jnp.split(value, 2)
    first = jnp.where(odd, high, low)
    second = jnp.where(odd, low, high)
    back_same = [(b, a) for a, b in move_pairs(dp_size, blk_size, True)]
    back_other = [(b, a) for a, b in move_pairs(dp_size, blk_size, False)]
    first = lax.ppermute(first, ("dp", "blk"), back_same)
    second = lax.ppermute(second, ("dp", "blk"), back_other)
    return jnp.where(odd, jnp.stack([second, first]), jnp.stack([first, second]))


def window(core, row_start, col_start, half, span):
    base = col_start - row_start + span
    turns = (row_start >= half) - (col_start >= half)
    return pl.multiple_of(base + core * (turns * 2 * half), LANE) if turns else base


def split_three(value):
    high = value.astype(bf16).astype(f32)
    middle = (value - high).astype(bf16).astype(f32)
    low = (value - high - middle).astype(bf16).astype(f32)
    return high, middle, low


def forward_kernel(head_count, head_size, qkv, bias_row, key_mask, mixture, attended, log_total, table, scores, weights, key_ext, query_ext, value_ext):
    core = lax.axis_index("dp") % 2
    width = head_count * head_size
    span = qkv.shape[1]
    half = span // 2
    step = 2 * LANE
    row_id = lax.broadcasted_iota(jnp.int32, (16, span), 0)
    key_ext[pl.ds(head_size, 16), :] = jnp.where(row_id == 0, key_mask[...], 0.0).astype(bf16)
    query_ext[pl.ds(head_size, 16), :] = jnp.where(row_id == 0, 1.0, 0.0).astype(bf16)
    value_ext[pl.ds(head_size, 16), :] = jnp.where(row_id == 0, 1.0, 0.0).astype(bf16)

    def one_head(head, _):
        first = pl.multiple_of(head * head_size, head_size)
        row = bias_row[pl.ds(head, 1), :]
        table[...] = pltpu.roll(jnp.broadcast_to(row, table.shape), 0, 1, stride=1, stride_axis=0)
        query_ext[pl.ds(0, head_size), :] = qkv[pl.ds(first, head_size), :]
        key_ext[pl.ds(0, head_size), :] = qkv[pl.ds(width + first, head_size), :]
        value_ext[pl.ds(0, head_size), :] = qkv[pl.ds(2 * width + first, head_size), :]
        for row_start in range(0, span, step):
            query = query_ext[:, row_start : row_start + step]
            best = None
            for col_start in range(0, span, LANE):
                part = dot(key_ext[:, col_start : col_start + LANE], query, 0, 0)
                place = window(core, col_start, row_start, half, span)
                part = part + table[:, pl.ds(place, step)]
                scores[col_start : col_start + LANE, :] = part
                folded = jnp.max(part.reshape(LANE // 8, 8, step), axis=0)
                best = folded if best is None else jnp.maximum(best, folded)
            top = jnp.max(best, axis=0, keepdims=True)
            for col_start in range(0, span, LANE):
                weights[col_start : col_start + LANE, :] = jnp.exp(
                    scores[col_start : col_start + LANE, :] - top
                ).astype(bf16)
            summed = dot(value_ext[...], weights[...], 1, 0)
            total = summed[head_size : head_size + 1]
            part = summed[:head_size] / total
            attended[pl.ds(first, head_size), row_start : row_start + step] = part
            mixture[pl.ds(first, head_size), row_start : row_start + step] = part.astype(bf16)
            log_total[pl.ds(head, 1), row_start : row_start + step] = top + jnp.log(total)
        return 0

    lax.fori_loop(0, head_count, one_head, 0)


def attention_forward(qkv, bias_row, key_mask, head_count):
    wide, span = qkv.shape
    width = wide // 3
    head_size = width // head_count
    ext = pltpu.VMEM((head_size + 16, span), bf16)
    return pl.pallas_call(
        functools.partial(forward_kernel, head_count, head_size),
        out_shape=(
            jax.ShapeDtypeStruct((width, span), bf16),
            jax.ShapeDtypeStruct((width, span), f32),
            jax.ShapeDtypeStruct((8, span), f32),
        ),
        scratch_shapes=[
            pltpu.VMEM((LANE, 2 * span), f32),
            pltpu.VMEM((span, 2 * LANE), f32),
            pltpu.VMEM((span, 2 * LANE), bf16),
            ext,
            ext,
            ext,
        ],
        compiler_params=pltpu.CompilerParams(vmem_limit_bytes=VMEM_BYTES),
        name="attention_forward",
    )(qkv, bias_row, key_mask)


def backward_kernel(head_count, head_size, qkv, grad_mixture, attended, log_total, bias_row, key_mask, grads, diagonals, table, sums, weights, slopes, key_ext, query_ext, value_ext, grad_ext):
    core = lax.axis_index("dp") % 2
    width = head_count * head_size
    span = qkv.shape[1]
    half = span // 2
    row_id = lax.broadcasted_iota(jnp.int32, (16, span), 0)
    key_tail = jnp.where(row_id == 0, key_mask[...], jnp.where(row_id < 4, 1.0, 0.0))
    key_ext[pl.ds(head_size, 16), :] = key_tail.astype(bf16)
    value_ext[pl.ds(head_size, 16), :] = jnp.where(row_id < 3, 1.0, 0.0).astype(bf16)

    def one_head(head, _):
        first = pl.multiple_of(head * head_size, head_size)
        row = bias_row[pl.ds(head, 1), :]
        table[...] = pltpu.roll(jnp.broadcast_to(row, table.shape), 0, 1, stride=1, stride_axis=0)
        sums[...] = jnp.zeros_like(sums)
        query = qkv[pl.ds(first, head_size), :]
        key = qkv[pl.ds(width + first, head_size), :]
        grad = grad_mixture[pl.ds(first, head_size), :]
        key_ext[pl.ds(0, head_size), :] = key
        value_ext[pl.ds(0, head_size), :] = qkv[pl.ds(2 * width + first, head_size), :]
        query_ext[pl.ds(0, head_size), :] = query
        grad_ext[pl.ds(0, head_size), :] = grad
        a, b, c = split_three(-log_total[pl.ds(head, 1), :])
        query_ext[pl.ds(head_size, 16), :] = jnp.where(
            row_id == 0, 1.0, jnp.where(row_id == 1, a, jnp.where(row_id == 2, b, jnp.where(row_id == 3, c, 0.0)))
        ).astype(bf16)
        row_dot = jnp.sum(
            grad.astype(f32) * attended[pl.ds(first, head_size), :], axis=0, keepdims=True
        )
        a, b, c = split_three(-row_dot)
        grad_ext[pl.ds(head_size, 16), :] = jnp.where(
            row_id == 0, a, jnp.where(row_id == 1, b, jnp.where(row_id == 2, c, 0.0))
        ).astype(bf16)
        for row_start in range(0, span, LANE):
            rows = slice(row_start, row_start + LANE)
            for col_start in range(0, span, half):
                cols = slice(col_start, col_start + half)
                place = pl.ds(window(core, row_start, col_start, half, span), half)
                part = dot(query_ext[:, rows], key_ext[:, cols], 0, 0)
                part = jnp.exp(part + table[:, place])
                slope = part * dot(grad_ext[:, rows], value_ext[:, cols], 0, 0)
                weights[rows, cols] = part.astype(bf16)
                slopes[rows, cols] = slope.astype(bf16)
                sums[:, place] += slope
        grads[pl.ds(first, head_size), :] = dot(key, slopes[...], 1, 1).astype(bf16)
        grads[pl.ds(width + first, head_size), :] = dot(query, slopes[...], 1, 0).astype(bf16)
        grads[pl.ds(2 * width + first, head_size), :] = dot(grad, weights[...], 1, 0).astype(bf16)
        folded = sums[...]
        count = LANE
        while count > 8:
            count //= 2
            folded = folded[:count] + pltpu.roll(folded[count:], 2 * span - count, 1)
        diagonals[pl.ds(pl.multiple_of(head * 8, 8), 8), :] = folded
        return 0

    lax.fori_loop(0, head_count, one_head, 0)


def attention_backward(qkv, grad_mixture, attended, log_total, bias_row, key_mask, head_count):
    wide, span = qkv.shape
    width = wide // 3
    head_size = width // head_count
    ext = pltpu.VMEM((head_size + 16, span), bf16)
    square = pltpu.VMEM((span, span), bf16)
    slab = pltpu.VMEM((LANE, 2 * span), f32)
    return pl.pallas_call(
        functools.partial(backward_kernel, head_count, head_size),
        out_shape=(
            jax.ShapeDtypeStruct((wide, span), bf16),
            jax.ShapeDtypeStruct((8 * head_count, 2 * span), f32),
        ),
        scratch_shapes=[slab, slab, square, square, ext, ext, ext, ext],
        compiler_params=pltpu.CompilerParams(vmem_limit_bytes=VMEM_BYTES),
        name="attention_backward",
    )(qkv, grad_mixture, attended, log_total, bias_row, key_mask)


ROWS_X, ROWS_Y, ROWS_Z = (0, 112), (112, 208), (208, 288)


def reduce_kernel(chain, shared_rows, other, own, small, result, small_total, total, from_core, ax, ay, az, bx, by, bz, cx, cy, cz, smalls, send_sem, recv_sem):
    dp, z = lax.axis_index("dp"), lax.axis_index("blk")
    x, y = (dp // 2) % 2, (dp // 4) % 2
    count = total.shape[3]
    wide = total.shape[4]
    partners = {"core": (dp ^ 1, z), "x": (dp ^ 2, z), "y": (dp ^ 4, z)}

    barrier = pltpu.get_barrier_semaphore()
    for name in ("core", "x", "y"):
        pl.semaphore_signal(barrier, inc=1, device_id=partners[name], device_id_type=MESH)

    @pl.when(z > 0)
    def _():
        pl.semaphore_signal(barrier, inc=1, device_id=(dp, z - 1), device_id_type=MESH)

    @pl.when(z < chain - 1)
    def _():
        pl.semaphore_signal(barrier, inc=1, device_id=(dp, z + 1), device_id_type=MESH)

    pl.semaphore_signal(barrier, inc=1, device_id=(dp, z ^ 2), device_id_type=MESH)
    pl.semaphore_wait(barrier, 6 - (z == 0).astype(jnp.int32) - (z == chain - 1).astype(jnp.int32))

    used = [0]

    def copy(source, target, device):
        slot = used[0]
        used[0] += 1
        return pltpu.make_async_remote_copy(
            src_ref=source,
            dst_ref=target,
            send_sem=send_sem.at[slot],
            recv_sem=recv_sem.at[slot],
            device_id=device,
            device_id_type=MESH,
        )

    def add(target, source):
        target[...] = (target[...].astype(f32) + source[...].astype(f32)).astype(bf16)

    def rows(span):
        return pl.ds(span[0], span[1] - span[0])

    class Chain:
        def __init__(self, pick, slots, spread):
            self.pick, self.slots, self.spread = pick, slots, spread
            self.up, self.down = [], []
            for k in range(chain - 1):
                self.up.append(copy(pick(chain - 1 - k), slots.at[k], (dp, z + 1)))
                self.down.append(copy(pick(k), slots.at[chain - 1 + k], (dp, z - 1)))

        def add_all(self, place, slot):
            for index in self.spread:
                add(self.pick(place).at[index], self.slots.at[slot].at[index])

        def step(self, k):
            high, low = chain - 1 - k, k
            if k < chain - 1:

                @pl.when(z == 0)
                def _():
                    self.up[k].start()

                @pl.when(z == chain - 1)
                def _():
                    self.down[k].start()

        def relay(self, k):
            high, low = chain - 1 - k, k

            @pl.when((z > 0) & (z <= high))
            def _():
                self.up[k].wait_recv()
                self.add_all(high, k)

            @pl.when((z > 0) & (z < high))
            def _():
                self.up[k].start()

            @pl.when((z < chain - 1) & (z >= low))
            def _():
                self.down[k].wait_recv()
                self.add_all(low, chain - 1 + k)

            @pl.when((z < chain - 1) & (z > low))
            def _():
                self.down[k].start()

        def close(self):
            for k in range(chain - 1):

                @pl.when(z < chain - 1 - k)
                def _(k=k):
                    self.up[k].wait_send()

                @pl.when(z > k)
                def _(k=k):
                    self.down[k].wait_send()

    part_rows = pl.ds(0, shared_rows)
    core_copy = copy(other, from_core, partners["core"])
    core_copy.start()
    smalls[0] = small[...]
    small_copies = [copy(smalls.at[0], smalls.at[1], partners["core"])]
    small_copies[0].start()

    def fill(index, _):
        block = total.at[index // (2 * chain), (index // chain) % 2, index % chain]
        block[...] = own[index]
        return 0

    lax.fori_loop(0, 4 * chain, fill, 0)
    core_copy.wait()

    def fold(index, _):
        block = total.at[index // (2 * chain), (index // chain) % 2, index % chain, part_rows]
        block[...] = (block[...].astype(f32) + from_core[index].astype(f32)).astype(bf16)
        return 0

    lax.fori_loop(0, 4 * chain, fold, 0)

    a_x = copy(total.at[:, pl.ds(1 - x, 1), :, rows(ROWS_X)], ax, partners["x"])
    b_y = copy(total.at[pl.ds(1 - y, 1), :, :, rows(ROWS_Y)], by, partners["y"])
    a_x.start()
    b_y.start()
    both = [(i, j) for i in range(2) for j in range(2)]
    c_z = Chain(lambda d: total.at[:, :, d, rows(ROWS_Z)], cz, both)
    for k in range(chain - 1):
        c_z.step(k)
    small_copies[0].wait()
    smalls[2] = smalls[0] + smalls[1]
    small_copies.append(copy(smalls.at[2], smalls.at[3], partners["x"]))
    small_copies[1].start()
    c_z.relay(0)
    c_z.relay(1)
    small_copies[1].wait()
    smalls[4] = smalls[2] + smalls[3]
    small_copies.append(copy(smalls.at[4], smalls.at[5], partners["y"]))
    small_copies[2].start()
    b_y.wait()
    for j in range(2):
        for d in range(chain):
            add(total.at[y, j, d, rows(ROWS_Y)], by.at[0, j, d])
    b_z = Chain(lambda d: total.at[y, :, d, rows(ROWS_Y)], bz, list(range(2)))
    for k in range(chain - 1):
        b_z.step(k)
    a_x.wait()
    for i in range(2):
        for d in range(chain):
            add(total.at[i, x, d, rows(ROWS_X)], ax.at[i, 0, d])
    a_y = copy(total.at[pl.ds(1 - y, 1), x, :, rows(ROWS_X)], ay, partners["y"])
    a_y.start()
    small_copies[2].wait()
    smalls[6] = smalls[4] + smalls[5]
    small_copies.append(copy(smalls.at[6], smalls.at[7], (dp, z ^ 1)))
    small_copies[3].start()
    for k in range(2, chain - 1):
        c_z.relay(k)
    c_x = copy(total.at[:, pl.ds(1 - x, 1), z, rows(ROWS_Z)], cx, partners["x"])
    c_x.start()
    b_z.relay(0)
    b_z.relay(1)
    a_y.wait()
    for d in range(chain):
        add(total.at[y, x, d, rows(ROWS_X)], ay.at[0, d])
    a_z = Chain(lambda d: total.at[y, x, d, rows(ROWS_X)], az, [slice(None)])
    for k in range(chain - 1):
        a_z.step(k)
    small_copies[3].wait()
    smalls[8] = smalls[6] + smalls[7]
    small_copies.append(copy(smalls.at[8], smalls.at[9], (dp, z ^ 2)))
    small_copies[4].start()
    c_x.wait()
    for i in range(2):
        add(total.at[i, x, z, rows(ROWS_Z)], cx.at[i, 0])
    c_y = copy(total.at[pl.ds(1 - y, 1), x, z, rows(ROWS_Z)], cy, partners["y"])
    c_y.start()
    for k in range(2, chain - 1):
        b_z.relay(k)
    b_x = copy(total.at[y, pl.ds(1 - x, 1), z, rows(ROWS_Y)], bx, partners["x"])
    b_x.start()
    for k in range(chain - 1):
        a_z.relay(k)
    result[rows(ROWS_X), :] = total[y, x, z, rows(ROWS_X)].astype(f32)
    c_y.wait()
    result[rows(ROWS_Z), :] = total[y, x, z, rows(ROWS_Z)].astype(f32) + cy[0].astype(f32)
    b_x.wait()
    result[rows(ROWS_Y), :] = total[y, x, z, rows(ROWS_Y)].astype(f32) + bx[0].astype(f32)
    small_copies[4].wait()
    small_total[...] = smalls[8] + smalls[9]
    for chained in (a_z, b_z, c_z):
        chained.close()


def reduce_over_chips(other, own, small, chain):
    blocks, row_count, wide = own.shape
    shared_rows = other.shape[1]
    sizes = [span[1] - span[0] for span in (ROWS_X, ROWS_Y, ROWS_Z)]
    steps = 2 * (chain - 1)
    copies = 12 + 3 * steps
    buffers = [
        (2, 1, chain, sizes[0], wide),
        (1, chain, sizes[0], wide),
        (steps, sizes[0], wide),
        (1, sizes[1], wide),
        (1, 2, chain, sizes[1], wide),
        (steps, 2, sizes[1], wide),
        (2, 1, sizes[2], wide),
        (1, sizes[2], wide),
        (steps, 2, 2, sizes[2], wide),
    ]
    whole = pl.BlockSpec(memory_space=pltpu.VMEM)
    return pl.pallas_call(
        functools.partial(reduce_kernel, chain, shared_rows),
        out_shape=(
            jax.ShapeDtypeStruct((row_count, wide), f32),
            jax.ShapeDtypeStruct(small.shape, f32),
        ),
        in_specs=[whole] * 3,
        out_specs=(whole, whole),
        scratch_shapes=[
            pltpu.VMEM((2, 2, chain, row_count, wide), bf16),
            pltpu.VMEM(other.shape, bf16),
            *[pltpu.VMEM(shape, bf16) for shape in buffers],
            pltpu.VMEM((10, *small.shape), f32),
            pltpu.SemaphoreType.DMA((copies,)),
            pltpu.SemaphoreType.DMA((copies,)),
        ],
        compiler_params=pltpu.CompilerParams(
            collective_id=0, has_side_effects=True, vmem_limit_bytes=VMEM_BYTES
        ),
        name="reduce_over_chips",
    )(other, own, small)


def rms_parts(values):
    return lax.rsqrt(jnp.mean(values * values, axis=-1, keepdims=True) + eps_norm)


def norm_back(grad, values, gain, scale):
    weighted = grad * gain
    inner = jnp.mean(weighted * values, axis=-1, keepdims=True)
    return scale * weighted - values * (scale * scale * scale) * inner, jnp.sum(grad * values * scale, axis=0)


def local(
    tokens,
    language,
    lengths,
    rel_bucket,
    lang_table,
    gain_first,
    w_query,
    w_key,
    w_value,
    w_output,
    bias_table,
    gain_second,
    w_in,
    w_out,
    cotangent,
):
    dp_size, blk_size = lax.axis_size("dp"), lax.axis_size("blk")
    device, place = lax.axis_index("dp"), lax.axis_index("blk")
    core = device % 2
    odd = place % 2 == 1
    width = tokens.shape[-1]
    bucket_count, all_heads = bias_table.shape
    head_count = all_heads // 2
    mine = width // 2
    span = tokens.shape[1] * blk_size
    half = span // 2
    ff_width = w_in.shape[1]

    own_tokens = to_rows(tokens, odd)
    own_cotangent = to_rows(cotangent, odd)
    other_tokens = swap_core(own_tokens)
    ids = jnp.stack([language, lengths])
    other_ids = swap_core(ids)
    mates = jnp.where(place // (blk_size // 2) == core, ids, other_ids)
    spoken, length = jnp.where(odd, mates[:, 1], mates[:, 0])

    head_first = core * mine
    own_weights = jnp.concatenate(
        [lax.dynamic_slice_in_dim(w, head_first, mine, 1) for w in (w_query, w_key, w_value)], 1
    )
    own_weights_t = own_weights.T
    own_bias = lax.dynamic_slice_in_dim(bias_table, core * head_count, head_count, 1)
    bucket_hot = (rel_bucket[:, None] == jnp.arange(bucket_count)[None, :]).astype(f32)
    hot_later = jnp.pad(bucket_hot, ((1, 0), (0, 0)))
    hot_back = jnp.pad(bucket_hot[::-1], ((1, 0), (0, 0)))
    bias_later = jnp.pad(jnp.dot(hot_later, own_bias, precision=highest).T, ((0, 8 - head_count), (0, 0)))
    bias_back = jnp.pad(jnp.dot(hot_back, own_bias, precision=highest).T, ((0, 8 - head_count), (0, 0)))
    position = (jnp.arange(span) + half * core) % span
    key_mask = jnp.where(position < length, 0.0, masked_score).astype(f32)[None]

    embedding = lax.dynamic_slice_in_dim(lang_table, spoken, 1, 0).astype(f32)
    with_lang_all = jnp.concatenate([own_tokens, other_tokens]).astype(f32) + embedding
    scale_all = rms_parts(with_lang_all)
    normed = (with_lang_all * scale_all * gain_first).astype(bf16)
    qkv = dot(own_weights_t, normed, 1, 1).astype(bf16)
    mixture_t, attended_t, log_total = attention_forward(qkv, bias_back, key_mask, head_count)

    with_lang = with_lang_all[:half]
    other_mixture_t = swap_core(mixture_t[:, half:])
    own_mixture_t = mixture_t[:, :half]
    full_mixture_t = jnp.where(
        core == 0,
        jnp.concatenate([own_mixture_t, other_mixture_t]),
        jnp.concatenate([other_mixture_t, own_mixture_t]),
    )
    middle = with_lang + dot(full_mixture_t, w_output, 0, 0)
    scale_second = rms_parts(middle)
    normed_second = (middle * scale_second * gain_second).astype(bf16)
    hidden = dot(normed_second, w_in, 1, 0)
    active, gelu_back = jax.vjp(functools.partial(jax.nn.gelu, approximate=True), hidden)
    active = active.astype(bf16)
    output_rows = (middle + dot(active, w_out, 1, 0)).astype(bf16)
    output = from_rows(output_rows, odd)
    grad_hidden = gelu_back(dot(own_cotangent, w_out, 1, 1))[0].astype(bf16)
    grad_normed_second = dot(grad_hidden, w_in, 1, 1)
    grad_middle_part, grad_gain_second = norm_back(grad_normed_second, middle, gain_second, scale_second)
    grad_middle = own_cotangent.astype(f32) + grad_middle_part
    grad_projected = grad_middle.astype(bf16)
    grad_w_out = dot(active, own_cotangent, 0, 0)
    grad_w_in = dot(normed_second, grad_hidden, 0, 0)
    grad_w_output = dot(full_mixture_t, grad_projected, 1, 0)

    other_projected = swap_core(grad_projected)
    projected_all = jnp.concatenate([grad_projected, other_projected])
    own_output_rows = lax.dynamic_slice_in_dim(w_output, head_first, mine, 0)
    grad_mixture_t = dot(own_output_rows, projected_all, 1, 1).astype(bf16)
    grad_qkv, diagonals = attention_backward(
        qkv, grad_mixture_t, attended_t, log_total, bias_later, key_mask, head_count
    )
    pieces = diagonals.reshape(head_count, 8, 2 * span)
    by_distance = sum(jnp.roll(pieces[:, i], -i, axis=-1) for i in range(8))
    grad_bias_own = jnp.dot(by_distance, hot_later, precision=highest).T
    grad_bias = lax.dynamic_update_slice_in_dim(
        jnp.zeros(bias_table.shape, f32), grad_bias_own, core * head_count, 1
    )

    grad_normed_all = dot(grad_qkv, own_weights_t, 0, 0)
    from_other = swap_core(grad_normed_all[half:].astype(bf16))
    grad_normed = grad_normed_all[:half] + from_other.astype(f32)
    grad_start, grad_gain_first = norm_back(grad_normed, with_lang, gain_first, scale_all[:half])
    grad_with_lang = grad_middle + grad_start
    grad_tokens = from_rows(grad_with_lang.astype(bf16), odd)
    lang_hot = (jnp.arange(lang_table.shape[0]) == spoken).astype(f32)
    grad_lang = lang_hot[:, None] * jnp.sum(grad_with_lang, axis=0)[None, :]
    grad_w_qkv = dot(normed, grad_qkv, 0, 1)

    names = ("dp", "blk")
    devices = dp_size * blk_size
    if (dp_size, blk_size) != (8, 4):

        def scattered(value, dim=0):
            return lax.psum_scatter(value, names, scatter_dimension=dim, tiled=True)

        grads_qkv = []
        for part in jnp.split(grad_w_qkv, 3, axis=1):
            whole = jnp.zeros((width, width), f32)
            grads_qkv.append(scattered(lax.dynamic_update_slice_in_dim(whole, part, head_first, 1)))
        return (
            output,
            grad_tokens,
            scattered(grad_lang, 1),
            scattered(grad_gain_first),
            *grads_qkv,
            scattered(grad_w_output),
            lax.psum(grad_bias, names),
            scattered(grad_gain_second),
            scattered(grad_w_in),
            scattered(grad_w_out),
        )

    chips = devices // 2
    lead = dp_size // 2

    def blocks(value):
        rows, columns = value.shape
        each = rows // devices
        value = value.reshape(lead, 2, blk_size, each, columns)
        return jnp.moveaxis(value, 1, 0).reshape(2, chips, each, columns)

    def folded(value, columns):
        value = value.reshape(*value.shape[:-1], -1, columns)
        value = jnp.moveaxis(value, -2, -3)
        return value.reshape(*value.shape[:-3], -1, columns)

    low = lambda value: value.astype(bf16)
    block_out = low(blocks(grad_w_out))
    block_in = low(folded(blocks(grad_w_in), width))
    block_output = low(folded(blocks(grad_w_output), mine))
    block_qkv = [jnp.moveaxis(blocks(low(part)), 0, 1).reshape(chips, -1, mine) for part in jnp.split(grad_w_qkv, 3, axis=1)]
    pick = lambda value, which: lax.dynamic_index_in_dim(value, which, 0, keepdims=False)
    other = jnp.concatenate(
        [
            pick(block_out, 1 - core),
            pick(block_in, 1 - core),
            jnp.concatenate([pick(block_output, 1 - core), jnp.zeros_like(block_qkv[0])], -1),
        ],
        1,
    )
    own = jnp.concatenate(
        [
            pick(block_out, core),
            pick(block_in, core),
            jnp.concatenate([pick(block_output, core), block_qkv[0]], -1),
            jnp.concatenate(block_qkv[1:], -1),
        ],
        1,
    )
    small = jnp.zeros((16, width), f32)
    small = small.at[:8].set(grad_lang).at[8].set(grad_gain_first).at[9].set(grad_gain_second)
    small = small.at[10, : grad_bias.size].set(grad_bias.reshape(-1))
    summed, small = reduce_over_chips(other, own, small, blk_size)

    each_out, each = ff_width // devices, width // devices
    total_w_out = summed[:each_out]
    part_in = summed[each_out : 2 * each_out].reshape(ff_width // width, each, width)
    total_w_in = jnp.moveaxis(part_in, 0, 1).reshape(each, ff_width)
    left = summed[2 * each_out : 2 * each_out + 2 * each]
    right = summed[2 * each_out + 2 * each :]
    total_w_output = jnp.moveaxis(left[:, :mine].reshape(2, each, mine), 0, 1).reshape(each, width)
    parts = jnp.stack([left[:, mine:], right[:, :mine], right[:, mine:]]).reshape(3, 2, each, mine)
    keep, give = jnp.where(core == 0, parts[:, 0], parts[:, 1]), jnp.where(core == 0, parts[:, 1], parts[:, 0])
    got = swap_core(give)
    qkv_total = jnp.where(core == 0, jnp.concatenate([keep, got], -1), jnp.concatenate([got, keep], -1))
    first = (device * blk_size + place) * each
    sliced = lax.dynamic_slice_in_dim(small, first, each, 1)
    return (
        output,
        grad_tokens,
        sliced[:8],
        sliced[8],
        qkv_total[0],
        qkv_total[1],
        qkv_total[2],
        total_w_output,
        small[10, : grad_bias.size].reshape(grad_bias.shape),
        sliced[9],
        total_w_in,
        total_w_out,
    )


def solution(mesh):
    rows = P("dp", "blk", None)
    shard = P(("dp", "blk"))
    matrix = P(("dp", "blk"), None)
    return jax.shard_map(
        local,
        mesh=mesh,
        in_specs=(rows, P("dp"), P("dp")) + (P(),) * 11 + (rows,),
        out_specs=(
            rows,
            rows,
            P(None, ("dp", "blk")),
            shard,
            matrix,
            matrix,
            matrix,
            matrix,
            P(),
            shard,
            matrix,
            matrix,
        ),
        check_vma=False,
    )
```

```python
import functools
import itertools

import jax
import jax.numpy as jnp
from jax import lax
from jax.experimental import pallas as pl
from jax.experimental.pallas import tpu as pltpu
from jax.sharding import PartitionSpec as P

MESH = pl.DeviceIdType.MESH
bf16 = jnp.bfloat16
f32 = jnp.float32
eps_norm = 1e-06
masked_score = -1e30
highest = lax.Precision.HIGHEST
LANE = 128
VMEM_BYTES = 63 * 2**20


def dot(left, right, left_dim, right_dim):
    return lax.dot_general(
        left, right, (((left_dim,), (right_dim,)), ((), ())), preferred_element_type=f32
    )


def move_pairs(dp_size, blk_size, same):
    half = blk_size // 2
    pairs = []
    for d in range(dp_size):
        for z in range(blk_size):
            low = z % 2 if same else 1 - z % 2
            target = (2 * (d // 2) + z // half, 2 * (d % 2) + low)
            pairs.append((d * blk_size + z, target[0] * blk_size + target[1]))
    return pairs


def swap_core(value):
    size = lax.axis_size("dp")
    return lax.ppermute(value, "dp", [(d, d ^ 1) for d in range(size)])


def to_rows(value, odd):
    dp_size, blk_size = lax.axis_size("dp"), lax.axis_size("blk")
    first = jnp.where(odd, value[1], value[0])
    second = jnp.where(odd, value[0], value[1])
    first = lax.ppermute(first, ("dp", "blk"), move_pairs(dp_size, blk_size, True))
    second = lax.ppermute(second, ("dp", "blk"), move_pairs(dp_size, blk_size, False))
    return jnp.where(odd, jnp.concatenate([second, first]), jnp.concatenate([first, second]))


def from_rows(value, odd):
    dp_size, blk_size = lax.axis_size("dp"), lax.axis_size("blk")
    low, high = jnp.split(value, 2)
    first = jnp.where(odd, high, low)
    second = jnp.where(odd, low, high)
    back_same = [(b, a) for a, b in move_pairs(dp_size, blk_size, True)]
    back_other = [(b, a) for a, b in move_pairs(dp_size, blk_size, False)]
    first = lax.ppermute(first, ("dp", "blk"), back_same)
    second = lax.ppermute(second, ("dp", "blk"), back_other)
    return jnp.where(odd, jnp.stack([second, first]), jnp.stack([first, second]))


def window(core, row_start, col_start, half, span):
    base = col_start - row_start + span
    turns = (row_start >= half) - (col_start >= half)
    return pl.multiple_of(base + core * (turns * 2 * half), LANE) if turns else base


def split_three(value):
    high = value.astype(bf16).astype(f32)
    middle = (value - high).astype(bf16).astype(f32)
    low = (value - high - middle).astype(bf16).astype(f32)
    return high, middle, low


def forward_kernel(head_count, head_size, qkv, bias_row, key_mask, mixture, attended, log_total, table, scores, weights, key_ext, query_ext, value_ext):
    core = lax.axis_index("dp") % 2
    width = head_count * head_size
    span = qkv.shape[1]
    half = span // 2
    step = 2 * LANE
    row_id = lax.broadcasted_iota(jnp.int32, (16, span), 0)
    key_ext[pl.ds(head_size, 16), :] = jnp.where(row_id == 0, key_mask[...], 0.0).astype(bf16)
    query_ext[pl.ds(head_size, 16), :] = jnp.where(row_id == 0, 1.0, 0.0).astype(bf16)
    value_ext[pl.ds(head_size, 16), :] = jnp.where(row_id == 0, 1.0, 0.0).astype(bf16)

    def one_head(head, _):
        first = pl.multiple_of(head * head_size, head_size)
        row = bias_row[pl.ds(head, 1), :]
        table[...] = pltpu.roll(jnp.broadcast_to(row, table.shape), 0, 1, stride=1, stride_axis=0)
        query_ext[pl.ds(0, head_size), :] = qkv[pl.ds(first, head_size), :]
        key_ext[pl.ds(0, head_size), :] = qkv[pl.ds(width + first, head_size), :]
        value_ext[pl.ds(0, head_size), :] = qkv[pl.ds(2 * width + first, head_size), :]
        for row_start in range(0, span, step):
            query = query_ext[:, row_start : row_start + step]
            best = None
            for col_start in range(0, span, LANE):
                part = dot(key_ext[:, col_start : col_start + LANE], query, 0, 0)
                place = window(core, col_start, row_start, half, span)
                part = part + table[:, pl.ds(place, step)]
                scores[col_start : col_start + LANE, :] = part
                folded = jnp.max(part.reshape(LANE // 8, 8, step), axis=0)
                best = folded if best is None else jnp.maximum(best, folded)
            top = jnp.max(best, axis=0, keepdims=True)
            for col_start in range(0, span, LANE):
                weights[col_start : col_start + LANE, :] = jnp.exp(
                    scores[col_start : col_start + LANE, :] - top
                ).astype(bf16)
            summed = dot(value_ext[...], weights[...], 1, 0)
            total = summed[head_size : head_size + 1]
            part = summed[:head_size] / total
            attended[pl.ds(first, head_size), row_start : row_start + step] = part
            mixture[pl.ds(first, head_size), row_start : row_start + step] = part.astype(bf16)
            log_total[pl.ds(head, 1), row_start : row_start + step] = top + jnp.log(total)
        return 0

    lax.fori_loop(0, head_count, one_head, 0)


def attention_forward(qkv, bias_row, key_mask, head_count):
    wide, span = qkv.shape
    width = wide // 3
    head_size = width // head_count
    ext = pltpu.VMEM((head_size + 16, span), bf16)
    return pl.pallas_call(
        functools.partial(forward_kernel, head_count, head_size),
        out_shape=(
            jax.ShapeDtypeStruct((width, span), bf16),
            jax.ShapeDtypeStruct((width, span), f32),
            jax.ShapeDtypeStruct((8, span), f32),
        ),
        scratch_shapes=[
            pltpu.VMEM((LANE, 2 * span), f32),
            pltpu.VMEM((span, 2 * LANE), f32),
            pltpu.VMEM((span, 2 * LANE), bf16),
            ext,
            ext,
            ext,
        ],
        compiler_params=pltpu.CompilerParams(vmem_limit_bytes=VMEM_BYTES),
        name="attention_forward",
    )(qkv, bias_row, key_mask)


def backward_kernel(head_count, head_size, qkv, grad_mixture, attended, log_total, bias_row, key_mask, grads, diagonals, table, sums, weights, slopes, key_ext, query_ext, value_ext, grad_ext):
    core = lax.axis_index("dp") % 2
    width = head_count * head_size
    span = qkv.shape[1]
    half = span // 2
    row_id = lax.broadcasted_iota(jnp.int32, (16, span), 0)
    key_tail = jnp.where(row_id == 0, key_mask[...], jnp.where(row_id < 4, 1.0, 0.0))
    key_ext[pl.ds(head_size, 16), :] = key_tail.astype(bf16)
    value_ext[pl.ds(head_size, 16), :] = jnp.where(row_id < 3, 1.0, 0.0).astype(bf16)

    def one_head(head, _):
        first = pl.multiple_of(head * head_size, head_size)
        row = bias_row[pl.ds(head, 1), :]
        table[...] = pltpu.roll(jnp.broadcast_to(row, table.shape), 0, 1, stride=1, stride_axis=0)
        sums[...] = jnp.zeros_like(sums)
        query = qkv[pl.ds(first, head_size), :]
        key = qkv[pl.ds(width + first, head_size), :]
        grad = grad_mixture[pl.ds(first, head_size), :]
        key_ext[pl.ds(0, head_size), :] = key
        value_ext[pl.ds(0, head_size), :] = qkv[pl.ds(2 * width + first, head_size), :]
        query_ext[pl.ds(0, head_size), :] = query
        grad_ext[pl.ds(0, head_size), :] = grad
        a, b, c = split_three(-log_total[pl.ds(head, 1), :])
        query_ext[pl.ds(head_size, 16), :] = jnp.where(
            row_id == 0, 1.0, jnp.where(row_id == 1, a, jnp.where(row_id == 2, b, jnp.where(row_id == 3, c, 0.0)))
        ).astype(bf16)
        row_dot = jnp.sum(
            grad.astype(f32) * attended[pl.ds(first, head_size), :], axis=0, keepdims=True
        )
        a, b, c = split_three(-row_dot)
        grad_ext[pl.ds(head_size, 16), :] = jnp.where(
            row_id == 0, a, jnp.where(row_id == 1, b, jnp.where(row_id == 2, c, 0.0))
        ).astype(bf16)
        for row_start in range(0, span, LANE):
            rows = slice(row_start, row_start + LANE)
            for col_start in range(0, span, half):
                cols = slice(col_start, col_start + half)
                place = pl.ds(window(core, row_start, col_start, half, span), half)
                part = dot(query_ext[:, rows], key_ext[:, cols], 0, 0)
                part = jnp.exp(part + table[:, place])
                slope = part * dot(grad_ext[:, rows], value_ext[:, cols], 0, 0)
                weights[rows, cols] = part.astype(bf16)
                slopes[rows, cols] = slope.astype(bf16)
                sums[:, place] += slope
        grads[pl.ds(first, head_size), :] = dot(key, slopes[...], 1, 1).astype(bf16)
        grads[pl.ds(width + first, head_size), :] = dot(query, slopes[...], 1, 0).astype(bf16)
        grads[pl.ds(2 * width + first, head_size), :] = dot(grad, weights[...], 1, 0).astype(bf16)
        folded = sums[...]
        count = LANE
        while count > 8:
            count //= 2
            folded = folded[:count] + pltpu.roll(folded[count:], 2 * span - count, 1)
        diagonals[pl.ds(pl.multiple_of(head * 8, 8), 8), :] = folded
        return 0

    lax.fori_loop(0, head_count, one_head, 0)


def attention_backward(qkv, grad_mixture, attended, log_total, bias_row, key_mask, head_count):
    wide, span = qkv.shape
    width = wide // 3
    head_size = width // head_count
    ext = pltpu.VMEM((head_size + 16, span), bf16)
    square = pltpu.VMEM((span, span), bf16)
    slab = pltpu.VMEM((LANE, 2 * span), f32)
    return pl.pallas_call(
        functools.partial(backward_kernel, head_count, head_size),
        out_shape=(
            jax.ShapeDtypeStruct((wide, span), bf16),
            jax.ShapeDtypeStruct((8 * head_count, 2 * span), f32),
        ),
        scratch_shapes=[slab, slab, square, square, ext, ext, ext, ext],
        compiler_params=pltpu.CompilerParams(vmem_limit_bytes=VMEM_BYTES),
        name="attention_backward",
    )(qkv, grad_mixture, attended, log_total, bias_row, key_mask)


def rms_parts(values):
    return lax.rsqrt(jnp.mean(values * values, axis=-1, keepdims=True) + eps_norm)


def norm_back(grad, values, gain, scale):
    weighted = grad * gain
    inner = jnp.mean(weighted * values, axis=-1, keepdims=True)
    return scale * weighted - values * (scale * scale * scale) * inner, jnp.sum(grad * values * scale, axis=0)


def gelu_both(value):
    root = 0.7978845608028654
    square = value * value
    bent = jnp.tanh(value * (root + root * 0.044715 * square))
    up = 0.5 * bent + 0.5
    active = value * up
    slope = up + active * ((1.0 - bent) * (root + 3 * 0.044715 * root * square))
    return active, slope


AXES = ("y", "x", "h", "l")


class Sums:
    def __init__(self, kernel, blocks, rows, columns, order, buffers):
        self.kernel, self.blocks, self.order, self.buffers = kernel, blocks, order, buffers
        self.rows, self.columns = pl.ds(*rows), pl.ds(*columns)
        self.copies = []
        for step, axis in enumerate(order):
            source = self.place(step, axis, 1 - kernel.at[axis])
            self.copies.append(kernel.copy(source, buffers[step], kernel.partner[axis]))

    def place(self, step, axis, which):
        picks = []
        for other in AXES:
            if other == axis:
                picks.append(pl.ds(which, 1))
            else:
                picks.append(pl.ds(self.kernel.at[other], 1) if other in self.order[:step] else pl.ds(0, 2))
        return self.blocks.at[(*picks, self.rows, self.columns)]

    def begin(self, step):
        self.copies[step].start()

    def end(self, step, result=None):
        self.copies[step].wait()
        axis = self.order[step]
        kept = self.place(step, axis, self.kernel.at[axis])
        buffer = self.buffers[step]
        for index in itertools.product(*(range(count) for count in buffer.shape[:4])):
            total = kept[index].astype(f32) + buffer[index].astype(f32)
            if result is None:
                kept[index] = total.astype(bf16)
            else:
                result[self.rows, self.columns] = total

    def shapes(rows, columns, order):
        return [
            (*(1 if axis in order[: step + 1] else 2 for axis in AXES), rows, columns) for step in range(len(order))
        ]


WAYS = (("x", "y", "l", "h"), ("y", "x", "l", "h"), ("l", "h", "x", "y"))
PARTS = {
    "out": [((32 * i, 32), (0, 768), WAYS[i]) for i in range(3)],
    "in": [((32 * i, 32), (0, 768), WAYS[i]) for i in range(3)],
    "most": [((0, 48), (0, 640), WAYS[0]), ((0, 48), (640, 512), WAYS[1])],
    "last": [((0, 48), (0, 256), WAYS[0]), ((0, 48), (256, 128), WAYS[1])],
}
GROUP_SHAPE = {"out": (96, 768), "in": (96, 768), "most": (48, 1152), "last": (48, 384)}
GROUPS = ("out", "in", "most", "last")


class Kernel:
    pass


def block_kernel(head_count, language_ids, length_ids, tokens, cotangent, w_query, w_key, w_value, w_output, w_in, w_out, lang_table, first_gain, second_gain, buckets, bias_table, *refs):
    k = Kernel()
    names = (
        "output", "grad_tokens", "o_query", "o_key", "o_value", "o_output", "o_in", "o_out",
        "o_lang", "o_first", "o_second", "o_bias", "tok", "meta_out", "meta_in", "wt",
        "wo", "win", "wout", "normed_t", "qkv", "att", "mix", "gmix",
        "middle", "acc", "ns", "slope", "acts", "act_in", "gh_in", "cot",
        "proj", "out_rows", "table", "sums", "prob", "ds", "key_ext", "value_ext",
        "query_ext", "grad_ext", "bias_rows", "back_rows", "distance", "small", "fin_send", "fin_recv",
        "fin_last", "result", "result_last", "g_out", "g_in", "g_most", "g_last",
    )
    for name, ref in zip(names, refs):
        setattr(k, name, ref)
    rest = list(refs[len(names):])
    send_sem, recv_sem, load_sem = rest[-3:]
    rest = rest[:-3]
    dp, z = lax.axis_index("dp"), lax.axis_index("blk")
    core = dp % 2
    mate_core = 1 - core
    base = dp - core
    k.dp = dp
    k.at = {"x": (dp // 2) % 2, "y": (dp // 4) % 2, "h": z // 2, "l": z % 2}
    k.partner = {"x": (dp ^ 2, z), "y": (dp ^ 4, z), "h": (dp, z ^ 2), "l": (dp, z ^ 1)}
    mate = (base + mate_core, z)
    used = [0]
    width = lang_table.shape[1]
    span = k.qkv.shape[1]
    half, quarter = span // 2, span // 4
    mine = width // 2
    head_size = mine // head_count
    tile = mine
    tiles = k.win.shape[1] // width

    def take(count=1):
        used[0] += count
        return used[0] - count

    def copy(source, target, device, slot=None):
        slot = take() if slot is None else slot
        return pltpu.make_async_remote_copy(
            src_ref=source,
            dst_ref=target,
            send_sem=send_sem.at[slot],
            recv_sem=recv_sem.at[slot],
            device_id=device,
            device_id_type=MESH,
        )

    k.copy = copy

    barrier = pltpu.get_barrier_semaphore()
    friends = [(base + (core + turn) % 2, z ^ far) for turn in range(2) for far in range(4) if turn or far]
    friends += [k.partner["x"], k.partner["y"], (dp ^ 6, z)]
    for friend in friends:
        pl.semaphore_signal(barrier, inc=1, device_id=friend, device_id_type=MESH)

    loads = []

    def load(source, target):
        item = pltpu.make_async_copy(source, target, load_sem.at[len(loads)])
        item.start()
        loads.append(item)

    own_lanes = pl.ds(pl.multiple_of(core * mine, LANE), mine)
    mate_lanes = pl.ds(pl.multiple_of(mate_core * mine, LANE), mine)
    def stage_rows(index):
        return pl.ds((index % 2) * width, width)

    def stage_lanes(index):
        return pl.ds((index // 2) * mine, mine)

    for index, source in enumerate((w_query, w_key, w_value)):
        load(source.at[:, own_lanes], k.acts.at[stage_rows(index), stage_lanes(index)])
    load(w_output.at[own_lanes], k.wo.at[pl.ds(0, mine)])
    load(w_output.at[mate_lanes], k.wo.at[pl.ds(mine, mine)])
    load(w_in, k.win)
    load(w_out, k.wout)

    row_id = lax.broadcasted_iota(jnp.int32, k.meta_out.shape[1:], 0)
    for index in range(2):
        k.meta_out[index] = jnp.where(row_id == 0, language_ids[index], length_ids[index])
    pl.semaphore_wait(barrier, len(friends))

    side = z % 2

    class Route:
        def __init__(self, pick, target):
            self.slots = take(2)
            self.items = []
            for index in range(2):
                device = (base + z // 2, 2 * core + index)
                here = (z // 2 == core) & (2 * core + index == z)
                source = pick(index)
                far = pltpu.make_async_remote_copy(
                    src_ref=source,
                    dst_ref=target(side),
                    send_sem=send_sem.at[self.slots + index],
                    recv_sem=recv_sem.at[self.slots + side],
                    device_id=device,
                    device_id_type=MESH,
                )
                near = pltpu.make_async_copy(source, target(side), recv_sem.at[self.slots + side])
                self.items.append((here, far, near))
            self.arrivals = [copy(target(j), target(j), mate, self.slots + j) for j in range(2)]

        def start(self):
            for here, far, near in self.items:
                pl.when(here)(near.start)
                pl.when(jnp.logical_not(here))(far.start)

        def arrive(self, index):
            self.arrivals[index].wait_recv()

        def close(self):
            for here, far, _ in self.items:
                pl.when(jnp.logical_not(here))(far.wait_send)

    def part_rows(index):
        return pl.ds(pl.multiple_of(index * quarter, quarter), quarter)

    way_meta = Route(lambda i: k.meta_out.at[i], lambda j: k.meta_in.at[j])
    way_tokens = Route(lambda i: tokens.at[i], lambda j: k.tok.at[part_rows(j)])
    way_meta.start()
    way_tokens.start()

    all_heads, bucket_count = bias_table.shape
    places = 2 * span

    def bucket_hot():
        return (lax.broadcasted_iota(jnp.int32, (bucket_count, places), 0) == buckets[...]).astype(f32)

    pick = (
        lax.broadcasted_iota(jnp.int32, (all_heads, 8), 0)
        == lax.broadcasted_iota(jnp.int32, (all_heads, 8), 1) + core * head_count
    ) & (lax.broadcasted_iota(jnp.int32, (all_heads, 8), 1) < head_count)

    def exact(left, right, left_dim, right_dim):
        return lax.dot_general(
            left, right, (((left_dim,), (right_dim,)), ((), ())), precision=highest, preferred_element_type=f32
        )

    own_bias = exact(bias_table[...], pick.astype(f32), 0, 0)
    bias_rows = exact(own_bias, bucket_hot(), 0, 0)
    k.bias_rows[...] = bias_rows
    flip = (
        lax.broadcasted_iota(jnp.int32, (LANE, LANE), 0) + lax.broadcasted_iota(jnp.int32, (LANE, LANE), 1) == LANE - 1
    ).astype(f32)
    for first in range(0, places, LANE):
        k.back_rows[:, first : first + LANE] = exact(bias_rows[:, places - LANE - first : places - first], flip, 1, 0)
    k.back_rows[...] = pltpu.roll(k.back_rows[...], 1, 1)
    for index in range(3):
        loads[index].wait()
        k.wt[index * mine : (index + 1) * mine, :] = k.acts[stage_rows(index), stage_lanes(index)].T

    for index in range(2):
        way_meta.arrive(index)
    language = k.meta_in[0, 0:1, :width]
    length = k.meta_in[0, 1:2, :span]
    embedding = jnp.zeros((1, width), f32)
    for index in range(8):
        embedding = embedding + jnp.where(language == index, lang_table[index : index + 1, :].astype(f32), 0.0)
    gain_first, gain_second = first_gain[...].reshape(1, width), second_gain[...].reshape(1, width)
    position = (lax.broadcasted_iota(jnp.int32, (1, span), 1) + half * core) % span
    key_mask = jnp.where(position < length, 0.0, masked_score)

    relays = [copy(k.tok.at[part_rows(j)], k.tok.at[part_rows(2 + j)], mate) for j in range(2)]
    way_cotangent = Route(lambda i: cotangent.at[i], lambda j: k.cot.at[part_rows(j)])

    def project(index):
        rows = slice(index * quarter, (index + 1) * quarter)
        values = k.tok[rows, :].astype(f32) + embedding
        normed = (values * rms_parts(values) * gain_first).astype(bf16)
        k.normed_t[:, rows] = normed.T
        k.qkv[:, rows] = dot(k.wt[...], k.normed_t[:, rows], 1, 0).astype(bf16)

    for index in range(2):
        way_tokens.arrive(index)
        relays[index].start()
    way_cotangent.start()
    for index in range(2):
        project(index)
    for index in range(2):
        relays[index].wait_recv()
        project(2 + index)

    step = 2 * LANE
    block = k.prob.shape[0]
    ext_row = lax.broadcasted_iota(jnp.int32, (16, span), 0)
    tail = pl.ds(head_size, 16)
    k.key_ext[tail, :] = jnp.where(ext_row == 0, key_mask, jnp.where(ext_row < 4, 1.0, 0.0)).astype(bf16)
    k.query_ext[tail, :] = jnp.where(ext_row == 0, 1.0, 0.0).astype(bf16)
    k.value_ext[tail, :] = jnp.where(ext_row < 3, 1.0, 0.0).astype(bf16)
    mix_slots = take(2 * head_count)

    def mix_copies(head):
        rows = pl.ds(pl.multiple_of(head * head_size, head_size), head_size)
        far = pl.ds(pl.multiple_of(mine + head * head_size, head_size), head_size)
        return [
            copy(
                k.mix.at[rows, pl.ds(side_at * half, half)],
                k.mix.at[far, pl.ds((1 - side_at) * half, half)],
                mate,
                mix_slots + 2 * head + side_at,
            )
            for side_at in range(2)
        ]

    def place_in(count, start):
        lane = (start // count) * step
        return slice(start % count, start % count + LANE), slice(lane, lane + step)

    def forward_head(head, _):
        first = pl.multiple_of(head * head_size, head_size)
        row = k.back_rows[pl.ds(head, 1), :]
        k.table[...] = pltpu.roll(jnp.broadcast_to(row, k.table.shape), 0, 1, stride=1, stride_axis=0)
        k.query_ext[pl.ds(0, head_size), :] = k.qkv[pl.ds(first, head_size), :]
        k.key_ext[pl.ds(0, head_size), :] = k.qkv[pl.ds(mine + first, head_size), :]
        k.value_ext[pl.ds(0, head_size), :] = k.qkv[pl.ds(2 * mine + first, head_size), :]
        for row_start in range(0, span, step):
            query = k.query_ext[:, row_start : row_start + step]
            best = None
            for start in range(0, span, LANE):
                part = dot(k.key_ext[:, start : start + LANE], query, 0, 0)
                part = part + k.table[:, pl.ds(window(core, start, row_start, half, span), step)]
                k.acc[place_in(half, start)] = part
                folded = jnp.max(part.reshape(LANE // 8, 8, step), axis=0)
                best = folded if best is None else jnp.maximum(best, folded)
            top = jnp.max(best, axis=0, keepdims=True)
            for start in range(0, span, LANE):
                k.prob[place_in(block, start)] = jnp.exp(k.acc[place_in(half, start)] - top).astype(bf16)
            summed = None
            for start in range(0, span, block):
                lanes = place_in(block, start)[1]
                more = dot(k.value_ext[:, start : start + block], k.prob[:, lanes], 1, 0)
                summed = more if summed is None else summed + more
            total = summed[head_size : head_size + 1]
            part = summed[:head_size] / total
            k.att[pl.ds(first, head_size), row_start : row_start + step] = part
            k.mix[pl.ds(first, head_size), row_start : row_start + step] = part.astype(bf16)
            k.distance[pl.ds(head, 1), row_start : row_start + step] = top + jnp.log(total)
        for item in mix_copies(head):
            item.start()
        return 0

    lax.fori_loop(0, head_count, forward_head, 0)

    loads[3].wait()
    loads[4].wait()
    for head in range(head_count):
        for item in mix_copies(head):
            item.wait_recv()
    for index in range(2):
        rows = slice(index * quarter, (index + 1) * quarter)
        values = k.tok[rows, :].astype(f32) + embedding + dot(k.mix[:, rows], k.wo[...], 0, 0)
        k.middle[rows, :] = values
        k.acc[rows, :] = values
        k.ns[rows, :] = (values * rms_parts(values) * gain_second).astype(bf16)
    ns_copy = copy(k.ns.at[pl.ds(0, half)], k.ns.at[pl.ds(half, half)], mate)
    ns_copy.start()
    loads[5].wait()
    loads[6].wait()
    act_slots = take(tiles)
    gh_slots = take(tiles)

    def tile_rows(index):
        return pl.ds(pl.multiple_of(index * half, half), half)

    def wide_lanes(index):
        return pl.ds(pl.multiple_of(index * width, width), width)

    def tile_lanes(index):
        return pl.ds(pl.multiple_of(index * tile, tile), tile)

    def act_copy(index):
        return copy(k.acts.at[tile_rows(index), mate_lanes], k.act_in.at[:, tile_lanes(index)], mate, act_slots + index)

    def gh_copy(index):
        return copy(k.acts.at[tile_rows(index), mate_lanes], k.gh_in.at[:, tile_lanes(index)], mate, gh_slots + index)

    def forward_tile(index, _):
        lanes = wide_lanes(index)
        for first in range(0, half, quarter):
            rows = pl.ds(pl.multiple_of(index * half + first, quarter), quarter)
            active, slope = gelu_both(dot(k.ns[first : first + quarter], k.win[:, lanes], 1, 0))
            active = active.astype(bf16)
            k.acts[rows, :] = active
            k.slope[rows, :] = slope.astype(bf16)
            k.acc[first : first + quarter] += dot(active, k.wout[lanes, :], 1, 0)
        act_copy(index).start()
        return 0

    lax.fori_loop(0, tiles, forward_tile, 0)
    way_output = Route(lambda i: k.out_rows.at[part_rows(i)], lambda j: k.output.at[j])
    k.out_rows[...] = k.acc[...].astype(bf16)
    way_output.start()

    cot_relays = [copy(k.cot.at[part_rows(j)], k.cot.at[part_rows(2 + j)], mate) for j in range(2)]
    for index in range(2):
        way_cotangent.arrive(index)
        cot_relays[index].start()
    for index in range(2):
        cot_relays[index].wait_recv()
    parts = {}
    for group in GROUPS:
        parts[group] = []
        for rows, columns, order in PARTS[group]:
            parts[group].append(Sums(k, getattr(k, "g_" + group), rows, columns, order, [rest.pop(0) for _ in order]))

    def begin(group, at):
        for part in parts[group]:
            part.begin(at)

    def end(group, at, result=None):
        for part in parts[group]:
            part.end(at, result)
            if at < 3:
                part.begin(at + 1)

    def out_tile(index, _):
        act_copy(index).wait_recv()
        grad = dot(k.acts[tile_rows(index), own_lanes], k.cot[:half], 0, 0)
        grad = grad + dot(k.act_in[:, tile_lanes(index)], k.cot[half:], 0, 0)
        k.g_out[index // 2, index % 2] = grad.reshape(2, 2, tile // 4, width).astype(bf16)
        return 0

    lax.fori_loop(0, tiles, out_tile, 0)
    begin("out", 0)

    def put_blocks(target, grad, rows, lanes, halves=(0, 1)):
        each = grad.shape[0] // 32
        for index in range(4):
            for at in range(4):
                first = (8 * index + at) * each
                both = jnp.concatenate([grad[first : first + each], grad[first + 4 * each : first + 5 * each]])
                up = index // 2
                up = halves[up] if up < len(halves) else up
                target[up, index % 2, at // 2, at % 2, rows, lanes] = both.astype(bf16)

    k.acc[...] = jnp.zeros_like(k.acc)
    for index in range(tiles):
        act_copy(index).wait_send()

    def back_tile(index, _):
        lanes = wide_lanes(index)
        grad = dot(k.cot[:half], k.wout[lanes, :], 1, 1)
        grad = (grad * k.slope[tile_rows(index), :].astype(f32)).astype(bf16)
        k.acts[tile_rows(index), :] = grad
        gh_copy(index).start()
        k.act_in[:, tile_lanes(index)] = k.acts[tile_rows(index), own_lanes]
        k.acc[...] += dot(grad, k.win[:, lanes], 1, 1)
        return 0

    lax.fori_loop(0, tiles, back_tile, 0)
    ns_copy.wait_recv()
    for index in range(tiles):
        gh_copy(index).wait_recv()
    for index in range(2):
        lanes = slice(index * width, (index + 1) * width)
        grad = dot(k.ns[:half], k.act_in[:, lanes], 0, 0) + dot(k.ns[half:], k.gh_in[:, lanes], 0, 0)
        put_blocks(k.g_in, grad, pl.ds(48 * index, 48), pl.ds(0, width))
    begin("in", 0)

    gain_grad = jnp.zeros((1, width), f32)
    for index in range(2):
        rows = slice(index * quarter, (index + 1) * quarter)
        values, grad = k.middle[rows, :], k.acc[rows, :]
        back, part = norm_back(grad, values, gain_second, rms_parts(values))
        gain_grad = gain_grad + part.reshape(1, width)
        back = back + k.cot[rows, :].astype(f32)
        k.middle[rows, :] = back
        k.proj[rows, :] = back.astype(bf16)
    proj_copy = copy(k.proj, k.tok.at[pl.ds(half, half)], mate)
    proj_copy.start()
    proj_copy.wait_recv()
    k.gmix[:, :half] = dot(k.wo[:mine], k.proj[...], 1, 1).astype(bf16)
    k.gmix[:, half:] = dot(k.wo[:mine], k.tok[half:], 1, 1).astype(bf16)
    grad = dot(k.mix[:, :half], k.proj[:, own_lanes], 1, 0) + dot(k.mix[:, half:], k.tok[half:, own_lanes], 1, 0)
    put_blocks(k.g_most, grad, pl.ds(0, 48), pl.ds(0, mine), (core, mate_core))
    end("out", 0)

    def backward_head(head, _):
        first = pl.multiple_of(head * head_size, head_size)
        row = k.bias_rows[pl.ds(head, 1), :]
        k.table[...] = pltpu.roll(jnp.broadcast_to(row, k.table.shape), 0, 1, stride=1, stride_axis=0)
        k.sums[...] = jnp.zeros_like(k.sums)
        query_rows, key_rows = pl.ds(first, head_size), pl.ds(mine + first, head_size)
        value_rows = pl.ds(2 * mine + first, head_size)
        query, key = k.qkv[query_rows, :], k.qkv[key_rows, :]
        grad = k.gmix[pl.ds(first, head_size), :]
        k.key_ext[pl.ds(0, head_size), :] = key
        k.value_ext[pl.ds(0, head_size), :] = k.qkv[value_rows, :]
        k.query_ext[pl.ds(0, head_size), :] = query
        k.grad_ext[pl.ds(0, head_size), :] = grad

        def three(value, start):
            found = jnp.where(ext_row == 0, 1.0, 0.0) if start else 0.0
            for at, piece in enumerate(split_three(value)):
                found = jnp.where(ext_row == start + at, piece, found)
            return found.astype(bf16)

        k.query_ext[tail, :] = three(-k.distance[pl.ds(head, 1), :span], 1)
        row_dot = jnp.sum(grad.astype(f32) * k.att[pl.ds(first, head_size), :], axis=0, keepdims=True)
        k.grad_ext[tail, :] = three(-row_dot, 0)
        grad_key = grad_value = None
        for outer in range(0, span, block):
            for row_start in range(outer, outer + block, LANE):
                rows = slice(row_start, row_start + LANE)
                inner = slice(row_start - outer, row_start - outer + LANE)
                for col_start in range(0, span, half):
                    cols = slice(col_start, col_start + half)
                    place = pl.ds(window(core, row_start, col_start, half, span), half)
                    part = dot(k.query_ext[:, rows], k.key_ext[:, cols], 0, 0)
                    part = jnp.exp(part + k.table[:, place])
                    slope = part * dot(k.grad_ext[:, rows], k.value_ext[:, cols], 0, 0)
                    k.prob[inner, cols] = part.astype(bf16)
                    k.ds[inner, cols] = slope.astype(bf16)
                    k.sums[:, place] += slope
            wide = slice(outer, outer + block)
            k.qkv[query_rows, wide] = dot(key, k.ds[...], 1, 1).astype(bf16)
            more_key = dot(query[:, wide], k.ds[...], 1, 0)
            more_value = dot(grad[:, wide], k.prob[...], 1, 0)
            grad_key = more_key if grad_key is None else grad_key + more_key
            grad_value = more_value if grad_value is None else grad_value + more_value
        k.qkv[key_rows, :] = grad_key.astype(bf16)
        k.qkv[value_rows, :] = grad_value.astype(bf16)
        folded = k.sums[...]
        count = LANE
        while count > 8:
            count //= 2
            folded = folded[:count] + pltpu.roll(folded[count:], 2 * span - count, 1)
        at = lax.broadcasted_iota(jnp.int32, folded.shape, 0)
        for bit in (4, 2, 1):
            folded = jnp.where(at % (2 * bit) >= bit, pltpu.roll(folded, 2 * span - bit, 1), folded)
        k.back_rows[pl.ds(head, 1), :] = jnp.sum(folded, axis=0, keepdims=True)
        for at, tick in ticks.items():
            pl.when(head == at)(tick)
        return 0

    most_heads = 4

    def after_fourth():
        for index in range(3):
            rows = slice(index * mine, index * mine + most_heads * head_size)
            grad = dot(k.normed_t[...], k.qkv[rows, :], 1, 1)
            first = mine + index * most_heads * head_size
            put_blocks(k.g_most, grad, pl.ds(0, 48), pl.ds(first, most_heads * head_size))
        begin("most", 0)

    def after_fifth():
        end("in", 1)
        end("out", 2)

    ticks = {1: lambda: end("in", 0), 2: lambda: end("out", 1), 3: after_fourth, 4: after_fifth}
    lax.fori_loop(0, head_count, backward_head, 0)
    last = (head_count - most_heads) * head_size

    for index in range(2):
        way_output.arrive(index)
    way_output.close()
    ns_copy.wait_send()
    k.ns[:half] = dot(k.qkv[:, half:], k.wt[...], 0, 0).astype(bf16)
    gn_copy = copy(k.ns.at[pl.ds(0, half)], k.ns.at[pl.ds(half, half)], mate)
    gn_copy.start()
    for index in range(3):
        rows = slice(index * mine + most_heads * head_size, (index + 1) * mine)
        grad = dot(k.normed_t[...], k.qkv[rows, :], 1, 1)
        put_blocks(k.g_last, grad, pl.ds(0, 48), pl.ds(index * last, last))
    begin("last", 0)
    end("in", 2)
    end("out", 3, k.o_out)
    gn_copy.wait_recv()
    first_grad = jnp.zeros((1, width), f32)
    lang_grad = jnp.zeros((1, width), f32)
    for index in range(2):
        rows = slice(index * quarter, (index + 1) * quarter)
        grad = dot(k.qkv[:, rows], k.wt[...], 0, 0) + k.ns[half + index * quarter : half + (index + 1) * quarter, :].astype(f32)
        values = k.tok[rows, :].astype(f32) + embedding
        back, part = norm_back(grad, values, gain_first, rms_parts(values))
        first_grad = first_grad + part.reshape(1, width)
        back = back + k.middle[rows, :]
        lang_grad = lang_grad + jnp.sum(back, axis=0, keepdims=True)
        k.out_rows[rows, :] = back.astype(bf16)
    way_grad = Route(lambda i: k.out_rows.at[part_rows(i)], lambda j: k.grad_tokens.at[j])
    way_grad.start()

    at_row = lax.broadcasted_iota(jnp.int32, (16, width), 0)
    mixed = jnp.where(at_row == language, lang_grad, 0.0)
    mixed = jnp.where(at_row == 8, first_grad, jnp.where(at_row == 9, gain_grad, mixed))
    k.small[0, :, :width] = mixed
    head_row = lax.broadcasted_iota(jnp.int32, k.back_rows.shape, 0)
    by_bucket = exact(jnp.where(head_row < head_count, k.back_rows[...], 0.0), bucket_hot(), 1, 1)
    spread = (
        lax.broadcasted_iota(jnp.int32, (16, 8), 0) == lax.broadcasted_iota(jnp.int32, (16, 8), 1) + core * head_count
    ) & (lax.broadcasted_iota(jnp.int32, (16, 8), 1) < head_count)
    k.small[0, :, width:] = jnp.zeros((16, span - width), f32)
    k.small[0, :, width : width + bucket_count] = exact(spread.astype(f32), by_bucket, 1, 0)
    def small_step(first, devices):
        items = [copy(k.small.at[first], k.small.at[first + 1 + i], device) for i, device in enumerate(devices)]
        for item in items:
            item.start()

        def finish():
            for item in items:
                item.wait()
            total = k.small[first]
            for i in range(len(items)):
                total = total + k.small[first + 1 + i]
            return total

        return finish

    finish = small_step(0, [mate])
    end("in", 3, k.result)

    each = 24
    own_part, mate_part = pl.ds(pl.multiple_of(core * each, 8), each), pl.ds(pl.multiple_of(mate_core * each, 8), each)

    def rows_of(which, first):
        return pl.ds(pl.multiple_of(first + which * each, 8), each)

    for index in range(tiles):
        lanes = slice((index % 2) * tile, (index % 2 + 1) * tile)
        to_lanes = pl.ds(pl.multiple_of((2 * index + core) * tile, LANE), tile)
        k.o_in[:, to_lanes] = k.result[rows_of(core, 48 * (index // 2)), lanes]
        k.fin_send[:, index * tile : (index + 1) * tile] = k.result[rows_of(mate_core, 48 * (index // 2)), lanes]
    in_copy = copy(k.fin_send, k.fin_recv, mate)
    in_copy.start()
    end("most", 0)
    k.small[2] = finish()
    finish = small_step(2, [(dp ^ 2, z), (dp ^ 4, z), (dp ^ 6, z)])
    end("last", 0)
    end("most", 1)
    in_copy.wait_recv()
    for index in range(tiles):
        to_lanes = pl.ds(pl.multiple_of((2 * index + mate_core) * tile, LANE), tile)
        k.o_in[:, to_lanes] = k.fin_recv[:, index * tile : (index + 1) * tile]
    end("last", 1)
    k.small[6] = finish()
    finish = small_step(6, [(dp, z ^ turn) for turn in range(1, 4)])
    end("most", 2)
    end("last", 2)
    total = finish()
    flat = dp * 4 + z
    keep = (
        lax.broadcasted_iota(jnp.int32, (width, each), 0) == lax.broadcasted_iota(jnp.int32, (width, each), 1) + flat * each
    ).astype(f32)
    shares = exact(total[:, :width], keep, 1, 0)
    k.o_lang[...] = shares[:8]
    k.o_first[...] = shares[8:9]
    k.o_second[...] = shares[9:10]
    k.o_bias[...] = total[:all_heads, width : width + bucket_count]
    wide = GROUP_SHAPE["most"][1]
    end("most", 3, k.result_last.at[:, pl.ds(0, wide)])
    end("last", 3, k.result_last.at[:, pl.ds(wide, mine)])
    in_copy.wait_send()
    k.fin_send[:, : wide + mine] = k.result_last[mate_part, : wide + mine]
    last_copy = copy(k.fin_send, k.fin_last, mate)
    last_copy.start()


    def put_projections(read, lanes):
        k.o_output[:, lanes] = read(0, mine)
        for index, target in enumerate((k.o_query, k.o_key, k.o_value)):
            size = most_heads * head_size
            target[:, lanes] = jnp.concatenate(
                [read(mine + index * size, size), read(wide + index * last, last)], axis=1
            )

    put_projections(lambda first, size: k.result_last[own_part, first : first + size], own_lanes)
    last_copy.wait_recv()
    put_projections(lambda first, size: k.fin_last[:, first : first + size], mate_lanes)

    for item in (way_meta, way_tokens, way_cotangent, way_grad):
        item.close()
    for index in range(2):
        way_grad.arrive(index)
    for head in range(head_count):
        for item in mix_copies(head):
            item.wait_send()
    for index in range(tiles):
        gh_copy(index).wait_send()
    for item in (*relays, *cot_relays, proj_copy, gn_copy, last_copy):
        item.wait_send()


def hand_on(*refs):
    count = len(refs) // 2
    for source, target in zip(refs[:count], refs[count:]):
        target[...] = source[...]


def local(
    tokens,
    language,
    lengths,
    rel_bucket,
    lang_table,
    gain_first,
    w_query,
    w_key,
    w_value,
    w_output,
    bias_table,
    gain_second,
    w_in,
    w_out,
    cotangent,
):
    seqs, rows, width = tokens.shape
    span = rows * lax.axis_size("blk")
    half, mine = span // 2, width // 2
    bucket_count, all_heads = bias_table.shape
    head_count = all_heads // 2
    ff_width = w_in.shape[1]
    devices = lax.axis_size("dp") * lax.axis_size("blk")
    each, each_out = width // devices, ff_width // devices
    tiles = ff_width // width
    buckets = jnp.pad(rel_bucket, (1, 0), constant_values=-1)[None]
    vmem, anywhere = pl.BlockSpec(memory_space=pltpu.VMEM), pl.BlockSpec(memory_space=pl.ANY)
    shape = jax.ShapeDtypeStruct
    ext = pltpu.VMEM((mine // head_count + 16, span), bf16)
    sum_buffers = [
        pltpu.VMEM(found, bf16)
        for group in GROUPS
        for part_rows, part_columns, order in PARTS[group]
        for found in Sums.shapes(part_rows[1], part_columns[1], order)
    ]
    found = pl.pallas_call(
        functools.partial(block_kernel, head_count),
        out_shape=(
            shape(tokens.shape, bf16),
            shape(tokens.shape, bf16),
            *[shape((each, width), f32)] * 4,
            shape((each, ff_width), f32),
            shape((each_out, width), f32),
            shape((8, each), f32),
            shape((1, each), f32),
            shape((1, each), f32),
            shape(bias_table.shape[::-1], f32),
        ),
        in_specs=[pl.BlockSpec(memory_space=pltpu.SMEM)] * 2 + [anywhere] * 8 + [vmem] * 5,
        out_specs=(anywhere, anywhere) + (vmem,) * 10,
        scratch_shapes=[
            pltpu.VMEM((span, width), bf16),
            pltpu.VMEM((seqs, 8, span), jnp.int32),
            pltpu.VMEM((seqs, 8, span), jnp.int32),
            pltpu.VMEM((3 * mine, width), bf16),
            pltpu.VMEM((width, width), bf16),
            pltpu.VMEM((width, ff_width), bf16),
            pltpu.VMEM((ff_width, width), bf16),
            pltpu.VMEM((width, span), bf16),
            pltpu.VMEM((3 * mine, span), bf16),
            pltpu.VMEM((mine, span), f32),
            pltpu.VMEM((width, span), bf16),
            pltpu.VMEM((mine, span), bf16),
            pltpu.VMEM((half, width), f32),
            pltpu.VMEM((half, width), f32),
            pltpu.VMEM((span, width), bf16),
            pltpu.VMEM((tiles * half, width), bf16),
            pltpu.VMEM((tiles * half, width), bf16),
            pltpu.VMEM((half, tiles * mine), bf16),
            pltpu.VMEM((half, tiles * mine), bf16),
            pltpu.VMEM((span, width), bf16),
            pltpu.VMEM((half, width), bf16),
            pltpu.VMEM((half, width), bf16),
            pltpu.VMEM((LANE, 2 * span), f32),
            pltpu.VMEM((LANE, 2 * span), f32),
            pltpu.VMEM((half // 2, span), bf16),
            pltpu.VMEM((half // 2, span), bf16),
            ext,
            ext,
            ext,
            ext,
            pltpu.VMEM((8, 2 * span), f32),
            pltpu.VMEM((8, 2 * span), f32),
            pltpu.VMEM((8, span), f32),
            pltpu.VMEM((11, 16, span), f32),
            pltpu.VMEM((each, 2 * width), f32),
            pltpu.VMEM((each, 2 * width), f32),
            pltpu.VMEM((each, 2 * width), f32),
            pltpu.VMEM((4 * each, width), f32),
            pltpu.VMEM((2 * each, 2 * width), f32),
            *[pltpu.VMEM((2, 2, 2, 2, *GROUP_SHAPE[group]), bf16) for group in GROUPS],
            *sum_buffers,
            pltpu.SemaphoreType.DMA((104,)),
            pltpu.SemaphoreType.DMA((104,)),
            pltpu.SemaphoreType.DMA((8,)),
        ],
        compiler_params=pltpu.CompilerParams(
            collective_id=0, has_side_effects=True, vmem_limit_bytes=VMEM_BYTES
        ),
        name="encoder_block",
    )(
        language,
        lengths,
        tokens,
        cotangent,
        w_query,
        w_key,
        w_value,
        w_output,
        w_in,
        w_out,
        lang_table,
        gain_first,
        gain_second,
        buckets,
        bias_table.T,
    )
    found = pl.pallas_call(
        hand_on,
        out_shape=tuple(shape(part.shape, part.dtype) for part in found),
        in_specs=[vmem] * len(found),
        out_specs=tuple([vmem] * len(found)),
        compiler_params=pltpu.CompilerParams(vmem_limit_bytes=VMEM_BYTES),
        name="hand_on",
    )(*found)
    output, grad_tokens, query, key, value, out, grad_in, grad_out, lang, first, second, bias = found
    return output, grad_tokens, lang, first[0], query, key, value, out, bias.T, second[0], grad_in, grad_out


def local_plain(
    tokens,
    language,
    lengths,
    rel_bucket,
    lang_table,
    gain_first,
    w_query,
    w_key,
    w_value,
    w_output,
    bias_table,
    gain_second,
    w_in,
    w_out,
    cotangent,
):
    dp_size, blk_size = lax.axis_size("dp"), lax.axis_size("blk")
    device, place = lax.axis_index("dp"), lax.axis_index("blk")
    core = device % 2
    odd = place % 2 == 1
    width = tokens.shape[-1]
    bucket_count, all_heads = bias_table.shape
    head_count = all_heads // 2
    mine = width // 2
    span = tokens.shape[1] * blk_size
    half = span // 2
    ff_width = w_in.shape[1]

    own_tokens = to_rows(tokens, odd)
    own_cotangent = to_rows(cotangent, odd)
    other_tokens = swap_core(own_tokens)
    ids = jnp.stack([language, lengths])
    other_ids = swap_core(ids)
    mates = jnp.where(place // (blk_size // 2) == core, ids, other_ids)
    spoken, length = jnp.where(odd, mates[:, 1], mates[:, 0])

    head_first = core * mine
    own_weights = jnp.concatenate(
        [lax.dynamic_slice_in_dim(w, head_first, mine, 1) for w in (w_query, w_key, w_value)], 1
    )
    own_weights_t = own_weights.T
    own_bias = lax.dynamic_slice_in_dim(bias_table, core * head_count, head_count, 1)
    bucket_hot = (rel_bucket[:, None] == jnp.arange(bucket_count)[None, :]).astype(f32)
    hot_later = jnp.pad(bucket_hot, ((1, 0), (0, 0)))
    hot_back = jnp.pad(bucket_hot[::-1], ((1, 0), (0, 0)))
    bias_later = jnp.pad(jnp.dot(hot_later, own_bias, precision=highest).T, ((0, 8 - head_count), (0, 0)))
    bias_back = jnp.pad(jnp.dot(hot_back, own_bias, precision=highest).T, ((0, 8 - head_count), (0, 0)))
    position = (jnp.arange(span) + half * core) % span
    key_mask = jnp.where(position < length, 0.0, masked_score).astype(f32)[None]

    embedding = lax.dynamic_slice_in_dim(lang_table, spoken, 1, 0).astype(f32)
    with_lang_all = jnp.concatenate([own_tokens, other_tokens]).astype(f32) + embedding
    scale_all = rms_parts(with_lang_all)
    normed = (with_lang_all * scale_all * gain_first).astype(bf16)
    qkv = dot(own_weights_t, normed, 1, 1).astype(bf16)
    mixture_t, attended_t, log_total = attention_forward(qkv, bias_back, key_mask, head_count)

    with_lang = with_lang_all[:half]
    other_mixture_t = swap_core(mixture_t[:, half:])
    own_mixture_t = mixture_t[:, :half]
    full_mixture_t = jnp.where(
        core == 0,
        jnp.concatenate([own_mixture_t, other_mixture_t]),
        jnp.concatenate([other_mixture_t, own_mixture_t]),
    )
    middle = with_lang + dot(full_mixture_t, w_output, 0, 0)
    scale_second = rms_parts(middle)
    normed_second = (middle * scale_second * gain_second).astype(bf16)
    hidden = dot(normed_second, w_in, 1, 0)
    active, gelu_back = jax.vjp(functools.partial(jax.nn.gelu, approximate=True), hidden)
    active = active.astype(bf16)
    output_rows = (middle + dot(active, w_out, 1, 0)).astype(bf16)
    output = from_rows(output_rows, odd)
    grad_hidden = gelu_back(dot(own_cotangent, w_out, 1, 1))[0].astype(bf16)
    grad_normed_second = dot(grad_hidden, w_in, 1, 1)
    grad_middle_part, grad_gain_second = norm_back(grad_normed_second, middle, gain_second, scale_second)
    grad_middle = own_cotangent.astype(f32) + grad_middle_part
    grad_projected = grad_middle.astype(bf16)
    grad_w_out = dot(active, own_cotangent, 0, 0)
    grad_w_in = dot(normed_second, grad_hidden, 0, 0)
    grad_w_output = dot(full_mixture_t, grad_projected, 1, 0)

    other_projected = swap_core(grad_projected)
    projected_all = jnp.concatenate([grad_projected, other_projected])
    own_output_rows = lax.dynamic_slice_in_dim(w_output, head_first, mine, 0)
    grad_mixture_t = dot(own_output_rows, projected_all, 1, 1).astype(bf16)
    grad_qkv, diagonals = attention_backward(
        qkv, grad_mixture_t, attended_t, log_total, bias_later, key_mask, head_count
    )
    pieces = diagonals.reshape(head_count, 8, 2 * span)
    by_distance = sum(jnp.roll(pieces[:, i], -i, axis=-1) for i in range(8))
    grad_bias_own = jnp.dot(by_distance, hot_later, precision=highest).T
    grad_bias = lax.dynamic_update_slice_in_dim(
        jnp.zeros(bias_table.shape, f32), grad_bias_own, core * head_count, 1
    )

    grad_normed_all = dot(grad_qkv, own_weights_t, 0, 0)
    from_other = swap_core(grad_normed_all[half:].astype(bf16))
    grad_normed = grad_normed_all[:half] + from_other.astype(f32)
    grad_start, grad_gain_first = norm_back(grad_normed, with_lang, gain_first, scale_all[:half])
    grad_with_lang = grad_middle + grad_start
    grad_tokens = from_rows(grad_with_lang.astype(bf16), odd)
    lang_hot = (jnp.arange(lang_table.shape[0]) == spoken).astype(f32)
    grad_lang = lang_hot[:, None] * jnp.sum(grad_with_lang, axis=0)[None, :]
    grad_w_qkv = dot(normed, grad_qkv, 0, 1)

    names = ("dp", "blk")

    def scattered(value, dim=0):
        return lax.psum_scatter(value, names, scatter_dimension=dim, tiled=True)

    grads_qkv = []
    for part in jnp.split(grad_w_qkv, 3, axis=1):
        whole = jnp.zeros((width, width), f32)
        grads_qkv.append(scattered(lax.dynamic_update_slice_in_dim(whole, part, head_first, 1)))
    return (
        output,
        grad_tokens,
        scattered(grad_lang, 1),
        scattered(grad_gain_first),
        *grads_qkv,
        scattered(grad_w_output),
        lax.psum(grad_bias, names),
        scattered(grad_gain_second),
        scattered(grad_w_in),
        scattered(grad_w_out),
    )


def solution(mesh):
    rows = P("dp", "blk", None)
    shard = P(("dp", "blk"))
    matrix = P(("dp", "blk"), None)
    fits = (mesh.shape["dp"], mesh.shape["blk"]) == (8, 4)
    return jax.shard_map(
        local if fits else local_plain,
        mesh=mesh,
        in_specs=(rows, P("dp"), P("dp")) + (P(),) * 11 + (rows,),
        out_specs=(
            rows,
            rows,
            P(None, ("dp", "blk")),
            shard,
            matrix,
            matrix,
            matrix,
            matrix,
            P(),
            shard,
            matrix,
            matrix,
        ),
        check_vma=False,
    )
```

```python
import functools
import itertools

import jax
import jax.numpy as jnp
from jax import lax
from jax.experimental import pallas as pl
from jax.experimental.pallas import tpu as pltpu
from jax.sharding import PartitionSpec as P

MESH = pl.DeviceIdType.MESH
bf16 = jnp.bfloat16
f32 = jnp.float32
eps_norm = 1e-06
masked_score = -1e30
highest = lax.Precision.HIGHEST
LANE = 128
VMEM_BYTES = 63 * 2**20


def dot(left, right, left_dim, right_dim):
    return lax.dot_general(
        left, right, (((left_dim,), (right_dim,)), ((), ())), preferred_element_type=f32
    )


def move_pairs(dp_size, blk_size, same):
    half = blk_size // 2
    pairs = []
    for d in range(dp_size):
        for z in range(blk_size):
            low = z % 2 if same else 1 - z % 2
            target = (2 * (d // 2) + z // half, 2 * (d % 2) + low)
            pairs.append((d * blk_size + z, target[0] * blk_size + target[1]))
    return pairs


def swap_core(value):
    size = lax.axis_size("dp")
    return lax.ppermute(value, "dp", [(d, d ^ 1) for d in range(size)])


def to_rows(value, odd):
    dp_size, blk_size = lax.axis_size("dp"), lax.axis_size("blk")
    first = jnp.where(odd, value[1], value[0])
    second = jnp.where(odd, value[0], value[1])
    first = lax.ppermute(first, ("dp", "blk"), move_pairs(dp_size, blk_size, True))
    second = lax.ppermute(second, ("dp", "blk"), move_pairs(dp_size, blk_size, False))
    return jnp.where(odd, jnp.concatenate([second, first]), jnp.concatenate([first, second]))


def from_rows(value, odd):
    dp_size, blk_size = lax.axis_size("dp"), lax.axis_size("blk")
    low, high = jnp.split(value, 2)
    first = jnp.where(odd, high, low)
    second = jnp.where(odd, low, high)
    back_same = [(b, a) for a, b in move_pairs(dp_size, blk_size, True)]
    back_other = [(b, a) for a, b in move_pairs(dp_size, blk_size, False)]
    first = lax.ppermute(first, ("dp", "blk"), back_same)
    second = lax.ppermute(second, ("dp", "blk"), back_other)
    return jnp.where(odd, jnp.stack([second, first]), jnp.stack([first, second]))


def window(core, row_start, col_start, half, span):
    base = col_start - row_start + span
    turns = (row_start >= half) - (col_start >= half)
    return pl.multiple_of(base + core * (turns * 2 * half), LANE) if turns else base


def split_three(value):
    high = value.astype(bf16).astype(f32)
    middle = (value - high).astype(bf16).astype(f32)
    low = (value - high - middle).astype(bf16).astype(f32)
    return high, middle, low


def forward_kernel(head_count, head_size, qkv, bias_row, key_mask, mixture, attended, log_total, table, scores, weights, key_ext, query_ext, value_ext):
    core = lax.axis_index("dp") % 2
    width = head_count * head_size
    span = qkv.shape[1]
    half = span // 2
    step = 2 * LANE
    row_id = lax.broadcasted_iota(jnp.int32, (16, span), 0)
    key_ext[pl.ds(head_size, 16), :] = jnp.where(row_id == 0, key_mask[...], 0.0).astype(bf16)
    query_ext[pl.ds(head_size, 16), :] = jnp.where(row_id == 0, 1.0, 0.0).astype(bf16)
    value_ext[pl.ds(head_size, 16), :] = jnp.where(row_id == 0, 1.0, 0.0).astype(bf16)

    def one_head(head, _):
        first = pl.multiple_of(head * head_size, head_size)
        row = bias_row[pl.ds(head, 1), :]
        table[...] = pltpu.roll(jnp.broadcast_to(row, table.shape), 0, 1, stride=1, stride_axis=0)
        query_ext[pl.ds(0, head_size), :] = qkv[pl.ds(first, head_size), :]
        key_ext[pl.ds(0, head_size), :] = qkv[pl.ds(width + first, head_size), :]
        value_ext[pl.ds(0, head_size), :] = qkv[pl.ds(2 * width + first, head_size), :]
        for row_start in range(0, span, step):
            query = query_ext[:, row_start : row_start + step]
            best = None
            for col_start in range(0, span, LANE):
                part = dot(key_ext[:, col_start : col_start + LANE], query, 0, 0)
                place = window(core, col_start, row_start, half, span)
                part = part + table[:, pl.ds(place, step)]
                scores[col_start : col_start + LANE, :] = part
                folded = jnp.max(part.reshape(LANE // 8, 8, step), axis=0)
                best = folded if best is None else jnp.maximum(best, folded)
            top = jnp.max(best, axis=0, keepdims=True)
            for col_start in range(0, span, LANE):
                weights[col_start : col_start + LANE, :] = jnp.exp(
                    scores[col_start : col_start + LANE, :] - top
                ).astype(bf16)
            summed = dot(value_ext[...], weights[...], 1, 0)
            total = summed[head_size : head_size + 1]
            part = summed[:head_size] / total
            attended[pl.ds(first, head_size), row_start : row_start + step] = part
            mixture[pl.ds(first, head_size), row_start : row_start + step] = part.astype(bf16)
            log_total[pl.ds(head, 1), row_start : row_start + step] = top + jnp.log(total)
        return 0

    lax.fori_loop(0, head_count, one_head, 0)


def attention_forward(qkv, bias_row, key_mask, head_count):
    wide, span = qkv.shape
    width = wide // 3
    head_size = width // head_count
    ext = pltpu.VMEM((head_size + 16, span), bf16)
    return pl.pallas_call(
        functools.partial(forward_kernel, head_count, head_size),
        out_shape=(
            jax.ShapeDtypeStruct((width, span), bf16),
            jax.ShapeDtypeStruct((width, span), f32),
            jax.ShapeDtypeStruct((8, span), f32),
        ),
        scratch_shapes=[
            pltpu.VMEM((LANE, 2 * span), f32),
            pltpu.VMEM((span, 2 * LANE), f32),
            pltpu.VMEM((span, 2 * LANE), bf16),
            ext,
            ext,
            ext,
        ],
        compiler_params=pltpu.CompilerParams(vmem_limit_bytes=VMEM_BYTES),
        name="attention_forward",
    )(qkv, bias_row, key_mask)


def backward_kernel(head_count, head_size, qkv, grad_mixture, attended, log_total, bias_row, key_mask, grads, diagonals, table, sums, weights, slopes, key_ext, query_ext, value_ext, grad_ext):
    core = lax.axis_index("dp") % 2
    width = head_count * head_size
    span = qkv.shape[1]
    half = span // 2
    row_id = lax.broadcasted_iota(jnp.int32, (16, span), 0)
    key_tail = jnp.where(row_id == 0, key_mask[...], jnp.where(row_id < 4, 1.0, 0.0))
    key_ext[pl.ds(head_size, 16), :] = key_tail.astype(bf16)
    value_ext[pl.ds(head_size, 16), :] = jnp.where(row_id < 3, 1.0, 0.0).astype(bf16)

    def one_head(head, _):
        first = pl.multiple_of(head * head_size, head_size)
        row = bias_row[pl.ds(head, 1), :]
        table[...] = pltpu.roll(jnp.broadcast_to(row, table.shape), 0, 1, stride=1, stride_axis=0)
        sums[...] = jnp.zeros_like(sums)
        query = qkv[pl.ds(first, head_size), :]
        key = qkv[pl.ds(width + first, head_size), :]
        grad = grad_mixture[pl.ds(first, head_size), :]
        key_ext[pl.ds(0, head_size), :] = key
        value_ext[pl.ds(0, head_size), :] = qkv[pl.ds(2 * width + first, head_size), :]
        query_ext[pl.ds(0, head_size), :] = query
        grad_ext[pl.ds(0, head_size), :] = grad
        a, b, c = split_three(-log_total[pl.ds(head, 1), :])
        query_ext[pl.ds(head_size, 16), :] = jnp.where(
            row_id == 0, 1.0, jnp.where(row_id == 1, a, jnp.where(row_id == 2, b, jnp.where(row_id == 3, c, 0.0)))
        ).astype(bf16)
        row_dot = jnp.sum(
            grad.astype(f32) * attended[pl.ds(first, head_size), :], axis=0, keepdims=True
        )
        a, b, c = split_three(-row_dot)
        grad_ext[pl.ds(head_size, 16), :] = jnp.where(
            row_id == 0, a, jnp.where(row_id == 1, b, jnp.where(row_id == 2, c, 0.0))
        ).astype(bf16)
        for row_start in range(0, span, LANE):
            rows = slice(row_start, row_start + LANE)
            for col_start in range(0, span, half):
                cols = slice(col_start, col_start + half)
                place = pl.ds(window(core, row_start, col_start, half, span), half)
                part = dot(query_ext[:, rows], key_ext[:, cols], 0, 0)
                part = jnp.exp(part + table[:, place])
                slope = part * dot(grad_ext[:, rows], value_ext[:, cols], 0, 0)
                weights[rows, cols] = part.astype(bf16)
                slopes[rows, cols] = slope.astype(bf16)
                sums[:, place] += slope
        grads[pl.ds(first, head_size), :] = dot(key, slopes[...], 1, 1).astype(bf16)
        grads[pl.ds(width + first, head_size), :] = dot(query, slopes[...], 1, 0).astype(bf16)
        grads[pl.ds(2 * width + first, head_size), :] = dot(grad, weights[...], 1, 0).astype(bf16)
        folded = sums[...]
        count = LANE
        while count > 8:
            count //= 2
            folded = folded[:count] + pltpu.roll(folded[count:], 2 * span - count, 1)
        diagonals[pl.ds(pl.multiple_of(head * 8, 8), 8), :] = folded
        return 0

    lax.fori_loop(0, head_count, one_head, 0)


def attention_backward(qkv, grad_mixture, attended, log_total, bias_row, key_mask, head_count):
    wide, span = qkv.shape
    width = wide // 3
    head_size = width // head_count
    ext = pltpu.VMEM((head_size + 16, span), bf16)
    square = pltpu.VMEM((span, span), bf16)
    slab = pltpu.VMEM((LANE, 2 * span), f32)
    return pl.pallas_call(
        functools.partial(backward_kernel, head_count, head_size),
        out_shape=(
            jax.ShapeDtypeStruct((wide, span), bf16),
            jax.ShapeDtypeStruct((8 * head_count, 2 * span), f32),
        ),
        scratch_shapes=[slab, slab, square, square, ext, ext, ext, ext],
        compiler_params=pltpu.CompilerParams(vmem_limit_bytes=VMEM_BYTES),
        name="attention_backward",
    )(qkv, grad_mixture, attended, log_total, bias_row, key_mask)


def rms_parts(values):
    return lax.rsqrt(jnp.mean(values * values, axis=-1, keepdims=True) + eps_norm)


def norm_back(grad, values, gain, scale):
    weighted = grad * gain
    inner = jnp.mean(weighted * values, axis=-1, keepdims=True)
    return scale * weighted - values * (scale * scale * scale) * inner, jnp.sum(grad * values * scale, axis=0)


def gelu_both(value):
    root = 0.7978845608028654
    square = value * value
    bent = jnp.tanh(value * (root + root * 0.044715 * square))
    up = 0.5 * bent + 0.5
    active = value * up
    slope = up + active * ((1.0 - bent) * (root + 3 * 0.044715 * root * square))
    return active, slope


AXES = ("y", "x", "h", "l")


class Sums:
    def __init__(self, kernel, blocks, rows, columns, order, buffers):
        self.kernel, self.blocks, self.order, self.buffers = kernel, blocks, order, buffers
        self.rows, self.columns = pl.ds(*rows), pl.ds(*columns)
        self.copies = []
        for step, axis in enumerate(order):
            source = self.place(step, axis, 1 - kernel.at[axis])
            self.copies.append(kernel.copy(source, buffers[step], kernel.partner[axis]))

    def place(self, step, axis, which):
        picks = []
        for other in AXES:
            if other == axis:
                picks.append(pl.ds(which, 1))
            else:
                picks.append(pl.ds(self.kernel.at[other], 1) if other in self.order[:step] else pl.ds(0, 2))
        return self.blocks.at[(*picks, self.rows, self.columns)]

    def begin(self, step):
        self.copies[step].start()

    def end(self, step, result=None):
        self.copies[step].wait()
        axis = self.order[step]
        kept = self.place(step, axis, self.kernel.at[axis])
        buffer = self.buffers[step]
        for index in itertools.product(*(range(count) for count in buffer.shape[:4])):
            total = kept[index].astype(f32) + buffer[index].astype(f32)
            if result is None:
                kept[index] = total.astype(bf16)
            else:
                result[self.rows, self.columns] = total

    def shapes(rows, columns, order):
        return [
            (*(1 if axis in order[: step + 1] else 2 for axis in AXES), rows, columns) for step in range(len(order))
        ]


FLAT, TALL, DEEP = ("x", "y", "l", "h"), ("y", "x", "l", "h"), ("l", "h", "x", "y")
PARTS = {
    "out": [((0, 64), (0, 384), FLAT), ((0, 64), (384, 384), TALL), ((64, 32), (0, 768), DEEP)],
    "in": [((0, 64), (0, 384), FLAT), ((0, 64), (384, 384), TALL), ((64, 32), (0, 768), DEEP)],
    "mix": [((0, 32), (0, 384), FLAT), ((32, 16), (0, 384), TALL)],
    "low": [((0, 32), (0, 384), TALL), ((32, 16), (0, 384), FLAT)],
    "mid": [((0, 32), (0, 384), FLAT), ((32, 16), (0, 384), TALL)],
    "high": [((0, 32), (0, 384), TALL), ((32, 16), (0, 384), FLAT)],
}
PLAN = {
    "mix": [("out", 0, 0), ("out", 1, 0)],
    "head2": [("mix", 1, 0), ("out", 2, 0)],
    "pair3": [("out", 0, 1), ("in", 2, 0), ("in", 1, 0), ("mix", 0, 0)],
    "head4": [("in", 0, 0), ("low", 0, 0), ("low", 1, 0), ("mix", 1, 1), ("out", 1, 1)],
    "head5": [("mid", 1, 0)],
    "high": [("mix", 0, 1), ("out", 0, 2), ("out", 2, 1)],
    "gtok": [("low", 1, 1), ("mid", 0, 0), ("mix", 1, 2), ("in", 1, 1), ("in", 0, 1), ("low", 0, 1), ("out", 1, 2)],
    "small": [("in", 2, 1), ("mid", 1, 1)],
    "tail": [("mix", 0, 2), ("out", 0, 3), ("high", 1, 0), ("out", 2, 2), ("high", 0, 0), ("mix", 1, 3), ("low", 1, 2), ("mid", 0, 1), ("in", 2, 2), ("mid", 1, 2), ("low", 0, 2), ("out", 1, 3), ("mix", 0, 3), ("high", 1, 1), ("out", 2, 3), ("high", 0, 1), ("low", 1, 3), ("in", 1, 2), ("in", 0, 2), ("mid", 0, 2), ("in", 2, 3), ("mid", 1, 3), ("high", 1, 2), ("low", 0, 3), ("high", 0, 2), ("mid", 0, 3), ("high", 1, 3), ("in", 1, 3), ("in", 0, 3), ("high", 0, 3)],
}
GROUP_SHAPE = {"out": (96, 768), "in": (96, 768), "mix": (48, 384), "low": (48, 384), "mid": (48, 384), "high": (48, 384)}
GROUPS = ("out", "in", "mix", "low", "mid", "high")


class Kernel:
    pass


def block_kernel(head_count, language_ids, length_ids, tokens, cotangent, w_query, w_key, w_value, w_output, w_in, w_out, lang_table, first_gain, second_gain, buckets, bias_table, *refs):
    k = Kernel()
    names = (
        "output", "grad_tokens", "o_query", "o_key", "o_value", "o_output", "o_in", "o_out",
        "o_lang", "o_first", "o_second", "o_bias", "tok", "meta_out", "meta_in", "wt",
        "wo", "win", "wout", "normed_t", "qkv", "att", "mix", "gmix",
        "middle", "acc", "ns", "slope", "acts", "act_in", "gh_in", "cot",
        "proj", "out_rows", "table", "sums", "prob", "ds", "key_ext", "value_ext",
        "query_ext", "grad_ext", "bias_rows", "back_rows", "distance", "small", "fin_send", "fin_recv",
        "fin_last", "result", "result_last", "g_out", "g_in", "g_mix", "g_low", "g_mid",
        "g_high",
    )
    for name, ref in zip(names, refs):
        setattr(k, name, ref)
    rest = list(refs[len(names):])
    send_sem, recv_sem, load_sem = rest[-3:]
    rest = rest[:-3]
    dp, z = lax.axis_index("dp"), lax.axis_index("blk")
    core = dp % 2
    mate_core = 1 - core
    base = dp - core
    k.dp = dp
    k.at = {"x": (dp // 2) % 2, "y": (dp // 4) % 2, "h": z // 2, "l": z % 2}
    k.partner = {"x": (dp ^ 2, z), "y": (dp ^ 4, z), "h": (dp, z ^ 2), "l": (dp, z ^ 1)}
    mate = (base + mate_core, z)
    used = [0]
    width = lang_table.shape[1]
    span = k.qkv.shape[1]
    half, quarter = span // 2, span // 4
    mine = width // 2
    head_size = mine // head_count
    tile = mine
    tiles = k.win.shape[1] // width

    def take(count=1):
        used[0] += count
        return used[0] - count

    def copy(source, target, device, slot=None):
        slot = take() if slot is None else slot
        return pltpu.make_async_remote_copy(
            src_ref=source,
            dst_ref=target,
            send_sem=send_sem.at[slot],
            recv_sem=recv_sem.at[slot],
            device_id=device,
            device_id_type=MESH,
        )

    k.copy = copy

    barrier = pltpu.get_barrier_semaphore()
    friends = [(base + (core + turn) % 2, z ^ far) for turn in range(2) for far in range(4) if turn or far]
    friends += [k.partner["x"], k.partner["y"], (dp ^ 6, z)]
    for friend in friends:
        pl.semaphore_signal(barrier, inc=1, device_id=friend, device_id_type=MESH)

    loads = []

    def load(source, target):
        item = pltpu.make_async_copy(source, target, load_sem.at[len(loads)])
        item.start()
        loads.append(item)

    own_lanes = pl.ds(pl.multiple_of(core * mine, LANE), mine)
    mate_lanes = pl.ds(pl.multiple_of(mate_core * mine, LANE), mine)
    def stage_rows(index):
        return pl.ds((index % 2) * width, width)

    def stage_lanes(index):
        return pl.ds((index // 2) * mine, mine)

    for index, source in enumerate((w_query, w_key, w_value)):
        load(source.at[:, own_lanes], k.acts.at[stage_rows(index), stage_lanes(index)])
    load(w_output.at[own_lanes], k.wo.at[pl.ds(0, mine)])
    load(w_output.at[mate_lanes], k.wo.at[pl.ds(mine, mine)])
    load(w_in, k.win)
    load(w_out, k.wout)

    row_id = lax.broadcasted_iota(jnp.int32, k.meta_out.shape[1:], 0)
    for index in range(2):
        k.meta_out[index] = jnp.where(row_id == 0, language_ids[index], length_ids[index])
    pl.semaphore_wait(barrier, len(friends))

    side = z % 2

    class Route:
        def __init__(self, pick, target):
            self.slots = take(2)
            self.items = []
            for index in range(2):
                device = (base + z // 2, 2 * core + index)
                here = (z // 2 == core) & (2 * core + index == z)
                source = pick(index)
                far = pltpu.make_async_remote_copy(
                    src_ref=source,
                    dst_ref=target(side),
                    send_sem=send_sem.at[self.slots + index],
                    recv_sem=recv_sem.at[self.slots + side],
                    device_id=device,
                    device_id_type=MESH,
                )
                near = pltpu.make_async_copy(source, target(side), recv_sem.at[self.slots + side])
                self.items.append((here, far, near))
            self.arrivals = [copy(target(j), target(j), mate, self.slots + j) for j in range(2)]

        def start(self):
            for here, far, near in self.items:
                pl.when(here)(near.start)
                pl.when(jnp.logical_not(here))(far.start)

        def arrive(self, index):
            self.arrivals[index].wait_recv()

        def close(self):
            for here, far, _ in self.items:
                pl.when(jnp.logical_not(here))(far.wait_send)

    def part_rows(index):
        return pl.ds(pl.multiple_of(index * quarter, quarter), quarter)

    way_meta = Route(lambda i: k.meta_out.at[i], lambda j: k.meta_in.at[j])
    way_tokens = Route(lambda i: tokens.at[i], lambda j: k.tok.at[part_rows(j)])
    way_meta.start()
    way_tokens.start()

    all_heads, bucket_count = bias_table.shape
    places = 2 * span

    def bucket_hot():
        return (lax.broadcasted_iota(jnp.int32, (bucket_count, places), 0) == buckets[...]).astype(f32)

    pick = (
        lax.broadcasted_iota(jnp.int32, (all_heads, 8), 0)
        == lax.broadcasted_iota(jnp.int32, (all_heads, 8), 1) + core * head_count
    ) & (lax.broadcasted_iota(jnp.int32, (all_heads, 8), 1) < head_count)

    def exact(left, right, left_dim, right_dim):
        return lax.dot_general(
            left, right, (((left_dim,), (right_dim,)), ((), ())), precision=highest, preferred_element_type=f32
        )

    own_bias = exact(bias_table[...], pick.astype(f32), 0, 0)
    bias_rows = exact(own_bias, bucket_hot(), 0, 0)
    k.bias_rows[...] = bias_rows
    flip = (
        lax.broadcasted_iota(jnp.int32, (LANE, LANE), 0) + lax.broadcasted_iota(jnp.int32, (LANE, LANE), 1) == LANE - 1
    ).astype(f32)
    for first in range(0, places, LANE):
        k.back_rows[:, first : first + LANE] = exact(bias_rows[:, places - LANE - first : places - first], flip, 1, 0)
    k.back_rows[...] = pltpu.roll(k.back_rows[...], 1, 1)
    for index in range(3):
        loads[index].wait()
        k.wt[index * mine : (index + 1) * mine, :] = k.acts[stage_rows(index), stage_lanes(index)].T

    for index in range(2):
        way_meta.arrive(index)
    language = k.meta_in[0, 0:1, 0:1]
    length = k.meta_in[0, 1:2, 0:1]
    embedding = jnp.zeros((1, width), f32)
    for index in range(8):
        embedding = embedding + jnp.where(language == index, lang_table[index : index + 1, :].astype(f32), 0.0)
    gain_first, gain_second = first_gain[...].reshape(1, width), second_gain[...].reshape(1, width)
    position = (lax.broadcasted_iota(jnp.int32, (1, span), 1) + half * core) % span
    key_mask = jnp.where(position < length, 0.0, masked_score)

    relays = [copy(k.tok.at[part_rows(j)], k.tok.at[part_rows(2 + j)], mate) for j in range(2)]
    way_cotangent = Route(lambda i: cotangent.at[i], lambda j: k.cot.at[part_rows(j)])

    def project(index):
        rows = slice(index * quarter, (index + 1) * quarter)
        values = k.tok[rows, :].astype(f32) + embedding
        normed = (values * rms_parts(values) * gain_first).astype(bf16)
        k.normed_t[:, rows] = normed.T
        k.qkv[:, rows] = dot(k.wt[...], k.normed_t[:, rows], 1, 0).astype(bf16)

    for index in range(2):
        way_tokens.arrive(index)
        relays[index].start()
    for index in range(2):
        project(index)
    for index in range(2):
        relays[index].wait_recv()
    for index in range(2):
        relays[index].wait_send()
    way_cotangent.start()
    for index in range(2):
        project(2 + index)

    step = 2 * LANE
    block = k.prob.shape[0]
    ext_row = lax.broadcasted_iota(jnp.int32, (16, span), 0)
    tail = pl.ds(head_size, 16)
    k.key_ext[tail, :] = jnp.where(ext_row == 0, key_mask, jnp.where(ext_row < 4, 1.0, 0.0)).astype(bf16)
    k.query_ext[tail, :] = jnp.where(ext_row == 0, 1.0, 0.0).astype(bf16)
    k.value_ext[tail, :] = jnp.where(ext_row < 3, 1.0, 0.0).astype(bf16)
    mix_slots = take(2 * head_count)

    def mix_copies(head):
        rows = pl.ds(pl.multiple_of(head * head_size, head_size), head_size)
        far = pl.ds(pl.multiple_of(mine + head * head_size, head_size), head_size)
        return [
            copy(
                k.mix.at[rows, pl.ds(side_at * half, half)],
                k.mix.at[far, pl.ds((1 - side_at) * half, half)],
                mate,
                mix_slots + 2 * head + side_at,
            )
            for side_at in range(2)
        ]

    def place_in(count, start):
        lane = (start // count) * step
        return slice(start % count, start % count + LANE), slice(lane, lane + step)

    def forward_head(head, _):
        first = pl.multiple_of(head * head_size, head_size)
        row = k.back_rows[pl.ds(head, 1), :]
        k.table[...] = pltpu.roll(jnp.broadcast_to(row, k.table.shape), 0, 1, stride=1, stride_axis=0)
        k.query_ext[pl.ds(0, head_size), :] = k.qkv[pl.ds(first, head_size), :]
        k.key_ext[pl.ds(0, head_size), :] = k.qkv[pl.ds(mine + first, head_size), :]
        k.value_ext[pl.ds(0, head_size), :] = k.qkv[pl.ds(2 * mine + first, head_size), :]
        for row_start in range(0, span, step):
            query = k.query_ext[:, row_start : row_start + step]
            best = None
            for start in range(0, span, LANE):
                part = dot(k.key_ext[:, start : start + LANE], query, 0, 0)
                part = part + k.table[:, pl.ds(window(core, start, row_start, half, span), step)]
                k.acc[place_in(half, start)] = part
                folded = jnp.max(part.reshape(LANE // 8, 8, step), axis=0)
                best = folded if best is None else jnp.maximum(best, folded)
            top = jnp.max(best, axis=0, keepdims=True)
            for start in range(0, span, LANE):
                k.prob[place_in(block, start)] = jnp.exp(k.acc[place_in(half, start)] - top).astype(bf16)
            summed = None
            for start in range(0, span, block):
                lanes = place_in(block, start)[1]
                more = dot(k.value_ext[:, start : start + block], k.prob[:, lanes], 1, 0)
                summed = more if summed is None else summed + more
            total = summed[head_size : head_size + 1]
            part = summed[:head_size] / total
            k.att[pl.ds(first, head_size), row_start : row_start + step] = part
            k.mix[pl.ds(first, head_size), row_start : row_start + step] = part.astype(bf16)
            k.distance[pl.ds(head, 1), row_start : row_start + step] = top + jnp.log(total)
        for item in mix_copies(head):
            item.start()
        return 0

    lax.fori_loop(0, head_count, forward_head, 0)

    loads[3].wait()
    loads[4].wait()
    for head in range(head_count):
        for item in mix_copies(head):
            item.wait_recv()
    for index in range(2):
        rows = slice(index * quarter, (index + 1) * quarter)
        values = k.tok[rows, :].astype(f32) + embedding + dot(k.mix[:, rows], k.wo[...], 0, 0)
        k.middle[rows, :] = values
        k.acc[rows, :] = values
        k.ns[rows, :] = (values * rms_parts(values) * gain_second).astype(bf16)
    ns_copy = copy(k.ns.at[pl.ds(0, half)], k.ns.at[pl.ds(half, half)], mate)
    ns_copy.start()
    loads[5].wait()
    loads[6].wait()
    act_slots = take(tiles)
    gh_slots = take(tiles)

    def tile_rows(index):
        return pl.ds(pl.multiple_of(index * half, half), half)

    def wide_lanes(index):
        return pl.ds(pl.multiple_of(index * width, width), width)

    def tile_lanes(index):
        return pl.ds(pl.multiple_of(index * tile, tile), tile)

    def act_copy(index):
        return copy(k.acts.at[tile_rows(index), mate_lanes], k.act_in.at[:, tile_lanes(index)], mate, act_slots + index)

    def gh_copy(index):
        return copy(k.acts.at[tile_rows(index), mate_lanes], k.gh_in.at[:, tile_lanes(index)], mate, gh_slots + index)

    def forward_tile(index, _):
        lanes = wide_lanes(index)
        for first in range(0, half, quarter):
            rows = pl.ds(pl.multiple_of(index * half + first, quarter), quarter)
            active, slope = gelu_both(dot(k.ns[first : first + quarter], k.win[:, lanes], 1, 0))
            active = active.astype(bf16)
            k.acts[rows, :] = active
            k.slope[rows, :] = slope.astype(bf16)
            k.acc[first : first + quarter] += dot(active, k.wout[lanes, :], 1, 0)
        act_copy(index).start()
        return 0

    lax.fori_loop(0, tiles, forward_tile, 0)
    way_output = Route(lambda i: k.out_rows.at[part_rows(i)], lambda j: k.output.at[j])
    k.out_rows[...] = k.acc[...].astype(bf16)
    way_output.start()

    cot_relays = [copy(k.cot.at[part_rows(j)], k.cot.at[part_rows(2 + j)], mate) for j in range(2)]
    for index in range(2):
        way_cotangent.arrive(index)
        cot_relays[index].start()
    for index in range(2):
        cot_relays[index].wait_recv()
    parts = {}
    for group in GROUPS:
        parts[group] = []
        for rows, columns, order in PARTS[group]:
            parts[group].append(Sums(k, getattr(k, "g_" + group), rows, columns, order, [rest.pop(0) for _ in order]))

    def begin(group):
        for part in parts[group]:
            part.begin(0)

    results = {"out": k.o_out, "in": k.result}
    for index, group in enumerate(GROUPS[2:]):
        results[group] = k.result_last.at[:, pl.ds(index * mine, mine)]

    def advance(group, part, at):
        parts[group][part].end(at, results[group] if at == 3 else None)
        if at < 3:
            parts[group][part].begin(at + 1)

    def tick(name):
        for item in PLAN.get(name, ()):
            advance(*item)

    def out_tile(index, _):
        act_copy(index).wait_recv()
        grad = dot(k.acts[tile_rows(index), own_lanes], k.cot[:half], 0, 0)
        grad = grad + dot(k.act_in[:, tile_lanes(index)], k.cot[half:], 0, 0)
        k.g_out[index // 2, index % 2] = grad.reshape(2, 2, tile // 4, width).astype(bf16)
        return 0

    lax.fori_loop(0, tiles, out_tile, 0)
    begin("out")

    def put_blocks(target, grad, rows, lanes, halves=(0, 1)):
        each = grad.shape[0] // 32
        for index in range(4):
            for at in range(4):
                first = (8 * index + at) * each
                both = jnp.concatenate([grad[first : first + each], grad[first + 4 * each : first + 5 * each]])
                up = index // 2
                up = halves[up] if up < len(halves) else up
                target[up, index % 2, at // 2, at % 2, rows, lanes] = both.astype(bf16)

    k.acc[...] = jnp.zeros_like(k.acc)
    for index in range(tiles):
        act_copy(index).wait_send()

    def back_tile(index, _):
        lanes = wide_lanes(index)
        grad = dot(k.cot[:half], k.wout[lanes, :], 1, 1)
        grad = (grad * k.slope[tile_rows(index), :].astype(f32)).astype(bf16)
        k.acts[tile_rows(index), :] = grad
        gh_copy(index).start()
        k.act_in[:, tile_lanes(index)] = k.acts[tile_rows(index), own_lanes]
        k.acc[...] += dot(grad, k.win[:, lanes], 1, 1)
        for at in range(tiles):
            if f"back{at}" in PLAN:
                pl.when(index == at)(functools.partial(tick, f"back{at}"))
        return 0

    lax.fori_loop(0, tiles, back_tile, 0)
    ns_copy.wait_recv()
    for index in range(tiles):
        gh_copy(index).wait_recv()
    for index in range(2):
        lanes = slice(index * width, (index + 1) * width)
        grad = dot(k.ns[:half], k.act_in[:, lanes], 0, 0) + dot(k.ns[half:], k.gh_in[:, lanes], 0, 0)
        put_blocks(k.g_in, grad, pl.ds(48 * index, 48), pl.ds(0, width))
        tick(f"in{index}")
    begin("in")

    gain_grad = jnp.zeros((1, width), f32)
    for index in range(2):
        rows = slice(index * quarter, (index + 1) * quarter)
        values, grad = k.middle[rows, :], k.acc[rows, :]
        back, part = norm_back(grad, values, gain_second, rms_parts(values))
        gain_grad = gain_grad + part.reshape(1, width)
        back = back + k.cot[rows, :].astype(f32)
        k.middle[rows, :] = back
        k.proj[rows, :] = back.astype(bf16)
    proj_copy = copy(k.proj, k.tok.at[pl.ds(half, half)], mate)
    proj_copy.start()
    tick("norm")
    proj_copy.wait_recv()
    k.gmix[:, :half] = dot(k.wo[:mine], k.proj[...], 1, 1).astype(bf16)
    k.gmix[:, half:] = dot(k.wo[:mine], k.tok[half:], 1, 1).astype(bf16)
    grad = dot(k.mix[:, :half], k.proj[:, own_lanes], 1, 0) + dot(k.mix[:, half:], k.tok[half:, own_lanes], 1, 0)
    put_blocks(k.g_mix, grad, pl.ds(0, 48), pl.ds(0, mine), (core, mate_core))
    begin("mix")
    tick("mix")

    def backward_head(head, _):
        first = pl.multiple_of(head * head_size, head_size)
        row = k.bias_rows[pl.ds(head, 1), :]
        k.table[...] = pltpu.roll(jnp.broadcast_to(row, k.table.shape), 0, 1, stride=1, stride_axis=0)
        k.sums[...] = jnp.zeros_like(k.sums)
        query_rows, key_rows = pl.ds(first, head_size), pl.ds(mine + first, head_size)
        value_rows = pl.ds(2 * mine + first, head_size)
        query, key = k.qkv[query_rows, :], k.qkv[key_rows, :]
        grad = k.gmix[pl.ds(first, head_size), :]
        k.key_ext[pl.ds(0, head_size), :] = key
        k.value_ext[pl.ds(0, head_size), :] = k.qkv[value_rows, :]
        k.query_ext[pl.ds(0, head_size), :] = query
        k.grad_ext[pl.ds(0, head_size), :] = grad

        def three(value, start):
            found = jnp.where(ext_row == 0, 1.0, 0.0) if start else 0.0
            for at, piece in enumerate(split_three(value)):
                found = jnp.where(ext_row == start + at, piece, found)
            return found.astype(bf16)

        k.query_ext[tail, :] = three(-k.distance[pl.ds(head, 1), :span], 1)
        row_dot = jnp.sum(grad.astype(f32) * k.att[pl.ds(first, head_size), :], axis=0, keepdims=True)
        k.grad_ext[tail, :] = three(-row_dot, 0)
        grad_key = grad_value = None
        for outer in range(0, span, block):
            for row_start in range(outer, outer + block, LANE):
                rows = slice(row_start, row_start + LANE)
                inner = slice(row_start - outer, row_start - outer + LANE)
                for col_start in range(0, span, half):
                    cols = slice(col_start, col_start + half)
                    place = pl.ds(window(core, row_start, col_start, half, span), half)
                    part = dot(k.query_ext[:, rows], k.key_ext[:, cols], 0, 0)
                    part = jnp.exp(part + k.table[:, place])
                    slope = part * dot(k.grad_ext[:, rows], k.value_ext[:, cols], 0, 0)
                    k.prob[inner, cols] = part.astype(bf16)
                    k.ds[inner, cols] = slope.astype(bf16)
                    k.sums[:, place] += slope
            wide = slice(outer, outer + block)
            k.qkv[query_rows, wide] = dot(key, k.ds[...], 1, 1).astype(bf16)
            more_key = dot(query[:, wide], k.ds[...], 1, 0)
            more_value = dot(grad[:, wide], k.prob[...], 1, 0)
            grad_key = more_key if grad_key is None else grad_key + more_key
            grad_value = more_value if grad_value is None else grad_value + more_value
        k.qkv[key_rows, :] = grad_key.astype(bf16)
        k.qkv[value_rows, :] = grad_value.astype(bf16)
        folded = k.sums[...]
        count = LANE
        while count > 8:
            count //= 2
            folded = folded[:count] + pltpu.roll(folded[count:], 2 * span - count, 1)
        at = lax.broadcasted_iota(jnp.int32, folded.shape, 0)
        for bit in (4, 2, 1):
            folded = jnp.where(at % (2 * bit) >= bit, pltpu.roll(folded, 2 * span - bit, 1), folded)
        k.back_rows[pl.ds(head, 1), :] = jnp.sum(folded, axis=0, keepdims=True)
        for at in range(head_count):
            pl.when(head == at)(functools.partial(after_head, at))
        return 0

    pair = 2 * head_size

    def put_pair(target, index):
        rows = [k.qkv[which * mine + index * pair : which * mine + (index + 1) * pair, :] for which in range(3)]
        grad = dot(k.normed_t[...], jnp.concatenate(rows), 1, 1)
        put_blocks(target, grad, pl.ds(0, 48), pl.ds(0, 3 * pair))

    def after_head(head):
        tick(f"head{head}")
        if head in (1, 3):
            group = GROUPS[3 + head // 2]
            put_pair(getattr(k, "g_" + group), head // 2)
            begin(group)
            tick(f"pair{head}")

    lax.fori_loop(0, head_count, backward_head, 0)

    for index in range(2):
        way_output.arrive(index)
    way_output.close()
    ns_copy.wait_send()
    gn_copies = []
    for index in range(2):
        rows = slice(index * quarter, (index + 1) * quarter)
        k.ns[rows, :] = dot(k.qkv[:, half + index * quarter : half + (index + 1) * quarter], k.wt[...], 0, 0).astype(bf16)
        gn_copies.append(copy(k.ns.at[part_rows(index)], k.ns.at[part_rows(2 + index)], mate))
        gn_copies[index].start()
    put_pair(k.g_high, 2)
    begin("high")
    tick("high")
    first_grad = jnp.zeros((1, width), f32)
    lang_grad = jnp.zeros((1, width), f32)
    for index in range(2):
        rows = slice(index * quarter, (index + 1) * quarter)
        gn_copies[index].wait_recv()
        grad = dot(k.qkv[:, rows], k.wt[...], 0, 0) + k.ns[half + index * quarter : half + (index + 1) * quarter, :].astype(f32)
        values = k.tok[rows, :].astype(f32) + embedding
        back, part = norm_back(grad, values, gain_first, rms_parts(values))
        first_grad = first_grad + part.reshape(1, width)
        back = back + k.middle[rows, :]
        lang_grad = lang_grad + jnp.sum(back, axis=0, keepdims=True)
        k.out_rows[rows, :] = back.astype(bf16)
    way_grad = Route(lambda i: k.out_rows.at[part_rows(i)], lambda j: k.grad_tokens.at[j])
    way_grad.start()
    tick("gtok")

    at_row = lax.broadcasted_iota(jnp.int32, (16, width), 0)
    mixed = jnp.where(at_row == language, lang_grad, 0.0)
    mixed = jnp.where(at_row == 8, first_grad, jnp.where(at_row == 9, gain_grad, mixed))
    k.small[0, :, :width] = mixed
    head_row = lax.broadcasted_iota(jnp.int32, k.back_rows.shape, 0)
    by_bucket = exact(jnp.where(head_row < head_count, k.back_rows[...], 0.0), bucket_hot(), 1, 1)
    spread = (
        lax.broadcasted_iota(jnp.int32, (16, 8), 0) == lax.broadcasted_iota(jnp.int32, (16, 8), 1) + core * head_count
    ) & (lax.broadcasted_iota(jnp.int32, (16, 8), 1) < head_count)
    k.small[0, :, width:] = jnp.zeros((16, span - width), f32)
    k.small[0, :, width : width + bucket_count] = exact(spread.astype(f32), by_bucket, 1, 0)
    def small_step(first, devices):
        items = [copy(k.small.at[first], k.small.at[first + 1 + i], device) for i, device in enumerate(devices)]
        for item in items:
            item.start()

        def finish():
            for item in items:
                item.wait()
            total = k.small[first]
            for i in range(len(items)):
                total = total + k.small[first + 1 + i]
            return total

        return finish

    finish = small_step(0, [mate])
    tick("small")

    each = 24
    own_part, mate_part = pl.ds(pl.multiple_of(core * each, 8), each), pl.ds(pl.multiple_of(mate_core * each, 8), each)

    def rows_of(which, first):
        return pl.ds(pl.multiple_of(first + which * each, 8), each)

    def exchange_in():
        for index in range(tiles):
            lanes = slice((index % 2) * tile, (index % 2 + 1) * tile)
            to_lanes = pl.ds(pl.multiple_of((2 * index + core) * tile, LANE), tile)
            k.o_in[:, to_lanes] = k.result[rows_of(core, 48 * (index // 2)), lanes]
            k.fin_send[:, index * tile : (index + 1) * tile] = k.result[rows_of(mate_core, 48 * (index // 2)), lanes]
        in_copy.start()

    in_copy = copy(k.fin_send, k.fin_recv, mate)
    tail = PLAN["tail"]
    last_in = [at for at, item in enumerate(tail) if item[0] == "in"][-1]
    for at, item in enumerate(tail):
        if at == 2:
            k.small[2] = finish()
            finish = small_step(2, [(dp ^ 2, z), (dp ^ 4, z), (dp ^ 6, z)])
        if at == len(tail) // 2:
            k.small[6] = finish()
            finish = small_step(6, [(dp, z ^ turn) for turn in range(1, 4)])
        advance(*item)
        if at == last_in:
            exchange_in()
    total = finish()
    flat = dp * 4 + z
    keep = (
        lax.broadcasted_iota(jnp.int32, (width, each), 0) == lax.broadcasted_iota(jnp.int32, (width, each), 1) + flat * each
    ).astype(f32)
    shares = exact(total[:, :width], keep, 1, 0)
    k.o_lang[...] = shares[:8]
    k.o_first[...] = shares[8:9]
    k.o_second[...] = shares[9:10]
    k.o_bias[...] = total[:all_heads, width : width + bucket_count]
    in_copy.wait_recv()
    for index in range(tiles):
        to_lanes = pl.ds(pl.multiple_of((2 * index + mate_core) * tile, LANE), tile)
        k.o_in[:, to_lanes] = k.fin_recv[:, index * tile : (index + 1) * tile]
    in_copy.wait_send()
    k.fin_send[...] = k.result_last[mate_part, :]
    last_copy = copy(k.fin_send, k.fin_last, mate)
    last_copy.start()


    def put_projections(read, lanes):
        k.o_output[:, lanes] = read(0, mine)
        for index, target in enumerate((k.o_query, k.o_key, k.o_value)):
            target[:, lanes] = jnp.concatenate([read((1 + at) * mine + index * pair, pair) for at in range(3)], axis=1)

    put_projections(lambda first, size: k.result_last[own_part, first : first + size], own_lanes)
    last_copy.wait_recv()
    put_projections(lambda first, size: k.fin_last[:, first : first + size], mate_lanes)

    for item in (way_meta, way_tokens, way_cotangent, way_grad):
        item.close()
    for index in range(2):
        way_grad.arrive(index)
    for head in range(head_count):
        for item in mix_copies(head):
            item.wait_send()
    for index in range(tiles):
        gh_copy(index).wait_send()
    for item in (*cot_relays, proj_copy, *gn_copies, last_copy):
        item.wait_send()


def hand_on(*refs):
    count = len(refs) // 2
    for source, target in zip(refs[:count], refs[count:]):
        target[...] = source[...]


def local(
    tokens,
    language,
    lengths,
    rel_bucket,
    lang_table,
    gain_first,
    w_query,
    w_key,
    w_value,
    w_output,
    bias_table,
    gain_second,
    w_in,
    w_out,
    cotangent,
):
    seqs, rows, width = tokens.shape
    span = rows * lax.axis_size("blk")
    half, mine = span // 2, width // 2
    bucket_count, all_heads = bias_table.shape
    head_count = all_heads // 2
    ff_width = w_in.shape[1]
    devices = lax.axis_size("dp") * lax.axis_size("blk")
    each, each_out = width // devices, ff_width // devices
    tiles = ff_width // width
    buckets = jnp.pad(rel_bucket, (1, 0), constant_values=-1)[None]
    vmem, anywhere = pl.BlockSpec(memory_space=pltpu.VMEM), pl.BlockSpec(memory_space=pl.ANY)
    shape = jax.ShapeDtypeStruct
    ext = pltpu.VMEM((mine // head_count + 16, span), bf16)
    sum_buffers = [
        pltpu.VMEM(found, bf16)
        for group in GROUPS
        for part_rows, part_columns, order in PARTS[group]
        for found in Sums.shapes(part_rows[1], part_columns[1], order)
    ]
    found = pl.pallas_call(
        functools.partial(block_kernel, head_count),
        out_shape=(
            shape(tokens.shape, bf16),
            shape(tokens.shape, bf16),
            *[shape((each, width), f32)] * 4,
            shape((each, ff_width), f32),
            shape((each_out, width), f32),
            shape((8, each), f32),
            shape((1, each), f32),
            shape((1, each), f32),
            shape(bias_table.shape[::-1], f32),
        ),
        in_specs=[pl.BlockSpec(memory_space=pltpu.SMEM)] * 2 + [anywhere] * 8 + [vmem] * 5,
        out_specs=(anywhere, anywhere) + (vmem,) * 10,
        scratch_shapes=[
            pltpu.VMEM((span, width), bf16),
            pltpu.VMEM((seqs, 8, LANE), jnp.int32),
            pltpu.VMEM((seqs, 8, LANE), jnp.int32),
            pltpu.VMEM((3 * mine, width), bf16),
            pltpu.VMEM((width, width), bf16),
            pltpu.VMEM((width, ff_width), bf16),
            pltpu.VMEM((ff_width, width), bf16),
            pltpu.VMEM((width, span), bf16),
            pltpu.VMEM((3 * mine, span), bf16),
            pltpu.VMEM((mine, span), f32),
            pltpu.VMEM((width, span), bf16),
            pltpu.VMEM((mine, span), bf16),
            pltpu.VMEM((half, width), f32),
            pltpu.VMEM((half, width), f32),
            pltpu.VMEM((span, width), bf16),
            pltpu.VMEM((tiles * half, width), bf16),
            pltpu.VMEM((tiles * half, width), bf16),
            pltpu.VMEM((half, tiles * mine), bf16),
            pltpu.VMEM((half, tiles * mine), bf16),
            pltpu.VMEM((span, width), bf16),
            pltpu.VMEM((half, width), bf16),
            pltpu.VMEM((half, width), bf16),
            pltpu.VMEM((LANE, 2 * span), f32),
            pltpu.VMEM((LANE, 2 * span), f32),
            pltpu.VMEM((half // 2, span), bf16),
            pltpu.VMEM((half // 2, span), bf16),
            ext,
            ext,
            ext,
            ext,
            pltpu.VMEM((8, 2 * span), f32),
            pltpu.VMEM((8, 2 * span), f32),
            pltpu.VMEM((8, span), f32),
            pltpu.VMEM((11, 16, span), f32),
            pltpu.VMEM((each, 2 * width), f32),
            pltpu.VMEM((each, 2 * width), f32),
            pltpu.VMEM((each, 2 * width), f32),
            pltpu.VMEM((4 * each, width), f32),
            pltpu.VMEM((2 * each, 2 * width), f32),
            *[pltpu.VMEM((2, 2, 2, 2, *GROUP_SHAPE[group]), bf16) for group in GROUPS],
            *sum_buffers,
            pltpu.SemaphoreType.DMA((144,)),
            pltpu.SemaphoreType.DMA((144,)),
            pltpu.SemaphoreType.DMA((8,)),
        ],
        compiler_params=pltpu.CompilerParams(
            collective_id=0, has_side_effects=True, vmem_limit_bytes=VMEM_BYTES
        ),
        name="encoder_block",
    )(
        language,
        lengths,
        tokens,
        cotangent,
        w_query,
        w_key,
        w_value,
        w_output,
        w_in,
        w_out,
        lang_table,
        gain_first,
        gain_second,
        buckets,
        bias_table.T,
    )
    found = pl.pallas_call(
        hand_on,
        out_shape=tuple(shape(part.shape, part.dtype) for part in found),
        in_specs=[vmem] * len(found),
        out_specs=tuple([vmem] * len(found)),
        compiler_params=pltpu.CompilerParams(vmem_limit_bytes=VMEM_BYTES),
        name="hand_on",
    )(*found)
    output, grad_tokens, query, key, value, out, grad_in, grad_out, lang, first, second, bias = found
    return output, grad_tokens, lang, first[0], query, key, value, out, bias.T, second[0], grad_in, grad_out


def local_plain(
    tokens,
    language,
    lengths,
    rel_bucket,
    lang_table,
    gain_first,
    w_query,
    w_key,
    w_value,
    w_output,
    bias_table,
    gain_second,
    w_in,
    w_out,
    cotangent,
):
    dp_size, blk_size = lax.axis_size("dp"), lax.axis_size("blk")
    device, place = lax.axis_index("dp"), lax.axis_index("blk")
    core = device % 2
    odd = place % 2 == 1
    width = tokens.shape[-1]
    bucket_count, all_heads = bias_table.shape
    head_count = all_heads // 2
    mine = width // 2
    span = tokens.shape[1] * blk_size
    half = span // 2
    ff_width = w_in.shape[1]

    own_tokens = to_rows(tokens, odd)
    own_cotangent = to_rows(cotangent, odd)
    other_tokens = swap_core(own_tokens)
    ids = jnp.stack([language, lengths])
    other_ids = swap_core(ids)
    mates = jnp.where(place // (blk_size // 2) == core, ids, other_ids)
    spoken, length = jnp.where(odd, mates[:, 1], mates[:, 0])

    head_first = core * mine
    own_weights = jnp.concatenate(
        [lax.dynamic_slice_in_dim(w, head_first, mine, 1) for w in (w_query, w_key, w_value)], 1
    )
    own_weights_t = own_weights.T
    own_bias = lax.dynamic_slice_in_dim(bias_table, core * head_count, head_count, 1)
    bucket_hot = (rel_bucket[:, None] == jnp.arange(bucket_count)[None, :]).astype(f32)
    hot_later = jnp.pad(bucket_hot, ((1, 0), (0, 0)))
    hot_back = jnp.pad(bucket_hot[::-1], ((1, 0), (0, 0)))
    bias_later = jnp.pad(jnp.dot(hot_later, own_bias, precision=highest).T, ((0, 8 - head_count), (0, 0)))
    bias_back = jnp.pad(jnp.dot(hot_back, own_bias, precision=highest).T, ((0, 8 - head_count), (0, 0)))
    position = (jnp.arange(span) + half * core) % span
    key_mask = jnp.where(position < length, 0.0, masked_score).astype(f32)[None]

    embedding = lax.dynamic_slice_in_dim(lang_table, spoken, 1, 0).astype(f32)
    with_lang_all = jnp.concatenate([own_tokens, other_tokens]).astype(f32) + embedding
    scale_all = rms_parts(with_lang_all)
    normed = (with_lang_all * scale_all * gain_first).astype(bf16)
    qkv = dot(own_weights_t, normed, 1, 1).astype(bf16)
    mixture_t, attended_t, log_total = attention_forward(qkv, bias_back, key_mask, head_count)

    with_lang = with_lang_all[:half]
    other_mixture_t = swap_core(mixture_t[:, half:])
    own_mixture_t = mixture_t[:, :half]
    full_mixture_t = jnp.where(
        core == 0,
        jnp.concatenate([own_mixture_t, other_mixture_t]),
        jnp.concatenate([other_mixture_t, own_mixture_t]),
    )
    middle = with_lang + dot(full_mixture_t, w_output, 0, 0)
    scale_second = rms_parts(middle)
    normed_second = (middle * scale_second * gain_second).astype(bf16)
    hidden = dot(normed_second, w_in, 1, 0)
    active, gelu_back = jax.vjp(functools.partial(jax.nn.gelu, approximate=True), hidden)
    active = active.astype(bf16)
    output_rows = (middle + dot(active, w_out, 1, 0)).astype(bf16)
    output = from_rows(output_rows, odd)
    grad_hidden = gelu_back(dot(own_cotangent, w_out, 1, 1))[0].astype(bf16)
    grad_normed_second = dot(grad_hidden, w_in, 1, 1)
    grad_middle_part, grad_gain_second = norm_back(grad_normed_second, middle, gain_second, scale_second)
    grad_middle = own_cotangent.astype(f32) + grad_middle_part
    grad_projected = grad_middle.astype(bf16)
    grad_w_out = dot(active, own_cotangent, 0, 0)
    grad_w_in = dot(normed_second, grad_hidden, 0, 0)
    grad_w_output = dot(full_mixture_t, grad_projected, 1, 0)

    other_projected = swap_core(grad_projected)
    projected_all = jnp.concatenate([grad_projected, other_projected])
    own_output_rows = lax.dynamic_slice_in_dim(w_output, head_first, mine, 0)
    grad_mixture_t = dot(own_output_rows, projected_all, 1, 1).astype(bf16)
    grad_qkv, diagonals = attention_backward(
        qkv, grad_mixture_t, attended_t, log_total, bias_later, key_mask, head_count
    )
    pieces = diagonals.reshape(head_count, 8, 2 * span)
    by_distance = sum(jnp.roll(pieces[:, i], -i, axis=-1) for i in range(8))
    grad_bias_own = jnp.dot(by_distance, hot_later, precision=highest).T
    grad_bias = lax.dynamic_update_slice_in_dim(
        jnp.zeros(bias_table.shape, f32), grad_bias_own, core * head_count, 1
    )

    grad_normed_all = dot(grad_qkv, own_weights_t, 0, 0)
    from_other = swap_core(grad_normed_all[half:].astype(bf16))
    grad_normed = grad_normed_all[:half] + from_other.astype(f32)
    grad_start, grad_gain_first = norm_back(grad_normed, with_lang, gain_first, scale_all[:half])
    grad_with_lang = grad_middle + grad_start
    grad_tokens = from_rows(grad_with_lang.astype(bf16), odd)
    lang_hot = (jnp.arange(lang_table.shape[0]) == spoken).astype(f32)
    grad_lang = lang_hot[:, None] * jnp.sum(grad_with_lang, axis=0)[None, :]
    grad_w_qkv = dot(normed, grad_qkv, 0, 1)

    names = ("dp", "blk")

    def scattered(value, dim=0):
        return lax.psum_scatter(value, names, scatter_dimension=dim, tiled=True)

    grads_qkv = []
    for part in jnp.split(grad_w_qkv, 3, axis=1):
        whole = jnp.zeros((width, width), f32)
        grads_qkv.append(scattered(lax.dynamic_update_slice_in_dim(whole, part, head_first, 1)))
    return (
        output,
        grad_tokens,
        scattered(grad_lang, 1),
        scattered(grad_gain_first),
        *grads_qkv,
        scattered(grad_w_output),
        lax.psum(grad_bias, names),
        scattered(grad_gain_second),
        scattered(grad_w_in),
        scattered(grad_w_out),
    )


def solution(mesh):
    rows = P("dp", "blk", None)
    shard = P(("dp", "blk"))
    matrix = P(("dp", "blk"), None)
    fits = (mesh.shape["dp"], mesh.shape["blk"]) == (8, 4)
    return jax.shard_map(
        local if fits else local_plain,
        mesh=mesh,
        in_specs=(rows, P("dp"), P("dp")) + (P(),) * 11 + (rows,),
        out_specs=(
            rows,
            rows,
            P(None, ("dp", "blk")),
            shard,
            matrix,
            matrix,
            matrix,
            matrix,
            P(),
            shard,
            matrix,
            matrix,
        ),
        check_vma=False,
    )
```

```python
import functools
import itertools

import jax
import jax.numpy as jnp
from jax import lax
from jax.experimental import pallas as pl
from jax.experimental.pallas import tpu as pltpu
from jax.sharding import PartitionSpec as P

MESH = pl.DeviceIdType.MESH
bf16 = jnp.bfloat16
f32 = jnp.float32
eps_norm = 1e-06
masked_score = -1e30
highest = lax.Precision.HIGHEST
LANE = 128
VMEM_BYTES = 63 * 2**20


def dot(left, right, left_dim, right_dim):
    return lax.dot_general(
        left, right, (((left_dim,), (right_dim,)), ((), ())), preferred_element_type=f32
    )


def move_pairs(dp_size, blk_size, same):
    half = blk_size // 2
    pairs = []
    for d in range(dp_size):
        for z in range(blk_size):
            low = z % 2 if same else 1 - z % 2
            target = (2 * (d // 2) + z // half, 2 * (d % 2) + low)
            pairs.append((d * blk_size + z, target[0] * blk_size + target[1]))
    return pairs


def swap_core(value):
    size = lax.axis_size("dp")
    return lax.ppermute(value, "dp", [(d, d ^ 1) for d in range(size)])


def to_rows(value, odd):
    dp_size, blk_size = lax.axis_size("dp"), lax.axis_size("blk")
    first = jnp.where(odd, value[1], value[0])
    second = jnp.where(odd, value[0], value[1])
    first = lax.ppermute(first, ("dp", "blk"), move_pairs(dp_size, blk_size, True))
    second = lax.ppermute(second, ("dp", "blk"), move_pairs(dp_size, blk_size, False))
    return jnp.where(odd, jnp.concatenate([second, first]), jnp.concatenate([first, second]))


def from_rows(value, odd):
    dp_size, blk_size = lax.axis_size("dp"), lax.axis_size("blk")
    low, high = jnp.split(value, 2)
    first = jnp.where(odd, high, low)
    second = jnp.where(odd, low, high)
    back_same = [(b, a) for a, b in move_pairs(dp_size, blk_size, True)]
    back_other = [(b, a) for a, b in move_pairs(dp_size, blk_size, False)]
    first = lax.ppermute(first, ("dp", "blk"), back_same)
    second = lax.ppermute(second, ("dp", "blk"), back_other)
    return jnp.where(odd, jnp.stack([second, first]), jnp.stack([first, second]))


def window(core, row_start, col_start, half, span):
    base = col_start - row_start + span
    turns = (row_start >= half) - (col_start >= half)
    return pl.multiple_of(base + core * (turns * 2 * half), LANE) if turns else base


def split_three(value):
    high = value.astype(bf16).astype(f32)
    middle = (value - high).astype(bf16).astype(f32)
    low = (value - high - middle).astype(bf16).astype(f32)
    return high, middle, low


def forward_kernel(head_count, head_size, qkv, bias_row, key_mask, mixture, attended, log_total, table, scores, weights, key_ext, query_ext, value_ext):
    core = lax.axis_index("dp") % 2
    width = head_count * head_size
    span = qkv.shape[1]
    half = span // 2
    step = 2 * LANE
    row_id = lax.broadcasted_iota(jnp.int32, (16, span), 0)
    key_ext[pl.ds(head_size, 16), :] = jnp.where(row_id == 0, key_mask[...], 0.0).astype(bf16)
    query_ext[pl.ds(head_size, 16), :] = jnp.where(row_id == 0, 1.0, 0.0).astype(bf16)
    value_ext[pl.ds(head_size, 16), :] = jnp.where(row_id == 0, 1.0, 0.0).astype(bf16)

    def one_head(head, _):
        first = pl.multiple_of(head * head_size, head_size)
        row = bias_row[pl.ds(head, 1), :]
        table[...] = pltpu.roll(jnp.broadcast_to(row, table.shape), 0, 1, stride=1, stride_axis=0)
        query_ext[pl.ds(0, head_size), :] = qkv[pl.ds(first, head_size), :]
        key_ext[pl.ds(0, head_size), :] = qkv[pl.ds(width + first, head_size), :]
        value_ext[pl.ds(0, head_size), :] = qkv[pl.ds(2 * width + first, head_size), :]
        for row_start in range(0, span, step):
            query = query_ext[:, row_start : row_start + step]
            best = None
            for col_start in range(0, span, LANE):
                part = dot(key_ext[:, col_start : col_start + LANE], query, 0, 0)
                place = window(core, col_start, row_start, half, span)
                part = part + table[:, pl.ds(place, step)]
                scores[col_start : col_start + LANE, :] = part
                folded = jnp.max(part.reshape(LANE // 8, 8, step), axis=0)
                best = folded if best is None else jnp.maximum(best, folded)
            top = jnp.max(best, axis=0, keepdims=True)
            for col_start in range(0, span, LANE):
                weights[col_start : col_start + LANE, :] = jnp.exp(
                    scores[col_start : col_start + LANE, :] - top
                ).astype(bf16)
            summed = dot(value_ext[...], weights[...], 1, 0)
            total = summed[head_size : head_size + 1]
            part = summed[:head_size] / total
            attended[pl.ds(first, head_size), row_start : row_start + step] = part
            mixture[pl.ds(first, head_size), row_start : row_start + step] = part.astype(bf16)
            log_total[pl.ds(head, 1), row_start : row_start + step] = top + jnp.log(total)
        return 0

    lax.fori_loop(0, head_count, one_head, 0)


def attention_forward(qkv, bias_row, key_mask, head_count):
    wide, span = qkv.shape
    width = wide // 3
    head_size = width // head_count
    ext = pltpu.VMEM((head_size + 16, span), bf16)
    return pl.pallas_call(
        functools.partial(forward_kernel, head_count, head_size),
        out_shape=(
            jax.ShapeDtypeStruct((width, span), bf16),
            jax.ShapeDtypeStruct((width, span), f32),
            jax.ShapeDtypeStruct((8, span), f32),
        ),
        scratch_shapes=[
            pltpu.VMEM((LANE, 2 * span), f32),
            pltpu.VMEM((span, 2 * LANE), f32),
            pltpu.VMEM((span, 2 * LANE), bf16),
            ext,
            ext,
            ext,
        ],
        compiler_params=pltpu.CompilerParams(vmem_limit_bytes=VMEM_BYTES),
        name="attention_forward",
    )(qkv, bias_row, key_mask)


def backward_kernel(head_count, head_size, qkv, grad_mixture, attended, log_total, bias_row, key_mask, grads, diagonals, table, sums, weights, slopes, key_ext, query_ext, value_ext, grad_ext):
    core = lax.axis_index("dp") % 2
    width = head_count * head_size
    span = qkv.shape[1]
    half = span // 2
    row_id = lax.broadcasted_iota(jnp.int32, (16, span), 0)
    key_tail = jnp.where(row_id == 0, key_mask[...], jnp.where(row_id < 4, 1.0, 0.0))
    key_ext[pl.ds(head_size, 16), :] = key_tail.astype(bf16)
    value_ext[pl.ds(head_size, 16), :] = jnp.where(row_id < 3, 1.0, 0.0).astype(bf16)

    def one_head(head, _):
        first = pl.multiple_of(head * head_size, head_size)
        row = bias_row[pl.ds(head, 1), :]
        table[...] = pltpu.roll(jnp.broadcast_to(row, table.shape), 0, 1, stride=1, stride_axis=0)
        sums[...] = jnp.zeros_like(sums)
        query = qkv[pl.ds(first, head_size), :]
        key = qkv[pl.ds(width + first, head_size), :]
        grad = grad_mixture[pl.ds(first, head_size), :]
        key_ext[pl.ds(0, head_size), :] = key
        value_ext[pl.ds(0, head_size), :] = qkv[pl.ds(2 * width + first, head_size), :]
        query_ext[pl.ds(0, head_size), :] = query
        grad_ext[pl.ds(0, head_size), :] = grad
        a, b, c = split_three(-log_total[pl.ds(head, 1), :])
        query_ext[pl.ds(head_size, 16), :] = jnp.where(
            row_id == 0, 1.0, jnp.where(row_id == 1, a, jnp.where(row_id == 2, b, jnp.where(row_id == 3, c, 0.0)))
        ).astype(bf16)
        row_dot = jnp.sum(
            grad.astype(f32) * attended[pl.ds(first, head_size), :], axis=0, keepdims=True
        )
        a, b, c = split_three(-row_dot)
        grad_ext[pl.ds(head_size, 16), :] = jnp.where(
            row_id == 0, a, jnp.where(row_id == 1, b, jnp.where(row_id == 2, c, 0.0))
        ).astype(bf16)
        for row_start in range(0, span, LANE):
            rows = slice(row_start, row_start + LANE)
            for col_start in range(0, span, half):
                cols = slice(col_start, col_start + half)
                place = pl.ds(window(core, row_start, col_start, half, span), half)
                part = dot(query_ext[:, rows], key_ext[:, cols], 0, 0)
                part = jnp.exp(part + table[:, place])
                slope = part * dot(grad_ext[:, rows], value_ext[:, cols], 0, 0)
                weights[rows, cols] = part.astype(bf16)
                slopes[rows, cols] = slope.astype(bf16)
                sums[:, place] += slope
        grads[pl.ds(first, head_size), :] = dot(key, slopes[...], 1, 1).astype(bf16)
        grads[pl.ds(width + first, head_size), :] = dot(query, slopes[...], 1, 0).astype(bf16)
        grads[pl.ds(2 * width + first, head_size), :] = dot(grad, weights[...], 1, 0).astype(bf16)
        folded = sums[...]
        count = LANE
        while count > 8:
            count //= 2
            folded = folded[:count] + pltpu.roll(folded[count:], 2 * span - count, 1)
        diagonals[pl.ds(pl.multiple_of(head * 8, 8), 8), :] = folded
        return 0

    lax.fori_loop(0, head_count, one_head, 0)


def attention_backward(qkv, grad_mixture, attended, log_total, bias_row, key_mask, head_count):
    wide, span = qkv.shape
    width = wide // 3
    head_size = width // head_count
    ext = pltpu.VMEM((head_size + 16, span), bf16)
    square = pltpu.VMEM((span, span), bf16)
    slab = pltpu.VMEM((LANE, 2 * span), f32)
    return pl.pallas_call(
        functools.partial(backward_kernel, head_count, head_size),
        out_shape=(
            jax.ShapeDtypeStruct((wide, span), bf16),
            jax.ShapeDtypeStruct((8 * head_count, 2 * span), f32),
        ),
        scratch_shapes=[slab, slab, square, square, ext, ext, ext, ext],
        compiler_params=pltpu.CompilerParams(vmem_limit_bytes=VMEM_BYTES),
        name="attention_backward",
    )(qkv, grad_mixture, attended, log_total, bias_row, key_mask)


def rms_parts(values):
    return lax.rsqrt(jnp.mean(values * values, axis=-1, keepdims=True) + eps_norm)


def norm_back(grad, values, gain, scale):
    weighted = grad * gain
    inner = jnp.mean(weighted * values, axis=-1, keepdims=True)
    return scale * weighted - values * (scale * scale * scale) * inner, jnp.sum(grad * values * scale, axis=0)


def gelu_both(value):
    root = 0.7978845608028654
    square = value * value
    bent = jnp.tanh(value * (root + root * 0.044715 * square))
    up = 0.5 * bent + 0.5
    active = value * up
    slope = up + active * ((1.0 - bent) * (root + 3 * 0.044715 * root * square))
    return active, slope


AXES = ("y", "x", "h", "l")


class Sums:
    def __init__(self, kernel, blocks, rows, columns, order, buffers):
        self.kernel, self.blocks, self.order, self.buffers = kernel, blocks, order, buffers
        self.rows, self.columns = pl.ds(*rows), pl.ds(*columns)
        self.copies = []
        for step, axis in enumerate(order):
            source = self.place(step, axis, 1 - kernel.at[axis])
            self.copies.append(kernel.copy(source, buffers[step], kernel.partner[axis]))

    def place(self, step, axis, which):
        picks = []
        for other in AXES:
            if other == axis:
                picks.append(pl.ds(which, 1))
            else:
                picks.append(pl.ds(self.kernel.at[other], 1) if other in self.order[:step] else pl.ds(0, 2))
        return self.blocks.at[(*picks, self.rows, self.columns)]

    def begin(self, step):
        self.copies[step].start()

    def end(self, step, result=None):
        self.copies[step].wait()
        axis = self.order[step]
        kept = self.place(step, axis, self.kernel.at[axis])
        buffer = self.buffers[step]
        for index in itertools.product(*(range(count) for count in buffer.shape[:4])):
            total = kept[index].astype(f32) + buffer[index].astype(f32)
            if result is None:
                kept[index] = total.astype(bf16)
            else:
                result[self.rows, self.columns] = total

    def shapes(rows, columns, order):
        return [
            (*(1 if axis in order[: step + 1] else 2 for axis in AXES), rows, columns) for step in range(len(order))
        ]


FLAT, TALL, DEEP = ("x", "y", "l", "h"), ("y", "x", "l", "h"), ("l", "h", "x", "y")
PARTS = {
    "out": [((0, 64), (0, 384), FLAT), ((0, 64), (384, 384), TALL), ((64, 32), (0, 768), DEEP)],
    "in": [((0, 64), (0, 384), FLAT), ((0, 64), (384, 384), TALL), ((64, 32), (0, 768), DEEP)],
    "mix": [((0, 32), (0, 384), FLAT), ((32, 16), (0, 384), TALL)],
    "low": [((0, 32), (0, 384), TALL), ((32, 16), (0, 384), FLAT)],
    "mid": [((0, 32), (0, 384), FLAT), ((32, 16), (0, 384), TALL)],
    "high": [((0, 32), (0, 384), TALL), ((32, 16), (0, 384), FLAT)],
}
PLAN = {
    "mix": [("out", 0, 0), ("out", 1, 0)],
    "head2": [("mix", 1, 0), ("out", 2, 0)],
    "pair3": [("out", 0, 1), ("in", 2, 0), ("in", 1, 0), ("mix", 0, 0)],
    "head4": [("in", 0, 0), ("low", 0, 0), ("low", 1, 0), ("mix", 1, 1), ("out", 1, 1)],
    "head5": [("mid", 1, 0)],
    "high": [("mix", 0, 1), ("out", 0, 2), ("out", 2, 1)],
    "gtok": [("low", 1, 1), ("mid", 0, 0), ("mix", 1, 2), ("in", 1, 1), ("in", 0, 1), ("low", 0, 1), ("out", 1, 2)],
    "small": [("in", 2, 1), ("mid", 1, 1)],
    "tail": [("mix", 0, 2), ("out", 0, 3), ("high", 1, 0), ("out", 2, 2), ("high", 0, 0), ("mix", 1, 3), ("low", 1, 2), ("mid", 0, 1), ("in", 2, 2), ("mid", 1, 2), ("low", 0, 2), ("out", 1, 3), ("mix", 0, 3), ("high", 1, 1), ("out", 2, 3), ("high", 0, 1), ("low", 1, 3), ("in", 1, 2), ("in", 0, 2), ("mid", 0, 2), ("in", 2, 3), ("mid", 1, 3), ("high", 1, 2), ("low", 0, 3), ("high", 0, 2), ("mid", 0, 3), ("high", 1, 3), ("in", 1, 3), ("in", 0, 3), ("high", 0, 3)],
}
GROUP_SHAPE = {"out": (96, 768), "in": (96, 768), "mix": (48, 384), "low": (48, 384), "mid": (48, 384), "high": (48, 384)}
GROUPS = ("out", "in", "mix", "low", "mid", "high")


class Kernel:
    pass


def block_kernel(head_count, language_ids, length_ids, tokens, cotangent, w_query, w_key, w_value, w_output, w_in, w_out, lang_table, first_gain, second_gain, buckets, bias_table, *refs):
    k = Kernel()
    names = (
        "output", "grad_tokens", "o_query", "o_key", "o_value", "o_output", "o_in", "o_out",
        "o_lang", "o_first", "o_second", "o_bias", "tok", "meta_out", "meta_in", "wt",
        "wo", "win", "wout", "normed_t", "qkv", "att", "mix", "gmix",
        "middle", "acc", "ns", "slope", "acts", "act_in", "gh_in", "cot",
        "proj", "out_rows", "table", "sums", "prob", "ds", "key_ext", "value_ext",
        "query_ext", "grad_ext", "bias_rows", "back_rows", "distance", "small", "fin_send", "fin_recv",
        "fin_last", "result", "result_last", "g_out", "g_in", "g_mix", "g_low", "g_mid",
        "g_high",
    )
    for name, ref in zip(names, refs):
        setattr(k, name, ref)
    rest = list(refs[len(names):])
    send_sem, recv_sem, load_sem = rest[-3:]
    rest = rest[:-3]
    dp, z = lax.axis_index("dp"), lax.axis_index("blk")
    core = dp % 2
    mate_core = 1 - core
    base = dp - core
    k.dp = dp
    k.at = {"x": (dp // 2) % 2, "y": (dp // 4) % 2, "h": z // 2, "l": z % 2}
    k.partner = {"x": (dp ^ 2, z), "y": (dp ^ 4, z), "h": (dp, z ^ 2), "l": (dp, z ^ 1)}
    mate = (base + mate_core, z)
    used = [0]
    width = lang_table.shape[1]
    span = k.qkv.shape[1]
    half, quarter = span // 2, span // 4
    mine = width // 2
    head_size = mine // head_count
    tile = mine
    tiles = k.win.shape[1] // width

    def take(count=1):
        used[0] += count
        return used[0] - count

    def copy(source, target, device, slot=None):
        slot = take() if slot is None else slot
        return pltpu.make_async_remote_copy(
            src_ref=source,
            dst_ref=target,
            send_sem=send_sem.at[slot],
            recv_sem=recv_sem.at[slot],
            device_id=device,
            device_id_type=MESH,
        )

    k.copy = copy

    barrier = pltpu.get_barrier_semaphore()
    friends = [(base + (core + turn) % 2, z ^ far) for turn in range(2) for far in range(4) if turn or far]
    friends += [k.partner["x"], k.partner["y"], (dp ^ 6, z)]
    for friend in friends:
        pl.semaphore_signal(barrier, inc=1, device_id=friend, device_id_type=MESH)

    loads = []

    def load(source, target):
        item = pltpu.make_async_copy(source, target, load_sem.at[len(loads)])
        item.start()
        loads.append(item)

    own_lanes = pl.ds(pl.multiple_of(core * mine, LANE), mine)
    mate_lanes = pl.ds(pl.multiple_of(mate_core * mine, LANE), mine)
    def stage_rows(index):
        return pl.ds((index % 2) * width, width)

    def stage_lanes(index):
        return pl.ds((index // 2) * mine, mine)

    for index, source in enumerate((w_query, w_key, w_value)):
        load(source.at[:, own_lanes], k.acts.at[stage_rows(index), stage_lanes(index)])
    load(w_output.at[own_lanes], k.wo.at[pl.ds(0, mine)])
    load(w_output.at[mate_lanes], k.wo.at[pl.ds(mine, mine)])
    load(w_in, k.win)
    load(w_out, k.wout)

    row_id = lax.broadcasted_iota(jnp.int32, k.meta_out.shape[1:], 0)
    for index in range(2):
        k.meta_out[index] = jnp.where(row_id == 0, language_ids[index], length_ids[index])
    pl.semaphore_wait(barrier, len(friends))

    side = z % 2

    class Route:
        def __init__(self, pick, target):
            self.slots = take(2)
            self.items = []
            for index in range(2):
                device = (base + z // 2, 2 * core + index)
                here = (z // 2 == core) & (2 * core + index == z)
                source = pick(index)
                far = pltpu.make_async_remote_copy(
                    src_ref=source,
                    dst_ref=target(side),
                    send_sem=send_sem.at[self.slots + index],
                    recv_sem=recv_sem.at[self.slots + side],
                    device_id=device,
                    device_id_type=MESH,
                )
                near = pltpu.make_async_copy(source, target(side), recv_sem.at[self.slots + side])
                self.items.append((here, far, near))
            self.arrivals = [copy(target(j), target(j), mate, self.slots + j) for j in range(2)]

        def start(self):
            for here, far, near in self.items:
                pl.when(here)(near.start)
                pl.when(jnp.logical_not(here))(far.start)

        def arrive(self, index):
            self.arrivals[index].wait_recv()

        def close(self):
            for here, far, _ in self.items:
                pl.when(jnp.logical_not(here))(far.wait_send)

    def part_rows(index):
        return pl.ds(pl.multiple_of(index * quarter, quarter), quarter)

    way_meta = Route(lambda i: k.meta_out.at[i], lambda j: k.meta_in.at[j])
    way_tokens = Route(lambda i: tokens.at[i], lambda j: k.tok.at[part_rows(j)])
    way_meta.start()
    way_tokens.start()

    all_heads, bucket_count = bias_table.shape
    places = 2 * span

    def bucket_hot():
        return (lax.broadcasted_iota(jnp.int32, (bucket_count, places), 0) == buckets[...]).astype(f32)

    pick = (
        lax.broadcasted_iota(jnp.int32, (all_heads, 8), 0)
        == lax.broadcasted_iota(jnp.int32, (all_heads, 8), 1) + core * head_count
    ) & (lax.broadcasted_iota(jnp.int32, (all_heads, 8), 1) < head_count)

    def exact(left, right, left_dim, right_dim):
        return lax.dot_general(
            left, right, (((left_dim,), (right_dim,)), ((), ())), precision=highest, preferred_element_type=f32
        )

    own_bias = exact(bias_table[...], pick.astype(f32), 0, 0)
    bias_rows = exact(own_bias, bucket_hot(), 0, 0)
    k.bias_rows[...] = bias_rows
    flip = (
        lax.broadcasted_iota(jnp.int32, (LANE, LANE), 0) + lax.broadcasted_iota(jnp.int32, (LANE, LANE), 1) == LANE - 1
    ).astype(f32)
    for first in range(0, places, LANE):
        k.back_rows[:, first : first + LANE] = exact(bias_rows[:, places - LANE - first : places - first], flip, 1, 0)
    k.back_rows[...] = pltpu.roll(k.back_rows[...], 1, 1)
    for index in range(3):
        loads[index].wait()
        k.wt[index * mine : (index + 1) * mine, :] = k.acts[stage_rows(index), stage_lanes(index)].T

    for index in range(2):
        way_meta.arrive(index)
    language = k.meta_in[0, 0:1, 0:1]
    length = k.meta_in[0, 1:2, 0:1]
    embedding = jnp.zeros((1, width), f32)
    for index in range(8):
        embedding = embedding + jnp.where(language == index, lang_table[index : index + 1, :].astype(f32), 0.0)
    gain_first, gain_second = first_gain[...].reshape(1, width), second_gain[...].reshape(1, width)
    position = (lax.broadcasted_iota(jnp.int32, (1, span), 1) + half * core) % span
    key_mask = jnp.where(position < length, 0.0, masked_score)

    relays = [copy(k.tok.at[part_rows(j)], k.tok.at[part_rows(2 + j)], mate) for j in range(2)]
    way_cotangent = Route(lambda i: cotangent.at[i], lambda j: k.cot.at[part_rows(j)])

    def project(index):
        rows = slice(index * quarter, (index + 1) * quarter)
        values = k.tok[rows, :].astype(f32) + embedding
        normed = (values * rms_parts(values) * gain_first).astype(bf16)
        k.normed_t[:, rows] = normed.T
        k.qkv[:, rows] = dot(k.wt[...], k.normed_t[:, rows], 1, 0).astype(bf16)

    for index in range(2):
        way_tokens.arrive(index)
        relays[index].start()
    for index in range(2):
        project(index)
    for index in range(2):
        relays[index].wait_recv()
    for index in range(2):
        relays[index].wait_send()
    way_cotangent.start()
    for index in range(2):
        project(2 + index)

    step = half
    block = k.prob.shape[0]
    ext_row = lax.broadcasted_iota(jnp.int32, (16, span), 0)
    tail = pl.ds(head_size, 16)
    k.key_ext[tail, :] = jnp.where(ext_row == 0, key_mask, jnp.where(ext_row < 4, 1.0, 0.0)).astype(bf16)
    k.query_ext[tail, :] = jnp.where(ext_row == 0, 1.0, 0.0).astype(bf16)
    k.value_ext[tail, :] = jnp.where(ext_row < 3, 1.0, 0.0).astype(bf16)
    mix_slots = take(2 * head_count)

    def mix_copies(head):
        rows = pl.ds(pl.multiple_of(head * head_size, head_size), head_size)
        far = pl.ds(pl.multiple_of(mine + head * head_size, head_size), head_size)
        return [
            copy(
                k.mix.at[rows, pl.ds(side_at * half, half)],
                k.mix.at[far, pl.ds((1 - side_at) * half, half)],
                mate,
                mix_slots + 2 * head + side_at,
            )
            for side_at in range(2)
        ]

    def score_rows(start):
        return (k.acc if start < half else k.middle).at[start % half : start % half + LANE, :step]

    def weight_block(start):
        lane = (start // block) % 2 * step
        return (k.prob if start < half else k.ds).at[:, lane : lane + step]

    def forward_head(head, _):
        first = pl.multiple_of(head * head_size, head_size)
        row = k.back_rows[pl.ds(head, 1), :]
        k.table[...] = pltpu.roll(jnp.broadcast_to(row, k.table.shape), 0, 1, stride=1, stride_axis=0)
        k.query_ext[pl.ds(0, head_size), :] = k.qkv[pl.ds(first, head_size), :]
        k.key_ext[pl.ds(0, head_size), :] = k.qkv[pl.ds(mine + first, head_size), :]
        k.value_ext[pl.ds(0, head_size), :] = k.qkv[pl.ds(2 * mine + first, head_size), :]
        for row_start in range(0, span, step):
            query = k.query_ext[:, row_start : row_start + step]
            best = None
            for start in range(0, span, LANE):
                part = dot(k.key_ext[:, start : start + LANE], query, 0, 0)
                part = part + k.table[:, pl.ds(window(core, start, row_start, half, span), step)]
                score_rows(start)[...] = part
                folded = jnp.max(part.reshape(LANE // 8, 8, step), axis=0)
                best = folded if best is None else jnp.maximum(best, folded)
            top = jnp.max(best, axis=0, keepdims=True)
            for start in range(0, span, LANE):
                rows = slice(start % block, start % block + LANE)
                weight_block(start)[rows, :] = jnp.exp(score_rows(start)[...] - top).astype(bf16)
            summed = None
            for start in range(0, span, block):
                more = dot(k.value_ext[:, start : start + block], weight_block(start)[...], 1, 0)
                summed = more if summed is None else summed + more
            total = summed[head_size : head_size + 1]
            part = summed[:head_size] / total
            k.att[pl.ds(first, head_size), row_start : row_start + step] = part
            k.mix[pl.ds(first, head_size), row_start : row_start + step] = part.astype(bf16)
            k.distance[pl.ds(head, 1), row_start : row_start + step] = top + jnp.log(total)
        for item in mix_copies(head):
            item.start()
        return 0

    lax.fori_loop(0, head_count, forward_head, 0)

    loads[3].wait()
    loads[4].wait()
    for head in range(head_count):
        for item in mix_copies(head):
            item.wait_recv()
    for index in range(2):
        rows = slice(index * quarter, (index + 1) * quarter)
        values = k.tok[rows, :].astype(f32) + embedding + dot(k.mix[:, rows], k.wo[...], 0, 0)
        k.middle[rows, :] = values
        k.acc[rows, :] = values
        k.ns[rows, :] = (values * rms_parts(values) * gain_second).astype(bf16)
    ns_copy = copy(k.ns.at[pl.ds(0, half)], k.ns.at[pl.ds(half, half)], mate)
    ns_copy.start()
    loads[5].wait()
    loads[6].wait()
    act_slots = take(tiles)
    gh_slots = take(tiles)

    def tile_rows(index):
        return pl.ds(pl.multiple_of(index * half, half), half)

    def wide_lanes(index):
        return pl.ds(pl.multiple_of(index * width, width), width)

    def tile_lanes(index):
        return pl.ds(pl.multiple_of(index * tile, tile), tile)

    def act_copy(index):
        return copy(k.acts.at[tile_rows(index), mate_lanes], k.act_in.at[:, tile_lanes(index)], mate, act_slots + index)

    def gh_copy(index):
        return copy(k.acts.at[tile_rows(index), mate_lanes], k.gh_in.at[:, tile_lanes(index)], mate, gh_slots + index)

    def forward_tile(index, _):
        lanes = wide_lanes(index)
        for first in range(0, half, quarter):
            rows = pl.ds(pl.multiple_of(index * half + first, quarter), quarter)
            active, slope = gelu_both(dot(k.ns[first : first + quarter], k.win[:, lanes], 1, 0))
            active = active.astype(bf16)
            k.acts[rows, :] = active
            k.slope[rows, :] = slope.astype(bf16)
            k.acc[first : first + quarter] += dot(active, k.wout[lanes, :], 1, 0)
        act_copy(index).start()
        return 0

    lax.fori_loop(0, tiles, forward_tile, 0)
    way_output = Route(lambda i: k.out_rows.at[part_rows(i)], lambda j: k.output.at[j])
    k.out_rows[...] = k.acc[...].astype(bf16)
    way_output.start()

    cot_relays = [copy(k.cot.at[part_rows(j)], k.cot.at[part_rows(2 + j)], mate) for j in range(2)]
    for index in range(2):
        way_cotangent.arrive(index)
        cot_relays[index].start()
    for index in range(2):
        cot_relays[index].wait_recv()
    parts = {}
    for group in GROUPS:
        parts[group] = []
        for rows, columns, order in PARTS[group]:
            parts[group].append(Sums(k, getattr(k, "g_" + group), rows, columns, order, [rest.pop(0) for _ in order]))

    def begin(group):
        for part in parts[group]:
            part.begin(0)

    results = {"out": k.o_out, "in": k.result}
    for index, group in enumerate(GROUPS[2:]):
        results[group] = k.result_last.at[:, pl.ds(index * mine, mine)]

    def advance(group, part, at):
        parts[group][part].end(at, results[group] if at == 3 else None)
        if at < 3:
            parts[group][part].begin(at + 1)

    def tick(name):
        for item in PLAN.get(name, ()):
            advance(*item)

    def out_tile(index, _):
        act_copy(index).wait_recv()
        grad = dot(k.acts[tile_rows(index), own_lanes], k.cot[:half], 0, 0)
        grad = grad + dot(k.act_in[:, tile_lanes(index)], k.cot[half:], 0, 0)
        k.g_out[index // 2, index % 2] = grad.reshape(2, 2, tile // 4, width).astype(bf16)
        return 0

    lax.fori_loop(0, tiles, out_tile, 0)
    begin("out")

    def put_blocks(target, grad, rows, lanes, halves=(0, 1)):
        each = grad.shape[0] // 32
        for index in range(4):
            for at in range(4):
                first = (8 * index + at) * each
                both = jnp.concatenate([grad[first : first + each], grad[first + 4 * each : first + 5 * each]])
                up = index // 2
                up = halves[up] if up < len(halves) else up
                target[up, index % 2, at // 2, at % 2, rows, lanes] = both.astype(bf16)

    k.acc[...] = jnp.zeros_like(k.acc)
    for index in range(tiles):
        act_copy(index).wait_send()

    def back_tile(index, _):
        lanes = wide_lanes(index)
        grad = dot(k.cot[:half], k.wout[lanes, :], 1, 1)
        grad = (grad * k.slope[tile_rows(index), :].astype(f32)).astype(bf16)
        k.acts[tile_rows(index), :] = grad
        gh_copy(index).start()
        k.act_in[:, tile_lanes(index)] = k.acts[tile_rows(index), own_lanes]
        k.acc[...] += dot(grad, k.win[:, lanes], 1, 1)
        for at in range(tiles):
            if f"back{at}" in PLAN:
                pl.when(index == at)(functools.partial(tick, f"back{at}"))
        return 0

    lax.fori_loop(0, tiles, back_tile, 0)
    ns_copy.wait_recv()
    for index in range(tiles):
        gh_copy(index).wait_recv()
    for index in range(2):
        lanes = slice(index * width, (index + 1) * width)
        grad = dot(k.ns[:half], k.act_in[:, lanes], 0, 0) + dot(k.ns[half:], k.gh_in[:, lanes], 0, 0)
        put_blocks(k.g_in, grad, pl.ds(48 * index, 48), pl.ds(0, width))
        tick(f"in{index}")
    begin("in")

    gain_grad = jnp.zeros((1, width), f32)
    for index in range(2):
        rows = slice(index * quarter, (index + 1) * quarter)
        values, grad = k.middle[rows, :], k.acc[rows, :]
        back, part = norm_back(grad, values, gain_second, rms_parts(values))
        gain_grad = gain_grad + part.reshape(1, width)
        back = back + k.cot[rows, :].astype(f32)
        k.middle[rows, :] = back
        k.proj[rows, :] = back.astype(bf16)
    proj_copy = copy(k.proj, k.tok.at[pl.ds(half, half)], mate)
    proj_copy.start()
    tick("norm")
    proj_copy.wait_recv()
    k.gmix[:, :half] = dot(k.wo[:mine], k.proj[...], 1, 1).astype(bf16)
    k.gmix[:, half:] = dot(k.wo[:mine], k.tok[half:], 1, 1).astype(bf16)
    grad = dot(k.mix[:, :half], k.proj[:, own_lanes], 1, 0) + dot(k.mix[:, half:], k.tok[half:, own_lanes], 1, 0)
    put_blocks(k.g_mix, grad, pl.ds(0, 48), pl.ds(0, mine), (core, mate_core))
    begin("mix")
    tick("mix")

    def backward_head(head, _):
        first = pl.multiple_of(head * head_size, head_size)
        row = k.bias_rows[pl.ds(head, 1), :]
        k.table[...] = pltpu.roll(jnp.broadcast_to(row, k.table.shape), 0, 1, stride=1, stride_axis=0)
        k.sums[...] = jnp.zeros_like(k.sums)
        query_rows, key_rows = pl.ds(first, head_size), pl.ds(mine + first, head_size)
        value_rows = pl.ds(2 * mine + first, head_size)
        query, key = k.qkv[query_rows, :], k.qkv[key_rows, :]
        grad = k.gmix[pl.ds(first, head_size), :]
        k.key_ext[pl.ds(0, head_size), :] = key
        k.value_ext[pl.ds(0, head_size), :] = k.qkv[value_rows, :]
        k.query_ext[pl.ds(0, head_size), :] = query
        k.grad_ext[pl.ds(0, head_size), :] = grad

        def three(value, start):
            found = jnp.where(ext_row == 0, 1.0, 0.0) if start else 0.0
            for at, piece in enumerate(split_three(value)):
                found = jnp.where(ext_row == start + at, piece, found)
            return found.astype(bf16)

        k.query_ext[tail, :] = three(-k.distance[pl.ds(head, 1), :span], 1)
        row_dot = jnp.sum(grad.astype(f32) * k.att[pl.ds(first, head_size), :], axis=0, keepdims=True)
        k.grad_ext[tail, :] = three(-row_dot, 0)
        grad_key = grad_value = None
        for outer in range(0, span, block):
            for row_start in range(outer, outer + block, LANE):
                rows = slice(row_start, row_start + LANE)
                inner = slice(row_start - outer, row_start - outer + LANE)
                for col_start in range(0, span, half):
                    cols = slice(col_start, col_start + half)
                    place = pl.ds(window(core, row_start, col_start, half, span), half)
                    part = dot(k.query_ext[:, rows], k.key_ext[:, cols], 0, 0)
                    part = jnp.exp(part + k.table[:, place])
                    slope = part * dot(k.grad_ext[:, rows], k.value_ext[:, cols], 0, 0)
                    k.prob[inner, cols] = part.astype(bf16)
                    k.ds[inner, cols] = slope.astype(bf16)
                    k.sums[:, place] += slope
            wide = slice(outer, outer + block)
            k.qkv[query_rows, wide] = dot(key, k.ds[...], 1, 1).astype(bf16)
            more_key = dot(query[:, wide], k.ds[...], 1, 0)
            more_value = dot(grad[:, wide], k.prob[...], 1, 0)
            grad_key = more_key if grad_key is None else grad_key + more_key
            grad_value = more_value if grad_value is None else grad_value + more_value
        k.qkv[key_rows, :] = grad_key.astype(bf16)
        k.qkv[value_rows, :] = grad_value.astype(bf16)
        folded = k.sums[...]
        count = LANE
        while count > 8:
            count //= 2
            folded = folded[:count] + pltpu.roll(folded[count:], 2 * span - count, 1)
        at = lax.broadcasted_iota(jnp.int32, folded.shape, 0)
        for bit in (4, 2, 1):
            folded = jnp.where(at % (2 * bit) >= bit, pltpu.roll(folded, 2 * span - bit, 1), folded)
        k.back_rows[pl.ds(head, 1), :] = jnp.sum(folded, axis=0, keepdims=True)
        for at in range(head_count):
            pl.when(head == at)(functools.partial(after_head, at))
        return 0

    pair = 2 * head_size

    def put_pair(target, index):
        rows = [k.qkv[which * mine + index * pair : which * mine + (index + 1) * pair, :] for which in range(3)]
        grad = dot(k.normed_t[...], jnp.concatenate(rows), 1, 1)
        put_blocks(target, grad, pl.ds(0, 48), pl.ds(0, 3 * pair))

    def after_head(head):
        tick(f"head{head}")
        if head in (1, 3):
            group = GROUPS[3 + head // 2]
            put_pair(getattr(k, "g_" + group), head // 2)
            begin(group)
            tick(f"pair{head}")

    lax.fori_loop(0, head_count, backward_head, 0)

    for index in range(2):
        way_output.arrive(index)
    way_output.close()
    ns_copy.wait_send()
    gn_copies = []
    for index in range(2):
        rows = slice(index * quarter, (index + 1) * quarter)
        k.ns[rows, :] = dot(k.qkv[:, half + index * quarter : half + (index + 1) * quarter], k.wt[...], 0, 0).astype(bf16)
        gn_copies.append(copy(k.ns.at[part_rows(index)], k.ns.at[part_rows(2 + index)], mate))
        gn_copies[index].start()
    put_pair(k.g_high, 2)
    begin("high")
    tick("high")
    first_grad = jnp.zeros((1, width), f32)
    lang_grad = jnp.zeros((1, width), f32)
    for index in range(2):
        rows = slice(index * quarter, (index + 1) * quarter)
        gn_copies[index].wait_recv()
        grad = dot(k.qkv[:, rows], k.wt[...], 0, 0) + k.ns[half + index * quarter : half + (index + 1) * quarter, :].astype(f32)
        values = k.tok[rows, :].astype(f32) + embedding
        back, part = norm_back(grad, values, gain_first, rms_parts(values))
        first_grad = first_grad + part.reshape(1, width)
        back = back + k.middle[rows, :]
        lang_grad = lang_grad + jnp.sum(back, axis=0, keepdims=True)
        k.out_rows[rows, :] = back.astype(bf16)
    way_grad = Route(lambda i: k.out_rows.at[part_rows(i)], lambda j: k.grad_tokens.at[j])
    way_grad.start()
    tick("gtok")

    at_row = lax.broadcasted_iota(jnp.int32, (16, width), 0)
    mixed = jnp.where(at_row == language, lang_grad, 0.0)
    mixed = jnp.where(at_row == 8, first_grad, jnp.where(at_row == 9, gain_grad, mixed))
    k.small[0, :, :width] = mixed
    head_row = lax.broadcasted_iota(jnp.int32, k.back_rows.shape, 0)
    by_bucket = exact(jnp.where(head_row < head_count, k.back_rows[...], 0.0), bucket_hot(), 1, 1)
    spread = (
        lax.broadcasted_iota(jnp.int32, (16, 8), 0) == lax.broadcasted_iota(jnp.int32, (16, 8), 1) + core * head_count
    ) & (lax.broadcasted_iota(jnp.int32, (16, 8), 1) < head_count)
    k.small[0, :, width:] = jnp.zeros((16, span - width), f32)
    k.small[0, :, width : width + bucket_count] = exact(spread.astype(f32), by_bucket, 1, 0)
    def small_step(first, devices):
        items = [copy(k.small.at[first], k.small.at[first + 1 + i], device) for i, device in enumerate(devices)]
        for item in items:
            item.start()

        def finish():
            for item in items:
                item.wait()
            total = k.small[first]
            for i in range(len(items)):
                total = total + k.small[first + 1 + i]
            return total

        return finish

    finish = small_step(0, [mate])
    tick("small")

    each = 24
    own_part, mate_part = pl.ds(pl.multiple_of(core * each, 8), each), pl.ds(pl.multiple_of(mate_core * each, 8), each)

    def rows_of(which, first):
        return pl.ds(pl.multiple_of(first + which * each, 8), each)

    def exchange_in():
        for index in range(tiles):
            lanes = slice((index % 2) * tile, (index % 2 + 1) * tile)
            to_lanes = pl.ds(pl.multiple_of((2 * index + core) * tile, LANE), tile)
            k.o_in[:, to_lanes] = k.result[rows_of(core, 48 * (index // 2)), lanes]
            k.fin_send[:, index * tile : (index + 1) * tile] = k.result[rows_of(mate_core, 48 * (index // 2)), lanes]
        in_copy.start()

    in_copy = copy(k.fin_send, k.fin_recv, mate)
    tail = PLAN["tail"]
    last_in = [at for at, item in enumerate(tail) if item[0] == "in"][-1]
    for at, item in enumerate(tail):
        if at == 2:
            k.small[2] = finish()
            finish = small_step(2, [(dp ^ 2, z), (dp ^ 4, z), (dp ^ 6, z)])
        if at == len(tail) // 2:
            k.small[6] = finish()
            finish = small_step(6, [(dp, z ^ turn) for turn in range(1, 4)])
        advance(*item)
        if at == last_in:
            exchange_in()
    total = finish()
    flat = dp * 4 + z
    keep = (
        lax.broadcasted_iota(jnp.int32, (width, each), 0) == lax.broadcasted_iota(jnp.int32, (width, each), 1) + flat * each
    ).astype(f32)
    shares = exact(total[:, :width], keep, 1, 0)
    k.o_lang[...] = shares[:8]
    k.o_first[...] = shares[8:9]
    k.o_second[...] = shares[9:10]
    k.o_bias[...] = total[:all_heads, width : width + bucket_count]
    in_copy.wait_recv()
    for index in range(tiles):
        to_lanes = pl.ds(pl.multiple_of((2 * index + mate_core) * tile, LANE), tile)
        k.o_in[:, to_lanes] = k.fin_recv[:, index * tile : (index + 1) * tile]
    in_copy.wait_send()
    k.fin_send[...] = k.result_last[mate_part, :]
    last_copy = copy(k.fin_send, k.fin_last, mate)
    last_copy.start()


    def put_projections(read, lanes):
        k.o_output[:, lanes] = read(0, mine)
        for index, target in enumerate((k.o_query, k.o_key, k.o_value)):
            target[:, lanes] = jnp.concatenate([read((1 + at) * mine + index * pair, pair) for at in range(3)], axis=1)

    put_projections(lambda first, size: k.result_last[own_part, first : first + size], own_lanes)
    last_copy.wait_recv()
    put_projections(lambda first, size: k.fin_last[:, first : first + size], mate_lanes)

    for item in (way_meta, way_tokens, way_cotangent, way_grad):
        item.close()
    for index in range(2):
        way_grad.arrive(index)
    for head in range(head_count):
        for item in mix_copies(head):
            item.wait_send()
    for index in range(tiles):
        gh_copy(index).wait_send()
    for item in (*cot_relays, proj_copy, *gn_copies, last_copy):
        item.wait_send()


def hand_on(*refs):
    count = len(refs) // 2
    for source, target in zip(refs[:count], refs[count:]):
        target[...] = source[...]


def local(
    tokens,
    language,
    lengths,
    rel_bucket,
    lang_table,
    gain_first,
    w_query,
    w_key,
    w_value,
    w_output,
    bias_table,
    gain_second,
    w_in,
    w_out,
    cotangent,
):
    seqs, rows, width = tokens.shape
    span = rows * lax.axis_size("blk")
    half, mine = span // 2, width // 2
    bucket_count, all_heads = bias_table.shape
    head_count = all_heads // 2
    ff_width = w_in.shape[1]
    devices = lax.axis_size("dp") * lax.axis_size("blk")
    each, each_out = width // devices, ff_width // devices
    tiles = ff_width // width
    buckets = jnp.pad(rel_bucket, (1, 0), constant_values=-1)[None]
    vmem, anywhere = pl.BlockSpec(memory_space=pltpu.VMEM), pl.BlockSpec(memory_space=pl.ANY)
    shape = jax.ShapeDtypeStruct
    ext = pltpu.VMEM((mine // head_count + 16, span), bf16)
    sum_buffers = [
        pltpu.VMEM(found, bf16)
        for group in GROUPS
        for part_rows, part_columns, order in PARTS[group]
        for found in Sums.shapes(part_rows[1], part_columns[1], order)
    ]
    found = pl.pallas_call(
        functools.partial(block_kernel, head_count),
        out_shape=(
            shape(tokens.shape, bf16),
            shape(tokens.shape, bf16),
            *[shape((each, width), f32)] * 4,
            shape((each, ff_width), f32),
            shape((each_out, width), f32),
            shape((8, each), f32),
            shape((1, each), f32),
            shape((1, each), f32),
            shape(bias_table.shape[::-1], f32),
        ),
        in_specs=[pl.BlockSpec(memory_space=pltpu.SMEM)] * 2 + [anywhere] * 8 + [vmem] * 5,
        out_specs=(anywhere, anywhere) + (vmem,) * 10,
        scratch_shapes=[
            pltpu.VMEM((span, width), bf16),
            pltpu.VMEM((seqs, 8, LANE), jnp.int32),
            pltpu.VMEM((seqs, 8, LANE), jnp.int32),
            pltpu.VMEM((3 * mine, width), bf16),
            pltpu.VMEM((width, width), bf16),
            pltpu.VMEM((width, ff_width), bf16),
            pltpu.VMEM((ff_width, width), bf16),
            pltpu.VMEM((width, span), bf16),
            pltpu.VMEM((3 * mine, span), bf16),
            pltpu.VMEM((mine, span), f32),
            pltpu.VMEM((width, span), bf16),
            pltpu.VMEM((mine, span), bf16),
            pltpu.VMEM((half, width), f32),
            pltpu.VMEM((half, width), f32),
            pltpu.VMEM((span, width), bf16),
            pltpu.VMEM((tiles * half, width), bf16),
            pltpu.VMEM((tiles * half, width), bf16),
            pltpu.VMEM((half, tiles * mine), bf16),
            pltpu.VMEM((half, tiles * mine), bf16),
            pltpu.VMEM((span, width), bf16),
            pltpu.VMEM((half, width), bf16),
            pltpu.VMEM((half, width), bf16),
            pltpu.VMEM((LANE, 2 * span), f32),
            pltpu.VMEM((LANE, 2 * span), f32),
            pltpu.VMEM((half // 2, span), bf16),
            pltpu.VMEM((half // 2, span), bf16),
            ext,
            ext,
            ext,
            ext,
            pltpu.VMEM((8, 2 * span), f32),
            pltpu.VMEM((8, 2 * span), f32),
            pltpu.VMEM((8, span), f32),
            pltpu.VMEM((11, 16, span), f32),
            pltpu.VMEM((each, 2 * width), f32),
            pltpu.VMEM((each, 2 * width), f32),
            pltpu.VMEM((each, 2 * width), f32),
            pltpu.VMEM((4 * each, width), f32),
            pltpu.VMEM((2 * each, 2 * width), f32),
            *[pltpu.VMEM((2, 2, 2, 2, *GROUP_SHAPE[group]), bf16) for group in GROUPS],
            *sum_buffers,
            pltpu.SemaphoreType.DMA((144,)),
            pltpu.SemaphoreType.DMA((144,)),
            pltpu.SemaphoreType.DMA((8,)),
        ],
        compiler_params=pltpu.CompilerParams(
            collective_id=0, has_side_effects=True, vmem_limit_bytes=VMEM_BYTES
        ),
        name="encoder_block",
    )(
        language,
        lengths,
        tokens,
        cotangent,
        w_query,
        w_key,
        w_value,
        w_output,
        w_in,
        w_out,
        lang_table,
        gain_first,
        gain_second,
        buckets,
        bias_table.T,
    )
    found = pl.pallas_call(
        hand_on,
        out_shape=tuple(shape(part.shape, part.dtype) for part in found),
        in_specs=[vmem] * len(found),
        out_specs=tuple([vmem] * len(found)),
        compiler_params=pltpu.CompilerParams(vmem_limit_bytes=VMEM_BYTES),
        name="hand_on",
    )(*found)
    output, grad_tokens, query, key, value, out, grad_in, grad_out, lang, first, second, bias = found
    return output, grad_tokens, lang, first[0], query, key, value, out, bias.T, second[0], grad_in, grad_out


def local_plain(
    tokens,
    language,
    lengths,
    rel_bucket,
    lang_table,
    gain_first,
    w_query,
    w_key,
    w_value,
    w_output,
    bias_table,
    gain_second,
    w_in,
    w_out,
    cotangent,
):
    dp_size, blk_size = lax.axis_size("dp"), lax.axis_size("blk")
    device, place = lax.axis_index("dp"), lax.axis_index("blk")
    core = device % 2
    odd = place % 2 == 1
    width = tokens.shape[-1]
    bucket_count, all_heads = bias_table.shape
    head_count = all_heads // 2
    mine = width // 2
    span = tokens.shape[1] * blk_size
    half = span // 2
    ff_width = w_in.shape[1]

    own_tokens = to_rows(tokens, odd)
    own_cotangent = to_rows(cotangent, odd)
    other_tokens = swap_core(own_tokens)
    ids = jnp.stack([language, lengths])
    other_ids = swap_core(ids)
    mates = jnp.where(place // (blk_size // 2) == core, ids, other_ids)
    spoken, length = jnp.where(odd, mates[:, 1], mates[:, 0])

    head_first = core * mine
    own_weights = jnp.concatenate(
        [lax.dynamic_slice_in_dim(w, head_first, mine, 1) for w in (w_query, w_key, w_value)], 1
    )
    own_weights_t = own_weights.T
    own_bias = lax.dynamic_slice_in_dim(bias_table, core * head_count, head_count, 1)
    bucket_hot = (rel_bucket[:, None] == jnp.arange(bucket_count)[None, :]).astype(f32)
    hot_later = jnp.pad(bucket_hot, ((1, 0), (0, 0)))
    hot_back = jnp.pad(bucket_hot[::-1], ((1, 0), (0, 0)))
    bias_later = jnp.pad(jnp.dot(hot_later, own_bias, precision=highest).T, ((0, 8 - head_count), (0, 0)))
    bias_back = jnp.pad(jnp.dot(hot_back, own_bias, precision=highest).T, ((0, 8 - head_count), (0, 0)))
    position = (jnp.arange(span) + half * core) % span
    key_mask = jnp.where(position < length, 0.0, masked_score).astype(f32)[None]

    embedding = lax.dynamic_slice_in_dim(lang_table, spoken, 1, 0).astype(f32)
    with_lang_all = jnp.concatenate([own_tokens, other_tokens]).astype(f32) + embedding
    scale_all = rms_parts(with_lang_all)
    normed = (with_lang_all * scale_all * gain_first).astype(bf16)
    qkv = dot(own_weights_t, normed, 1, 1).astype(bf16)
    mixture_t, attended_t, log_total = attention_forward(qkv, bias_back, key_mask, head_count)

    with_lang = with_lang_all[:half]
    other_mixture_t = swap_core(mixture_t[:, half:])
    own_mixture_t = mixture_t[:, :half]
    full_mixture_t = jnp.where(
        core == 0,
        jnp.concatenate([own_mixture_t, other_mixture_t]),
        jnp.concatenate([other_mixture_t, own_mixture_t]),
    )
    middle = with_lang + dot(full_mixture_t, w_output, 0, 0)
    scale_second = rms_parts(middle)
    normed_second = (middle * scale_second * gain_second).astype(bf16)
    hidden = dot(normed_second, w_in, 1, 0)
    active, gelu_back = jax.vjp(functools.partial(jax.nn.gelu, approximate=True), hidden)
    active = active.astype(bf16)
    output_rows = (middle + dot(active, w_out, 1, 0)).astype(bf16)
    output = from_rows(output_rows, odd)
    grad_hidden = gelu_back(dot(own_cotangent, w_out, 1, 1))[0].astype(bf16)
    grad_normed_second = dot(grad_hidden, w_in, 1, 1)
    grad_middle_part, grad_gain_second = norm_back(grad_normed_second, middle, gain_second, scale_second)
    grad_middle = own_cotangent.astype(f32) + grad_middle_part
    grad_projected = grad_middle.astype(bf16)
    grad_w_out = dot(active, own_cotangent, 0, 0)
    grad_w_in = dot(normed_second, grad_hidden, 0, 0)
    grad_w_output = dot(full_mixture_t, grad_projected, 1, 0)

    other_projected = swap_core(grad_projected)
    projected_all = jnp.concatenate([grad_projected, other_projected])
    own_output_rows = lax.dynamic_slice_in_dim(w_output, head_first, mine, 0)
    grad_mixture_t = dot(own_output_rows, projected_all, 1, 1).astype(bf16)
    grad_qkv, diagonals = attention_backward(
        qkv, grad_mixture_t, attended_t, log_total, bias_later, key_mask, head_count
    )
    pieces = diagonals.reshape(head_count, 8, 2 * span)
    by_distance = sum(jnp.roll(pieces[:, i], -i, axis=-1) for i in range(8))
    grad_bias_own = jnp.dot(by_distance, hot_later, precision=highest).T
    grad_bias = lax.dynamic_update_slice_in_dim(
        jnp.zeros(bias_table.shape, f32), grad_bias_own, core * head_count, 1
    )

    grad_normed_all = dot(grad_qkv, own_weights_t, 0, 0)
    from_other = swap_core(grad_normed_all[half:].astype(bf16))
    grad_normed = grad_normed_all[:half] + from_other.astype(f32)
    grad_start, grad_gain_first = norm_back(grad_normed, with_lang, gain_first, scale_all[:half])
    grad_with_lang = grad_middle + grad_start
    grad_tokens = from_rows(grad_with_lang.astype(bf16), odd)
    lang_hot = (jnp.arange(lang_table.shape[0]) == spoken).astype(f32)
    grad_lang = lang_hot[:, None] * jnp.sum(grad_with_lang, axis=0)[None, :]
    grad_w_qkv = dot(normed, grad_qkv, 0, 1)

    names = ("dp", "blk")

    def scattered(value, dim=0):
        return lax.psum_scatter(value, names, scatter_dimension=dim, tiled=True)

    grads_qkv = []
    for part in jnp.split(grad_w_qkv, 3, axis=1):
        whole = jnp.zeros((width, width), f32)
        grads_qkv.append(scattered(lax.dynamic_update_slice_in_dim(whole, part, head_first, 1)))
    return (
        output,
        grad_tokens,
        scattered(grad_lang, 1),
        scattered(grad_gain_first),
        *grads_qkv,
        scattered(grad_w_output),
        lax.psum(grad_bias, names),
        scattered(grad_gain_second),
        scattered(grad_w_in),
        scattered(grad_w_out),
    )


def solution(mesh):
    rows = P("dp", "blk", None)
    shard = P(("dp", "blk"))
    matrix = P(("dp", "blk"), None)
    fits = (mesh.shape["dp"], mesh.shape["blk"]) == (8, 4)
    return jax.shard_map(
        local if fits else local_plain,
        mesh=mesh,
        in_specs=(rows, P("dp"), P("dp")) + (P(),) * 11 + (rows,),
        out_specs=(
            rows,
            rows,
            P(None, ("dp", "blk")),
            shard,
            matrix,
            matrix,
            matrix,
            matrix,
            P(),
            shard,
            matrix,
            matrix,
        ),
        check_vma=False,
    )
```
